32 devices in a mesh: grp: 4 (over x, core), mem: 8 (over z, y).
Axes of the slice: x: 2, y: 2, z: 4, core: 2. Of those that a mesh axis runs over, the one named last changes fastest.
Arguments:
- dec_input: bfloat16 [4, 4, 256, 1024], P('grp'), may hold values from -6 to 6
- memory: bfloat16 [4, 4, 512, 1024], P('grp', None, 'mem'), may hold values from -6 to 6
- out_grad: bfloat16 [4, 4, 256, 1024], P('grp'), may hold values from -6 to 6
- tgt_lengths: int32 [4, 4], P('grp'), may hold values from 128 to 256, as said below
- src_lengths: int32 [4, 4], P('grp'), may hold values from 64 to 512, as said below
- self_qkv: bfloat16 [3, 1024, 1024], replicated, may hold values from -0.1875 to 0.1875
- self_out: bfloat16 [1024, 1024], replicated, may hold values from -0.75 to 0.75
- cross_qkv: bfloat16 [3, 1024, 1024], replicated, may hold values from -0.1875 to 0.1875
- cross_out: bfloat16 [1024, 1024], replicated, may hold values from -1.5 to 1.5
- ffn_in: bfloat16 [1024, 4096], replicated, may hold values from -0.1875 to 0.1875
- ffn_out: bfloat16 [4096, 1024], replicated, may hold values from -0.09375 to 0.09375
- norm_gains: float32 [3, 1024], replicated, may hold values from 0.5 to 1.5
- norm_biases: float32 [3, 1024], replicated, may hold values from -1 to 1
- down_w: float32 [4, 1024, 512], P('grp', 'mem'), may hold values from -0.1875 to 0.1875
- up_w: float32 [4, 512, 1024], P('grp', 'mem'), may hold values from -0.0625 to 0.0625
- prefix_w: float32 [4, 2, 30, 1024], P('grp', None, None, 'mem'), may hold values from -5 to 5
- down_m: float32 [4, 1024, 512], P('grp', 'mem'), may hold values from -7.3161826 to 7.3161826
- down_v: float32 [4, 1024, 512], P('grp', 'mem'), may hold values from 0.27648 to 1.10592
- up_m: float32 [4, 512, 1024], P('grp', 'mem'), may hold values from -23.135801 to 23.135801
- up_v: float32 [4, 512, 1024], P('grp', 'mem'), may hold values from 2.7648 to 11.0592
- prefix_m: float32 [4, 2, 30, 1024], P('grp', None, None, 'mem'), may hold values from -0.21461475 to 0.21461475
- prefix_v: float32 [4, 2, 30, 1024], P('grp', None, None, 'mem'), may hold values from 0.00023791059 to 0.00095164235
- down_outer: float32 [1024, 512], P('mem'), may hold values from -0.1875 to 0.1875
- up_outer: float32 [512, 1024], P('mem'), may hold values from -0.0625 to 0.0625
- prefix_outer: float32 [2, 30, 1024], P(None, None, 'mem'), may hold values from -5 to 5
- down_mom: float32 [1024, 512], P('mem'), may hold values from -0.1875 to 0.1875
- up_mom: float32 [512, 1024], P('mem'), may hold values from -0.0625 to 0.0625
- prefix_mom: float32 [2, 30, 1024], P(None, None, 'mem'), may hold values from -5 to 5
Outputs:
- output: bfloat16 [4, 4, 256, 1024], P('grp')
- grad_input: float32 [4, 4, 256, 1024], P('grp')
- grad_memory: float32 [4, 4, 512, 1024], P('grp', None, 'mem')
- grad_down: float32 [4, 1024, 512], P('grp', 'mem')
- grad_up: float32 [4, 512, 1024], P('grp', 'mem')
- grad_prefix: float32 [4, 2, 30, 1024], P('grp', None, None, 'mem')
- new_down_m: float32 [4, 1024, 512], P('grp', 'mem')
- new_down_v: float32 [4, 1024, 512], P('grp', 'mem')
- new_down_w: float32 [4, 1024, 512], P('grp', 'mem')
- new_up_m: float32 [4, 512, 1024], P('grp', 'mem')
- new_up_v: float32 [4, 512, 1024], P('grp', 'mem')
- new_up_w: float32 [4, 512, 1024], P('grp', 'mem')
- new_prefix_m: float32 [4, 2, 30, 1024], P('grp', None, None, 'mem')
- new_prefix_v: float32 [4, 2, 30, 1024], P('grp', None, None, 'mem')
- new_prefix_w: float32 [4, 2, 30, 1024], P('grp', None, None, 'mem')
- new_down_mom: float32 [1024, 512], P('mem')
- new_down_outer: float32 [1024, 512], P('mem')
- new_up_mom: float32 [512, 1024], P('mem')
- new_up_outer: float32 [512, 1024], P('mem')
- new_prefix_mom: float32 [2, 30, 1024], P(None, None, 'mem')
- new_prefix_outer: float32 [2, 30, 1024], P(None, None, 'mem')
The draws below stay inside these ranges and needn't reach their ends.
Inputs may be any that keep to these rules, and one draw needn't show every extreme that they name: `tgt_lengths`: in each group one sequence, drawn from the seed, has exactly 256. `src_lengths`: in each group one sequence, drawn from the seed, has exactly 512.
All inputs are finite; a program needn't handle non-finite values.
Results may differ from the reference program's by a relative error of at most 0.025.
Values may be sent and summed in bfloat16 or wider, within the bound.
No kernel may reach another device: no remote copies, remote signals or barrier semaphores. Data moves between devices by JAX's collectives and lax.ppermute only.
A program may use at most 256 MiB of HBM per device.

```python
import math
import jax
import jax.numpy as jnp
from jax import lax

D = 1024
HEADS = 16
HDIM = 64
FF = 4096
ADAPT = 512
PREFIX = 30
SEQS = 4
TGT = 256
SRC_DEV = 64
STEP = 10
GROUPS = 4
SRC = 512
N_GRP = 4
N_MEM = 8


def lengths_with_full(key, lowest, highest):
    key_lengths, key_choice = jax.random.split(key)
    lengths = jax.random.randint(key_lengths, (GROUPS, SEQS), lowest, highest + 1)
    chosen = jax.random.randint(key_choice, (GROUPS, 1), 0, SEQS)
    return jnp.where(jnp.arange(SEQS)[None, :] == chosen, highest, lengths).astype(jnp.int32)


def draw_tgt_lengths(key, part):
    key = jax.random.fold_in(key, 11)
    return lengths_with_full(key, TGT // 2, TGT)


def draw_src_lengths(key, part):
    key = jax.random.fold_in(key, 23)
    return lengths_with_full(key, SRC // 8, SRC)


def block_levels(rng, shape, cuts, low, high):
    def one(position, blocks):
        steps = jax.random.uniform(jax.random.fold_in(jax.random.fold_in(rng, 6), position), (blocks,), jnp.float32, low / len(cuts), high / len(cuts))
        return jnp.repeat(jnp.exp(steps), shape[position] // blocks).reshape((-1,) + (1,) * (len(shape) - position - 1))

    factor_of = one(*cuts[0])
    for cut in cuts[1:]:
        factor_of = factor_of * one(*cut)
    return factor_of


def normal_values(stream_key, dims, scale, most, pieces=(), dtype=jnp.bfloat16):
    factor_of = block_levels(stream_key, dims, pieces, -0.22, 0.18) if pieces else 1.0
    entries = jax.random.normal(stream_key, dims, jnp.float32) * scale * factor_of
    return jnp.minimum(jnp.maximum(entries, -most), most).astype(dtype)


def setup_inputs(seed: int = 0) -> dict:
    key_of = jax.random.split(jax.random.key(seed), 29)
    dec_input = normal_values(key_of[0], (GROUPS, SEQS, TGT, D), 1.0, 6.0, ((0, 4),))
    memory = normal_values(key_of[1], (GROUPS, SEQS, SRC, D), 1.0, 6.0, ((0, 4), (2, 8)))
    out_grad = normal_values(key_of[2], (GROUPS, SEQS, TGT, D), 1.0, 6.0, ((0, 4),))
    tgt_lengths = draw_tgt_lengths(jax.random.fold_in(key_of[28], 71), 0)
    src_lengths = draw_src_lengths(jax.random.fold_in(key_of[28], 71), 0)
    self_qkv = normal_values(key_of[5], (3, D, D), D ** -0.5, 0.1875)
    self_out = normal_values(key_of[6], (D, D), (D // 16) ** -0.5, 0.75)
    cross_qkv = normal_values(key_of[7], (3, D, D), D ** -0.5, 0.1875)
    cross_out = normal_values(key_of[8], (D, D), (D // 64) ** -0.5, 1.5)
    ffn_in = normal_values(key_of[9], (D, FF), D ** -0.5, 0.1875)
    ffn_out = normal_values(key_of[10], (FF, D), FF ** -0.5, 0.09375)
    norm_gains = jnp.clip(1.0 + 0.1 * jax.random.normal(key_of[11], (3, D), jnp.float32), 0.5, 1.5)
    norm_biases = normal_values(key_of[12], (3, D), 0.2, 1.0, (), jnp.float32)
    down_w = normal_values(key_of[13], (GROUPS, D, ADAPT), D ** -0.5, 0.1875, ((0, 4), (1, 8)), jnp.float32)
    up_w = normal_values(key_of[14], (GROUPS, ADAPT, D), (16 * ADAPT) ** -0.5, 0.0625, ((0, 4), (1, 8)), jnp.float32)
    prefix_w = normal_values(key_of[15], (GROUPS, 2, PREFIX, D), 1.0, 5.0, ((0, 4), (3, 8)), jnp.float32)
    down_m = normal_values(key_of[16], (GROUPS, D, ADAPT), (0.11 * (0.27 * SEQS * TGT) ** 0.5), 7.3161826, ((0, 4), (1, 8)), jnp.float32)
    down_v = jnp.clip(jnp.exp(math.log(1.10592) - 1.3862944 * jax.random.uniform(key_of[17], (GROUPS, D, ADAPT), jnp.float32) ** block_levels(key_of[17], (GROUPS, D, ADAPT), ((0, 4), (1, 8)), -0.2, 0.2)), 0.27648, 1.10592)
    up_m = normal_values(key_of[18], (GROUPS, ADAPT, D), (0.11 * (2.7 * SEQS * TGT) ** 0.5), 23.135801, ((0, 4), (1, 8)), jnp.float32)
    up_v = jnp.clip(jnp.exp(math.log(11.0592) - 1.3862944 * jax.random.uniform(key_of[19], (GROUPS, ADAPT, D), jnp.float32) ** block_levels(key_of[19], (GROUPS, ADAPT, D), ((0, 4), (1, 8)), -0.2, 0.2)), 2.7648, 11.0592)
    prefix_m = normal_values(key_of[20], (GROUPS, 2, PREFIX, D), (0.11 * (5.8 * SEQS * TGT) ** 0.5 / (PREFIX + TGT // 2)), 0.21461475, ((0, 4), (3, 8)), jnp.float32)
    prefix_v = jnp.clip(jnp.exp(math.log(0.00095164235) - 1.3862944 * jax.random.uniform(key_of[21], (GROUPS, 2, PREFIX, D), jnp.float32) ** block_levels(key_of[21], (GROUPS, 2, PREFIX, D), ((0, 4), (3, 8)), -0.2, 0.2)), 0.00023791059, 0.00095164235)
    down_outer = normal_values(key_of[22], (D, ADAPT), D ** -0.5, 0.1875, ((0, 8),), jnp.float32)
    up_outer = normal_values(key_of[23], (ADAPT, D), (16 * ADAPT) ** -0.5, 0.0625, ((0, 8),), jnp.float32)
    prefix_outer = normal_values(key_of[24], (2, PREFIX, D), 1.0, 5.0, ((2, 8),), jnp.float32)
    down_mom = normal_values(key_of[25], (D, ADAPT), D ** -0.5, 0.1875, ((0, 8),), jnp.float32)
    up_mom = normal_values(key_of[26], (ADAPT, D), (16 * ADAPT) ** -0.5, 0.0625, ((0, 8),), jnp.float32)
    prefix_mom = normal_values(key_of[27], (2, PREFIX, D), 1.0, 5.0, ((2, 8),), jnp.float32)
    return dict(dec_input=dec_input, memory=memory, out_grad=out_grad, tgt_lengths=tgt_lengths, src_lengths=src_lengths, self_qkv=self_qkv, self_out=self_out, cross_qkv=cross_qkv, cross_out=cross_out, ffn_in=ffn_in, ffn_out=ffn_out, norm_gains=norm_gains, norm_biases=norm_biases, down_w=down_w, up_w=up_w, prefix_w=prefix_w, down_m=down_m, down_v=down_v, up_m=up_m, up_v=up_v, prefix_m=prefix_m, prefix_v=prefix_v, down_outer=down_outer, up_outer=up_outer, prefix_outer=prefix_outer, down_mom=down_mom, up_mom=up_mom, prefix_mom=prefix_mom)


@jax.custom_vjp
def low(v):
    return lax.optimization_barrier(v.astype(jnp.bfloat16)).astype(jnp.float32)

@jax.custom_vjp
def low_back(v):
    return v

def low_keep(v):
    return (low(v), None)

def low_pass(kept, grad):
    return (grad,)

def back_keep(v):
    return (v, None)

def back_low(kept, grad):
    return (low(grad),)
low.defvjp(low_keep, low_pass)
low_back.defvjp(back_keep, back_low)
EPSILON = 1e-05
NEGATIVE = -1e+30
HIGHEST = lax.Precision.HIGHEST

def both_ways(values_in):
    return low_back(low(values_in))

def layer_norm(values_in, gain_row, bias_row):
    centered = values_in - lax.optimization_barrier(jnp.mean(values_in, -1, keepdims=True))
    return centered * lax.rsqrt(lax.optimization_barrier(jnp.mean(centered * centered, -1, keepdims=True)) + EPSILON) * gain_row + bias_row

def heads_of(values_in):
    return values_in.reshape(values_in.shape[:-1] + (HEADS, HDIM))

def self_mask(lengths, target, prefix_len):
    rows_pos = jnp.arange(target)[:, None]
    keys_pos = jnp.arange(prefix_len + target)[None, :] - prefix_len
    causal = (keys_pos <= rows_pos)[None]
    inside = keys_pos[None] < lengths[:, None, None]
    return ((keys_pos[None] < 0) | causal & inside)[:, None]

def gelu_exact(values_in):
    return jax.nn.gelu(values_in, approximate=False)

def forward(tokens, memory_rows, down_master, up_master, prefix_master, frozen, tgt_len, src_len):
    self_qkv, self_out, cross_qkv, cross_out, ffn_in, ffn_out, gains, biases = frozen
    score_scale = HDIM ** (-0.5)
    projected = both_ways(jnp.einsum('std,cde->cste', tokens, self_qkv, precision=HIGHEST))
    queries = heads_of(projected[0])
    prefix_low = heads_of(low(prefix_master))
    keys_all = jnp.concatenate([jnp.broadcast_to(prefix_low[0][None], (SEQS, PREFIX, HEADS, HDIM)), heads_of(projected[1])], axis=1)
    values_all = jnp.concatenate([jnp.broadcast_to(prefix_low[1][None], (SEQS, PREFIX, HEADS, HDIM)), heads_of(projected[2])], axis=1)
    scores = low_back(jnp.einsum('sqhe,skhe->shqk', queries, keys_all, precision=HIGHEST) * score_scale)
    allowed = self_mask(tgt_len, TGT, PREFIX)
    weights = jax.nn.softmax(jnp.where(allowed, scores, NEGATIVE), axis=-1)
    context = both_ways(jnp.einsum('shqk,skhe->sqhe', low(weights), values_all, precision=HIGHEST))
    attended = low_back(jnp.matmul(context.reshape(SEQS, TGT, D), self_out, precision=HIGHEST))
    hidden_one = layer_norm(tokens + attended, gains[0], biases[0])
    cross_queries = heads_of(both_ways(jnp.matmul(low(hidden_one), cross_qkv[0], precision=HIGHEST)))
    mem_proj = both_ways(jnp.einsum('skd,cde->cske', memory_rows, cross_qkv[1:], precision=HIGHEST))
    mem_keys = heads_of(mem_proj[0])
    mem_values = heads_of(mem_proj[1]).reshape(SEQS, N_MEM, SRC_DEV, HEADS, HDIM)
    raw_scores = low_back(jnp.einsum('sqhe,skhe->shqk', cross_queries, mem_keys, precision=HIGHEST) * score_scale)
    valid_keys = (jnp.arange(SRC)[None, :] < src_len[:, None])[:, None, None, :]
    masked = jnp.where(valid_keys, raw_scores, NEGATIVE).reshape(SEQS, HEADS, TGT, N_MEM, SRC_DEV)
    valid_blocks = valid_keys.reshape(SEQS, 1, 1, N_MEM, SRC_DEV).astype(jnp.float32)
    local_max = lax.optimization_barrier(jnp.max(masked, -1))
    exponent = low(jnp.exp(masked - local_max[..., None])) * valid_blocks
    local_sum = lax.optimization_barrier(jnp.sum(exponent, -1))
    numerator = jnp.einsum('shqnk,snkhe->shqne', exponent, mem_values, precision=HIGHEST)
    top_max = lax.optimization_barrier(jnp.max(local_max, -1))
    factor = jnp.exp(local_max - top_max[..., None])
    total_sum = lax.optimization_barrier(jnp.sum(factor * local_sum, -1))
    cross_ctx = lax.optimization_barrier(jnp.sum(factor[..., None] * numerator, 3)) / total_sum[..., None]
    cross_ctx = both_ways(cross_ctx.transpose(0, 2, 1, 3).reshape(SEQS, TGT, D))
    crossed = low_back(jnp.matmul(cross_ctx, cross_out, precision=HIGHEST))
    hidden_two = layer_norm(hidden_one + crossed, gains[1], biases[1])
    normed = low(hidden_two)
    ffn_pre = low_back(jnp.matmul(normed, ffn_in, precision=HIGHEST))
    ffn_result = low_back(jnp.matmul(low(gelu_exact(ffn_pre)), ffn_out, precision=HIGHEST))
    adapt_pre = low_back(jnp.matmul(normed, low(down_master), precision=HIGHEST))
    adapted = low_back(jnp.matmul(low(gelu_exact(adapt_pre)), low(up_master), precision=HIGHEST))
    return layer_norm(hidden_two + ffn_result + 4.0 * adapted, gains[2], biases[2])

def adam_update(gradient, first_moment, second_moment, weight, step_rate):
    first_new = 0.9 * first_moment + 0.1 * gradient
    second_new = 0.999 * second_moment + 0.001 * gradient * gradient
    corrected_one = first_new / (1.0 - 0.9 ** STEP)
    corrected_two = second_new / (1.0 - 0.999 ** STEP)
    weight_new = weight - step_rate * (corrected_one / (jnp.sqrt(corrected_two) + 1e-08) + 0.01 * weight)
    return (first_new, second_new, weight_new)

def outer_update(outer_weight, momentum, group_weights):
    average = lax.optimization_barrier(jnp.sum(outer_weight[None] - group_weights, 0)) / N_GRP
    momentum_new = 0.9 * momentum + average
    return (momentum_new, outer_weight - 0.7 * (average + 0.9 * momentum_new))

def reference(dec_input, memory, out_grad, tgt_lengths, src_lengths, self_qkv, self_out, cross_qkv, cross_out, ffn_in, ffn_out, norm_gains, norm_biases, down_w, up_w, prefix_w, down_m, down_v, up_m, up_v, prefix_m, prefix_v, down_outer, up_outer, prefix_outer, down_mom, up_mom, prefix_mom):
    frozen = tuple((array_in.astype(jnp.float32) for array_in in (self_qkv, self_out, cross_qkv, cross_out, ffn_in, ffn_out, norm_gains, norm_biases)))

    def one_group(group_items):
        tokens, memory_rows, cotangent, tgt_len, src_len, down_master, up_master, prefix_master = group_items

        def apply_layer(token_values, memory_values, down_values, up_values, prefix_values):
            return forward(token_values, memory_values, down_values, up_values, prefix_values, frozen, tgt_len, src_len)
        result, pullback = jax.vjp(apply_layer, tokens.astype(jnp.float32), memory_rows.astype(jnp.float32), down_master, up_master, prefix_master)
        live_rows = (jnp.arange(TGT)[None, :] < tgt_len[:, None]).astype(jnp.float32)[..., None]
        gradients = pullback(cotangent.astype(jnp.float32) * live_rows)
        return (result.astype(jnp.bfloat16),) + tuple(gradients)
    output, grad_input, grad_memory, grad_down, grad_up, grad_prefix = lax.map(one_group, (dec_input, memory, out_grad, tgt_lengths, src_lengths, down_w, up_w, prefix_w))
    new_down_m, new_down_v, new_down_w = adam_update(grad_down, down_m, down_v, down_w, 0.06)
    new_up_m, new_up_v, new_up_w = adam_update(grad_up, up_m, up_v, up_w, 0.02)
    new_prefix_m, new_prefix_v, new_prefix_w = adam_update(grad_prefix, prefix_m, prefix_v, prefix_w, 2.0)
    new_down_mom, new_down_outer = outer_update(down_outer, down_mom, new_down_w)
    new_up_mom, new_up_outer = outer_update(up_outer, up_mom, new_up_w)
    new_prefix_mom, new_prefix_outer = outer_update(prefix_outer, prefix_mom, new_prefix_w)
    return (output, grad_input, grad_memory, grad_down, grad_up, grad_prefix, new_down_m, new_down_v, new_down_w, new_up_m, new_up_v, new_up_w, new_prefix_m, new_prefix_v, new_prefix_w, new_down_mom, new_down_outer, new_up_mom, new_up_outer, new_prefix_mom, new_prefix_outer)
```

```python
import jax
import jax.numpy as jnp
from jax import lax
from jax.sharding import PartitionSpec as P

HEADS = 16
HDIM = 64
STEP = 10


EPSILON = 1e-05
NEGATIVE = -1e30
ADAPTER_SCALE = 4.0
OUTER_MOMENTUM = 0.9
OUTER_RATE = 0.7


def normalize(values_in, gain_row, bias_row):
    centered = values_in - jnp.mean(values_in, -1, keepdims=True)
    scale_inv = lax.rsqrt(jnp.mean(centered * centered, -1, keepdims=True) + EPSILON)
    normal = centered * scale_inv
    return (normal * gain_row + bias_row, normal, scale_inv)


def normalize_back(gradient, normal, scale_inv, gain_row):
    scaled = gradient * gain_row
    return scale_inv * (
        scaled
        - jnp.mean(scaled, -1, keepdims=True)
        - normal * jnp.mean(scaled * normal, -1, keepdims=True)
    )


def gelu_exact(values_in):
    return jax.nn.gelu(values_in, approximate=False)


def gelu_back(pre_act, gradient):
    unused, pullback = jax.vjp(gelu_exact, pre_act)
    return pullback(gradient)[0]


def self_mask(length, target, prefix_len):
    rows_pos = jnp.arange(target)[:, None]
    keys_pos = jnp.arange(prefix_len + target)[None, :] - prefix_len
    return ((keys_pos < 0) | (keys_pos <= rows_pos) & (keys_pos < length))[None]


def self_scores(queries, keys_all, allowed, score_scale):
    scores = (
        jnp.einsum("qhe,khe->hqk", queries, keys_all, preferred_element_type=jnp.float32)
        * score_scale
    )
    return jnp.where(allowed, scores, NEGATIVE)


def adam_update(gradient, first_moment, second_moment, weight, step_rate):
    first_new = 0.9 * first_moment + 0.1 * gradient
    second_new = 0.999 * second_moment + 0.001 * gradient * gradient
    corrected_one = first_new / (1.0 - 0.9**STEP)
    corrected_two = second_new / (1.0 - 0.999**STEP)
    weight_new = weight - step_rate * (
        corrected_one / (jnp.sqrt(corrected_two) + 1e-08) + 0.01 * weight
    )
    return (first_new, second_new, weight_new)


def local(
    dec_input,
    memory,
    out_grad,
    tgt_lengths,
    src_lengths,
    self_qkv,
    self_out,
    cross_qkv,
    cross_out,
    ffn_in,
    ffn_out,
    norm_gains,
    norm_biases,
    down_w,
    up_w,
    prefix_w,
    down_m,
    down_v,
    up_m,
    up_v,
    prefix_m,
    prefix_v,
    down_outer,
    up_outer,
    prefix_outer,
    down_mom,
    up_mom,
    prefix_mom,
):
    seq_count, target, model_width = dec_input.shape[1:]
    source = memory.shape[2]
    num_heads = HEADS
    head_dim = HDIM
    prefix_len = prefix_w.shape[2]
    mem_size = lax.axis_size("mem")
    grp_size = lax.axis_size("grp")
    replicas = mem_size // seq_count
    score_scale = head_dim ** (-0.5)
    device = lax.axis_index("mem")
    seq = device % seq_count
    replica = device // seq_count

    def swap(values_in, bits):
        return lax.ppermute(values_in, "mem", [(j, j ^ bits) for j in range(mem_size)])

    def pick(values_in, index):
        return lax.dynamic_index_in_dim(values_in, index, 0, keepdims=False)

    def natural(pieces):
        return jnp.take(jnp.stack(pieces), device ^ jnp.arange(len(pieces)), axis=0)

    def plane_gather(values_in):
        half = values_in.shape[0] // 2
        low, high = values_in[:half], values_in[half:]
        low_one, high_two = swap(low, 1), swap(high, 2)
        low_two, high_one = swap(low, 2), swap(high, 1)
        low_three, high_three = swap(low_two, 1), swap(high_one, 2)
        return [
            values_in,
            jnp.concatenate([low_one, high_one]),
            jnp.concatenate([low_two, high_two]),
            jnp.concatenate([low_three, high_three]),
        ]

    def plane_order(pieces):
        return jnp.take(jnp.stack(pieces), seq ^ jnp.arange(seq_count), axis=0)

    mem_send = [pick(memory[0], seq ^ j) for j in range(seq_count)]
    mem_rows = natural(
        [mem_send[0]] + [swap(mem_send[k % seq_count], k) for k in range(1, mem_size)]
    ).reshape(mem_size * source, model_width)
    prefix = prefix_w[0].astype(jnp.bfloat16)
    bits = 1
    while bits < mem_size:
        other = swap(prefix, bits)
        prefix = jnp.where(
            (device & bits) > 0,
            jnp.concatenate([other, prefix], 2),
            jnp.concatenate([prefix, other], 2),
        )
        bits *= 2

    def gather_rows(values_in):
        pieces = [values_in]
        bits = mem_size // 2
        while bits >= seq_count:
            pieces = pieces + [swap(piece, bits) for piece in pieces]
            bits //= 2
        order = [0]
        bits = replicas // 2
        while bits:
            order = order + [o ^ bits for o in order]
            bits //= 2
        planes = [plane_gather(piece) for piece in pieces]
        every = [None] * mem_size
        for o, plane in zip(order, planes):
            for j in range(seq_count):
                every[o * seq_count + j] = plane[j]
        return natural(every).reshape(mem_size * values_in.shape[0], values_in.shape[1])

    gathered_down = gather_rows(down_w[0].astype(jnp.bfloat16))
    gathered_up = gather_rows(up_w[0].astype(jnp.bfloat16))

    tokens = pick(dec_input[0], seq)
    cotangent = pick(out_grad[0], seq)
    tgt_length = tgt_lengths[0, seq]
    src_length = src_lengths[0, seq]
    projected = jnp.einsum(
        "rd,cde->cre", tokens, self_qkv, preferred_element_type=jnp.float32
    ).astype(jnp.bfloat16)
    shaped = projected.reshape(3, target, num_heads, head_dim)
    queries = shaped[0]
    prefix_pair = prefix.reshape(2, prefix_len, num_heads, head_dim)
    keys_all = jnp.concatenate([prefix_pair[0], shaped[1]], axis=0)
    values_all = jnp.concatenate([prefix_pair[1], shaped[2]], axis=0)
    allowed = self_mask(tgt_length, target, prefix_len)
    masked_self = self_scores(queries, keys_all, allowed, score_scale)
    row_max = jnp.max(masked_self, -1, keepdims=True)
    self_exp = jnp.exp(masked_self - row_max)
    self_total = jnp.sum(self_exp, -1, keepdims=True)
    probs_self = self_exp / self_total
    context = (
        jnp.einsum(
            "hqk,khe->qhe",
            probs_self.astype(jnp.bfloat16),
            values_all,
            preferred_element_type=jnp.float32,
        )
        .astype(jnp.bfloat16)
        .reshape(target, model_width)
    )
    attended = jnp.dot(context, self_out, preferred_element_type=jnp.float32)
    hidden_one, normal_one, inverse_one = normalize(
        tokens.astype(jnp.float32) + attended, norm_gains[0], norm_biases[0]
    )
    cross_queries = (
        jnp.dot(hidden_one.astype(jnp.bfloat16), cross_qkv[0], preferred_element_type=jnp.float32)
        .astype(jnp.bfloat16)
        .reshape(target, num_heads, head_dim)
    )
    mem_proj = (
        jnp.einsum("rd,cde->cre", mem_rows, cross_qkv[1:], preferred_element_type=jnp.float32)
        .astype(jnp.bfloat16)
        .reshape(2, mem_size * source, num_heads, head_dim)
    )
    valid_keys = (jnp.arange(mem_size * source) < src_length)[None, None, :]
    raw_scores = (
        jnp.einsum("qhe,khe->hqk", cross_queries, mem_proj[0], preferred_element_type=jnp.float32)
        * score_scale
    )
    masked = jnp.where(valid_keys, raw_scores, NEGATIVE)
    top_max = jnp.max(masked, -1, keepdims=True)
    exponent = jnp.exp(masked - top_max)
    exponent_low = exponent.astype(jnp.bfloat16)
    total_sum = jnp.sum(exponent_low.astype(jnp.float32), -1)
    numerator = jnp.einsum(
        "hqk,khe->hqe", exponent_low, mem_proj[1], preferred_element_type=jnp.float32
    )
    cross_ctx = numerator / total_sum[..., None]
    cross_low = cross_ctx.transpose(1, 0, 2).reshape(target, model_width).astype(jnp.bfloat16)
    crossed = jnp.dot(cross_low, cross_out, preferred_element_type=jnp.float32)
    hidden_two, normal_two, inverse_two = normalize(
        hidden_one + crossed, norm_gains[1], norm_biases[1]
    )
    normed = hidden_two.astype(jnp.bfloat16)
    ffn_pre = jnp.dot(normed, ffn_in, preferred_element_type=jnp.float32)
    ffn_act = gelu_exact(ffn_pre).astype(jnp.bfloat16)
    ffn_result = jnp.dot(ffn_act, ffn_out, preferred_element_type=jnp.float32)
    adapt_pre = jnp.dot(normed, gathered_down, preferred_element_type=jnp.float32)
    adapt_act = gelu_exact(adapt_pre).astype(jnp.bfloat16)
    adapted = jnp.dot(adapt_act, gathered_up, preferred_element_type=jnp.float32)
    output_rows, normal_three, inverse_three = normalize(
        hidden_two + ffn_result + ADAPTER_SCALE * adapted, norm_gains[2], norm_biases[2]
    )
    output = plane_order(plane_gather(output_rows.astype(jnp.bfloat16)))
    live_rows = (jnp.arange(target) < tgt_length).astype(jnp.float32)[:, None]
    grad_three = normalize_back(
        cotangent.astype(jnp.float32) * live_rows, normal_three, inverse_three, norm_gains[2]
    )
    grad_adapted = (ADAPTER_SCALE * grad_three).astype(jnp.bfloat16)
    grad_ffn = grad_three.astype(jnp.bfloat16)
    grad_adapt_pre = gelu_back(
        adapt_pre, jnp.dot(grad_adapted, gathered_up.T, preferred_element_type=jnp.float32)
    ).astype(jnp.bfloat16)

    def owners_sum(left, right):
        columns = left.shape[1] // replicas
        share = lax.dynamic_slice_in_dim(left, replica * columns, columns, 1)
        partial = jnp.dot(share.T, right, preferred_element_type=jnp.float32)
        partial = partial.reshape(seq_count, columns // seq_count, right.shape[1])
        total = pick(partial, seq)
        low = partial.astype(jnp.bfloat16)
        for j in range(1, seq_count):
            total = total + swap(pick(low, seq ^ j), j).astype(jnp.float32)
        return total

    grad_up = owners_sum(adapt_act, grad_adapted)
    grad_down = owners_sum(normed, grad_adapt_pre)
    grad_ffn_pre = gelu_back(
        ffn_pre, jnp.dot(grad_ffn, ffn_out.T, preferred_element_type=jnp.float32)
    ).astype(jnp.bfloat16)
    grad_hidden_two = (
        grad_three
        + jnp.dot(grad_ffn_pre, ffn_in.T, preferred_element_type=jnp.float32)
        + jnp.dot(grad_adapt_pre, gathered_down.T, preferred_element_type=jnp.float32)
    )
    grad_two = normalize_back(grad_hidden_two, normal_two, inverse_two, norm_gains[1])
    grad_cross = (
        jnp.dot(grad_two.astype(jnp.bfloat16), cross_out.T, preferred_element_type=jnp.float32)
        .astype(jnp.bfloat16)
        .reshape(target, num_heads, head_dim)
        .transpose(1, 0, 2)
    )
    grad_probs = jnp.einsum(
        "hqe,khe->hqk", grad_cross, mem_proj[1], preferred_element_type=jnp.float32
    )
    cross_delta = jnp.sum(grad_cross.astype(jnp.float32) * cross_ctx, -1)
    grad_scores = (
        exponent / total_sum[..., None] * (grad_probs - cross_delta[..., None])
    ).astype(jnp.bfloat16)
    grad_queries = (
        (
            jnp.einsum(
                "hqk,khe->qhe", grad_scores, mem_proj[0], preferred_element_type=jnp.float32
            )
            * score_scale
        )
        .reshape(target, model_width)
        .astype(jnp.bfloat16)
    )
    grad_mem_keys = (
        jnp.einsum("hqk,qhe->khe", grad_scores, cross_queries, preferred_element_type=jnp.float32)
        * score_scale
    ).astype(jnp.bfloat16)
    grad_mem_values = jnp.einsum(
        "hqk,hqe->khe",
        exponent_low,
        (grad_cross.astype(jnp.float32) / total_sum[..., None]).astype(jnp.bfloat16),
        preferred_element_type=jnp.float32,
    ).astype(jnp.bfloat16)
    grad_mem_pair = jnp.stack([grad_mem_keys, grad_mem_values]).reshape(
        2, mem_size * source, model_width
    )
    plane_rows = seq_count * source
    grad_mem_share = lax.dynamic_slice_in_dim(grad_mem_pair, replica * plane_rows, plane_rows, 1)
    grad_mem_rows = (
        jnp.einsum("cre,cde->rd", grad_mem_share, cross_qkv[1:], preferred_element_type=jnp.float32)
        .reshape(seq_count, source, model_width)
        .astype(jnp.bfloat16)
    )
    grad_mem_sent = [pick(grad_mem_rows, seq ^ j) for j in range(seq_count)]
    grad_memory = plane_order(
        [grad_mem_sent[0]] + [swap(grad_mem_sent[j], j) for j in range(1, seq_count)]
    ).astype(jnp.float32)
    from_queries = jnp.dot(grad_queries, cross_qkv[0].T, preferred_element_type=jnp.float32)
    grad_one = normalize_back(grad_two + from_queries, normal_one, inverse_one, norm_gains[0])
    grad_context = (
        jnp.dot(grad_one.astype(jnp.bfloat16), self_out.T, preferred_element_type=jnp.float32)
        .astype(jnp.bfloat16)
        .reshape(target, num_heads, head_dim)
    )
    grad_weights = jnp.einsum(
        "qhe,khe->hqk", grad_context, values_all, preferred_element_type=jnp.float32
    )
    self_delta = jnp.sum(probs_self * grad_weights, -1, keepdims=True)
    grad_self_scores = (probs_self * (grad_weights - self_delta)).astype(jnp.bfloat16)
    grad_queries_self = (
        jnp.einsum("hqk,khe->qhe", grad_self_scores, keys_all, preferred_element_type=jnp.float32)
        * score_scale
    ).astype(jnp.bfloat16)
    grad_keys_all = (
        jnp.einsum("hqk,qhe->khe", grad_self_scores, queries, preferred_element_type=jnp.float32)
        * score_scale
    )
    grad_values_all = jnp.einsum(
        "hqk,qhe->khe",
        probs_self.astype(jnp.bfloat16),
        grad_context,
        preferred_element_type=jnp.float32,
    )
    grad_new = jnp.stack(
        [
            grad_queries_self,
            grad_keys_all[prefix_len:].astype(jnp.bfloat16),
            grad_values_all[prefix_len:].astype(jnp.bfloat16),
        ]
    ).reshape(3, target, model_width)
    grad_tokens = grad_one + jnp.einsum(
        "cre,cde->rd", grad_new, self_qkv, preferred_element_type=jnp.float32
    )
    grad_input = plane_order(plane_gather(grad_tokens.astype(jnp.bfloat16))).astype(jnp.float32)
    grad_prefix_full = jnp.stack(
        [grad_keys_all[:prefix_len], grad_values_all[:prefix_len]]
    ).reshape(2, prefix_len, model_width)
    prefix_share = prefix_w.shape[3]
    plane_columns = lax.dynamic_slice_in_dim(
        grad_prefix_full, replica * seq_count * prefix_share, seq_count * prefix_share, 2
    )
    grad_prefix = lax.dynamic_slice_in_dim(plane_columns, seq * prefix_share, prefix_share, 2)
    plane_low = plane_columns.astype(jnp.bfloat16)
    for j in range(1, seq_count):
        grad_prefix = grad_prefix + swap(
            lax.dynamic_slice_in_dim(plane_low, (seq ^ j) * prefix_share, prefix_share, 2), j
        ).astype(jnp.float32)
    new_down_m, new_down_v, new_down_w = adam_update(grad_down[None], down_m, down_v, down_w, 0.06)
    new_up_m, new_up_v, new_up_w = adam_update(grad_up[None], up_m, up_v, up_w, 0.02)
    new_prefix_m, new_prefix_v, new_prefix_w = adam_update(
        grad_prefix[None], prefix_m, prefix_v, prefix_w, 2.0
    )

    def group_sum(difference):
        total = difference.astype(jnp.bfloat16)
        bits = 1
        while bits < grp_size:
            other = lax.ppermute(total, "grp", [(j, j ^ bits) for j in range(grp_size)])
            total = total.astype(jnp.float32) + other.astype(jnp.float32)
            bits *= 2
            if bits < grp_size:
                total = total.astype(jnp.bfloat16)
        return total

    summed = (
        group_sum(down_outer - new_down_w[0]),
        group_sum(up_outer - new_up_w[0]),
        group_sum(prefix_outer - new_prefix_w[0]),
    )
    group_count = lax.axis_size("grp")
    outer_results = []
    for outer_weight, momentum, difference in (
        (down_outer, down_mom, summed[0]),
        (up_outer, up_mom, summed[1]),
        (prefix_outer, prefix_mom, summed[2]),
    ):
        average = difference / group_count
        momentum_new = OUTER_MOMENTUM * momentum + average
        outer_results.append(momentum_new)
        outer_results.append(outer_weight - OUTER_RATE * (average + OUTER_MOMENTUM * momentum_new))
    return (
        output[None],
        grad_input[None],
        grad_memory[None],
        grad_down[None],
        grad_up[None],
        grad_prefix[None],
        new_down_m,
        new_down_v,
        new_down_w,
        new_up_m,
        new_up_v,
        new_up_w,
        new_prefix_m,
        new_prefix_v,
        new_prefix_w,
        outer_results[0],
        outer_results[1],
        outer_results[2],
        outer_results[3],
        outer_results[4],
        outer_results[5],
    )


def solution(mesh):
    placed = (
        P("grp", None, None, None),
        P("grp", None, "mem", None),
        P("grp", None, None, None),
        P("grp", None),
        P("grp", None),
        P(),
        P(),
        P(),
        P(),
        P(),
        P(),
        P(),
        P(),
        P("grp", "mem", None),
        P("grp", "mem", None),
        P("grp", None, None, "mem"),
        P("grp", "mem", None),
        P("grp", "mem", None),
        P("grp", "mem", None),
        P("grp", "mem", None),
        P("grp", None, None, "mem"),
        P("grp", None, None, "mem"),
        P("mem", None),
        P("mem", None),
        P(None, None, "mem"),
        P("mem", None),
        P("mem", None),
        P(None, None, "mem"),
    )
    return jax.shard_map(
        local,
        mesh=mesh,
        in_specs=placed,
        out_specs=(
            P("grp", None, None, None),
            P("grp", None, None, None),
            P("grp", None, "mem", None),
            P("grp", "mem", None),
            P("grp", "mem", None),
            P("grp", None, None, "mem"),
            P("grp", "mem", None),
            P("grp", "mem", None),
            P("grp", "mem", None),
            P("grp", "mem", None),
            P("grp", "mem", None),
            P("grp", "mem", None),
            P("grp", None, None, "mem"),
            P("grp", None, None, "mem"),
            P("grp", None, None, "mem"),
            P("mem", None),
            P("mem", None),
            P("mem", None),
            P("mem", None),
            P(None, None, "mem"),
            P(None, None, "mem"),
        ),
        check_vma=False,
    )
```

```python
import functools

import jax
import jax.numpy as jnp
from jax import lax
from jax.experimental import pallas as pl
from jax.experimental.pallas import tpu as pltpu
from jax.sharding import PartitionSpec as P

HDIM = 64
STEP = 10


EPSILON = 1e-05
NEGATIVE = -1e30
ADAPTER_SCALE = 4.0
OUTER_MOMENTUM = 0.9
OUTER_RATE = 0.7
LANES = 128
FFN_BLOCK = 1024
RESIDENT_POSITIONS = 1024
VMEM_LIMIT = 16 * 1024 * 1024
LOW = jnp.bfloat16
FULL = jnp.float32


def normalize(values_in, gain_row, bias_row):
    centered = values_in - jnp.mean(values_in, -1, keepdims=True)
    scale_inv = lax.rsqrt(jnp.mean(centered * centered, -1, keepdims=True) + EPSILON)
    normal = centered * scale_inv
    return (normal * gain_row + bias_row, normal, scale_inv)


def normalize_back(gradient, normal, scale_inv, gain_row):
    scaled = gradient * gain_row
    return scale_inv * (
        scaled
        - jnp.mean(scaled, -1, keepdims=True)
        - normal * jnp.mean(scaled * normal, -1, keepdims=True)
    )


def dot_nn(left, right):
    return lax.dot_general(left, right, (((1,), (0,)), ((), ())), preferred_element_type=FULL)


def dot_nt(left, right):
    return lax.dot_general(left, right, (((1,), (1,)), ((), ())), preferred_element_type=FULL)


def dot_tn(left, right):
    return lax.dot_general(left, right, (((0,), (0,)), ((), ())), preferred_element_type=FULL)


def gelu_both(pre_act):
    tail = jnp.exp(-0.5 * pre_act * pre_act)
    inv = pl.reciprocal(1.0 + (0.3275911 * 0.7071067811865476) * jnp.abs(pre_act))
    poly = inv * (
        0.127414796
        + inv * (-0.142248368 + inv * (0.7107068705 + inv * (-0.7265760135 + inv * 0.5307027145)))
    )
    lower = poly * tail
    cdf = jnp.where(pre_act < 0, lower, 1.0 - lower)
    return pre_act * cdf, cdf + pre_act * (tail * 0.3989422804014327)


def first_lanes(shape):
    return lax.broadcasted_iota(jnp.int32, shape, 1) < HDIM


def stack_heads(pair):
    first = first_lanes(pair.shape)
    none = jnp.zeros_like(pair)
    return jnp.concatenate([jnp.where(first, pair, none), jnp.where(first, none, pair)], axis=0)


def merge_heads(stacked):
    rows = stacked.shape[0] // 2
    return jnp.where(first_lanes((rows, LANES)), stacked[:rows], stacked[rows:])


def scaled(queries):
    return queries * jnp.asarray(HDIM ** (-0.5), LOW)


def attend(stacked, keys, values, allowed):
    scores = jnp.where(allowed, dot_nt(stacked, keys), NEGATIVE)
    top = jnp.max(scores, -1, keepdims=True)
    expo = jnp.exp(scores - top).astype(LOW)
    total = jnp.sum(expo.astype(FULL), -1, keepdims=True)
    return dot_nn(expo, values) / total, top + jnp.log(total)


def attend_back(stacked, keys, values, allowed, log_total, grad_stacked):
    scores = jnp.where(allowed, dot_nt(stacked, keys), NEGATIVE)
    probs = jnp.exp(scores - log_total)
    grad_probs = dot_nt(grad_stacked, values)
    delta = jnp.sum(probs * grad_probs, -1, keepdims=True)
    grad_scores = (probs * (grad_probs - delta)).astype(LOW)
    grad_queries = merge_heads(dot_nn(grad_scores, keys)) * (HDIM ** (-0.5))
    grad_keys = dot_tn(grad_scores, stacked)
    grad_values = dot_tn(probs.astype(LOW), grad_stacked)
    return grad_queries.astype(LOW), grad_keys, grad_values


def self_allowed(length, target, prefix_pad, prefix_len):
    shape = (2 * target, prefix_pad + target)
    row = lax.broadcasted_iota(jnp.int32, shape, 0)
    row = jnp.where(row >= target, row - target, row)
    column = lax.broadcasted_iota(jnp.int32, shape, 1)
    key = column - prefix_pad
    return (column < prefix_len) | (key >= 0) & (key <= row) & (key < length)


def put_lanes(columns, shape):
    lane = lax.broadcasted_iota(jnp.int32, shape, 1)
    result = jnp.zeros(shape, FULL)
    for j, column in enumerate(columns):
        result = jnp.where(lane == j, column, result)
    return result


def lane_pairs(width):
    return [slice(at, at + LANES) for at in range(0, width, LANES)]


def pair_logs(log_total, j):
    return jnp.concatenate(
        [log_total[:, 2 * j : 2 * j + 1], log_total[:, 2 * j + 1 : 2 * j + 2]], axis=0
    )


def place(members):
    device = lax.axis_index("mem")
    return device, lax.rem(device, members), lax.div(device, members)


def self_forward_kernel(members, prefix_len, size, lengths, tokens_all, *refs):
    pieces, (self_qkv, self_out), refs = refs[:size], refs[size : size + 2], refs[size + 2 :]
    count = (len(refs) - 9) // 2
    sources, refs = refs[:count], refs[count:]
    prefix, qkv, log_total, summed = refs[:4]
    kept = refs[4 : 4 + count]
    tokens, ordered, qkv_w, out_w, sems = refs[4 + count :]
    device, seq, unused = place(members)
    moves = [pltpu.make_async_copy(tokens_all.at[0, seq], tokens, sems.at[0])]
    for j in range(3):
        moves.append(pltpu.make_async_copy(self_qkv.at[j], qkv_w.at[j], sems.at[1 + j]))
    moves.append(pltpu.make_async_copy(self_out, out_w, sems.at[4]))
    for j in range(count):
        moves.append(pltpu.make_async_copy(sources[j], kept[j], sems.at[5 + j]))
    for move in moves:
        move.start()
    share = ordered.shape[3]
    for k, piece in enumerate(pieces):
        ordered[device ^ k] = piece[...]
    for j in range(size):
        for c in range(2):
            prefix[c, :, j * share : (j + 1) * share] = ordered[j, c]
    moves[0].wait()
    rows = tokens[...]
    target, width = rows.shape
    for j in range(3):
        moves[1 + j].wait()
        qkv[j] = dot_nn(rows, qkv_w[j]).astype(LOW)
    allowed = self_allowed(lengths[0, seq], target, prefix.shape[1], prefix_len)
    contexts, logs = [], []
    for part in lane_pairs(width):
        keys = jnp.concatenate([prefix[0, :, part], qkv[1, :, part]], axis=0)
        values = jnp.concatenate([prefix[1, :, part], qkv[2, :, part]], axis=0)
        context, log = attend(stack_heads(scaled(qkv[0, :, part])), keys, values, allowed)
        contexts.append(merge_heads(context).astype(LOW))
        logs += [log[:target], log[target:]]
    log_total[...] = put_lanes(logs, log_total.shape)
    moves[4].wait()
    summed[...] = rows.astype(FULL) + dot_nn(jnp.concatenate(contexts, axis=1), out_w[...])
    for move in moves[5:]:
        move.wait()


def cross_forward_kernel(members, lengths, summed_one, gains, biases, qkv_w, out_w, *refs):
    blocks = refs[:-5]
    queries, keys_values, log_total, summed_two, mem_rows = refs[-5:]
    device, seq, unused = place(members)
    source = blocks[0].shape[0]
    target, width = queries.shape
    for k, block in enumerate(blocks):
        at = pl.multiple_of((device ^ k) * source, source)
        mem_rows[pl.ds(at, source), :] = block[...]
    hidden = normalize(summed_one[...], gains[0:1], biases[0:1])[0]
    queries[...] = dot_nn(hidden.astype(LOW), qkv_w[0]).astype(LOW)
    for j in range(2):
        keys_values[j] = dot_nn(mem_rows[...], qkv_w[1 + j]).astype(LOW)
    allowed = (
        lax.broadcasted_iota(jnp.int32, (2 * target, mem_rows.shape[0]), 1) < lengths[0, seq]
    )
    contexts, logs = [], []
    for part in lane_pairs(width):
        context, log = attend(
            stack_heads(scaled(queries[:, part])),
            keys_values[0, :, part],
            keys_values[1, :, part],
            allowed,
        )
        contexts.append(merge_heads(context).astype(LOW))
        logs += [log[:target], log[target:]]
    log_total[...] = put_lanes(logs, log_total.shape)
    summed_two[...] = hidden + dot_nn(jnp.concatenate(contexts, axis=1), out_w[...])


def ffn_forward_kernel(summed_two, gains, biases, in_w, out_w, normed, slope, partial):
    hidden = normalize(summed_two[...], gains[1:2], biases[1:2])[0]
    low = hidden.astype(LOW)
    normed[...] = low
    inner = in_w.shape[1]
    parts = [slice(at, at + FFN_BLOCK) for at in range(0, inner, FFN_BLOCK)]
    pre = dot_nn(low, in_w[:, parts[0]])
    total = hidden
    for j, part in enumerate(parts):
        following = dot_nn(low, in_w[:, parts[j + 1]]) if j + 1 < len(parts) else None
        act, slope_full = gelu_both(pre)
        slope[:, part] = slope_full.astype(LOW)
        total = total + dot_nn(act.astype(LOW), out_w[part, :])
        pre = following
    partial[...] = total


def adapter_kernel(members, lengths, partial, normed, gains, biases, cotangent_all, *refs):
    pieces = refs[: -(3 + members + 6)]
    output, grad_ffn, grad_hidden = refs[len(pieces) : len(pieces) + 3]
    grad_pieces = refs[len(pieces) + 3 : -6]
    down, up, grad_down, grad_up, cotangent, sem = refs[-6:]
    device, seq, replica = place(members)
    move = pltpu.make_async_copy(cotangent_all.at[0, seq], cotangent, sem)
    move.start()
    rows = pieces[0].shape[0]
    half = rows // 2
    wide = down.shape[1]
    for k, piece in enumerate(pieces):
        at = pl.multiple_of((device ^ k) * rows, rows)
        down[pl.ds(at, half), :] = piece[:half, :wide]
        down[pl.ds(at + half, half), :] = piece[:half, wide:]
        up[pl.ds(pl.multiple_of((device ^ k) * half, half), half), :] = piece[half:, :]
    act, slope = gelu_both(dot_nn(normed[...], down[...]))
    act = act.astype(LOW)
    total = partial[...] + ADAPTER_SCALE * dot_nn(act, up[...])
    rows_out, normal, inverse = normalize(total, gains[2:3], biases[2:3])
    output[...] = rows_out.astype(LOW)
    live = lax.broadcasted_iota(jnp.int32, (total.shape[0], 1), 0) < lengths[0, seq]
    move.wait()
    grad_three = normalize_back(
        jnp.where(live, cotangent[...].astype(FULL), 0.0), normal, inverse, gains[2:3]
    )
    grad_ffn[...] = grad_three.astype(LOW)
    grad_adapted = (ADAPTER_SCALE * grad_three).astype(LOW)
    grad_pre = (dot_nt(grad_adapted, up[...]) * slope).astype(LOW)
    grad_hidden[...] = grad_three + dot_nt(grad_pre, down[...])
    grad_down[...] = dot_tn(normed[...], grad_pre).astype(LOW)
    grad_up[...] = dot_tn(act, grad_adapted).astype(LOW)
    for k, piece in enumerate(grad_pieces):
        owner = replica * members + (seq ^ k)
        at = pl.multiple_of(owner * rows, rows)
        piece[:half, :wide] = grad_down[pl.ds(at, half), :]
        piece[:half, wide:] = grad_down[pl.ds(at + half, half), :]
        piece[half:, :] = grad_up[pl.ds(pl.multiple_of(owner * half, half), half), :]


def ffn_backward_kernel(
    grad_ffn, grad_hidden, summed_two, gains, biases, in_w, out_w, slope, grad_two
):
    low = grad_ffn[...]
    inner = in_w.shape[1]
    parts = [slice(at, at + FFN_BLOCK) for at in range(0, inner, FFN_BLOCK)]
    grad_act = dot_nt(low, out_w[parts[0], :])
    total = grad_hidden[...]
    for j, part in enumerate(parts):
        following = dot_nt(low, out_w[parts[j + 1], :]) if j + 1 < len(parts) else None
        grad_pre = (grad_act * slope[:, part].astype(FULL)).astype(LOW)
        total = total + dot_nt(grad_pre, in_w[:, part])
        grad_act = following
    unused, normal, inverse = normalize(summed_two[...], gains[1:2], biases[1:2])
    grad_two[...] = normalize_back(total, normal, inverse, gains[1:2])


def cross_backward_kernel(
    members,
    lengths,
    grad_two,
    summed_one,
    gains,
    biases,
    qkv_w,
    out_w,
    queries,
    keys_values,
    log_total,
    later_source,
    grad_one,
    later,
    *refs,
):
    grad_pieces = refs[:members]
    grad_keys, grad_values, grad_rows, sem = refs[members:]
    unused, seq, replica = place(members)
    target, width = queries.shape
    fetch = pltpu.make_async_copy(later_source, later, sem)
    fetch.start()
    grad_context = dot_nt(grad_two[...].astype(LOW), out_w[...]).astype(LOW)
    allowed = (
        lax.broadcasted_iota(jnp.int32, (2 * target, keys_values.shape[1]), 1) < lengths[0, seq]
    )
    grad_queries = []
    for j, part in enumerate(lane_pairs(width)):
        into_queries, into_keys, into_values = attend_back(
            stack_heads(scaled(queries[:, part])),
            keys_values[0, :, part],
            keys_values[1, :, part],
            allowed,
            pair_logs(log_total, j),
            stack_heads(grad_context[:, part]),
        )
        grad_queries.append(into_queries)
        grad_keys[:, part] = into_keys.astype(LOW)
        grad_values[:, part] = into_values.astype(LOW)
    rows = grad_rows.shape[0]
    mine = pl.ds(pl.multiple_of(replica * rows, rows), rows)
    grad_rows[...] = (
        dot_nt(grad_keys[mine, :], qkv_w[1]) + dot_nt(grad_values[mine, :], qkv_w[2])
    ).astype(LOW)
    source = rows // members
    for k, piece in enumerate(grad_pieces):
        piece[...] = grad_rows[pl.ds(pl.multiple_of((seq ^ k) * source, source), source), :]
    total = grad_two[...] + dot_nt(jnp.concatenate(grad_queries, axis=1), qkv_w[0])
    unused, normal, inverse = normalize(summed_one[...], gains[0:1], biases[0:1])
    grad_one[...] = normalize_back(total, normal, inverse, gains[0:1])
    fetch.wait()


def self_backward_kernel(
    members,
    lengths_prefix,
    lengths,
    grad_one,
    prefix,
    out_w,
    qkv,
    log_total,
    later_source,
    grad_qkv,
    later,
    *refs,
):
    grad_pieces, (blocks, sem) = refs[:members], refs[members:]
    unused, seq, replica = place(members)
    fetch = pltpu.make_async_copy(later_source, later, sem)
    fetch.start()
    target, width = grad_one.shape
    pad = prefix.shape[1]
    grad_context = dot_nt(grad_one[...].astype(LOW), out_w[...]).astype(LOW)
    allowed = self_allowed(lengths[0, seq], target, pad, lengths_prefix)
    size, unused, unused, share = blocks.shape
    prefix_grads = ([], [])
    for j, part in enumerate(lane_pairs(width)):
        into_queries, into_keys, into_values = attend_back(
            stack_heads(scaled(qkv[0, :, part])),
            jnp.concatenate([prefix[0, :, part], qkv[1, :, part]], axis=0),
            jnp.concatenate([prefix[1, :, part], qkv[2, :, part]], axis=0),
            allowed,
            pair_logs(log_total, j),
            stack_heads(grad_context[:, part]),
        )
        grad_qkv[0, :, part] = into_queries
        grad_qkv[1, :, part] = into_keys[pad:].astype(LOW)
        grad_qkv[2, :, part] = into_values[pad:].astype(LOW)
        prefix_grads[0].append(into_keys[:pad].astype(LOW))
        prefix_grads[1].append(into_values[:pad].astype(LOW))
    for c in range(2):
        row = jnp.concatenate(prefix_grads[c], axis=1)
        for j in range(size):
            blocks[j, c] = row[:, j * share : (j + 1) * share]
    for k, piece in enumerate(grad_pieces):
        piece[...] = blocks[replica * members + (seq ^ k)]
    fetch.wait()


def self_project_kernel(grad_one, qkv_w, grad_qkv, low, high):
    total = grad_one[...]
    for j in range(3):
        total = total + dot_nt(grad_qkv[j], qkv_w[j])
    half = low.shape[0]
    low[...] = total[:half].astype(LOW)
    high[...] = total[half:].astype(LOW)


def gather_kernel(members, counts, *refs):
    pieces, result, held, sems = refs[:-3], refs[-3], refs[-2], refs[-1]
    unused, seq, unused = place(members)
    moves, start = [], 0
    for k, count in enumerate(counts):
        at = 0
        for piece in pieces[start : start + count]:
            held[k, at : at + piece.shape[0], :] = piece[...].astype(held.dtype)
            at += piece.shape[0]
        start += count
        move = pltpu.make_async_copy(held.at[k], result.at[seq ^ k], sems.at[k])
        move.start()
        moves.append(move)
    for move in moves:
        move.wait()


def shaped(shape, dtype):
    return jax.ShapeDtypeStruct(shape, dtype)


def call_whole(
    kernel, spaces, outs, scratch, args, limit=VMEM_LIMIT, out_spaces=None, after=(), micros=0
):
    spaces = list(spaces) + [pltpu.VMEM] * (len(args) - len(spaces)) + [pl.ANY] * len(after)
    if after:
        inner_kernel, count = kernel, len(args)

        def kernel(*refs):
            inner_kernel(*refs[:count], *refs[count + len(after) :])

        args = tuple(args) + tuple(after)
    out_spaces = out_spaces or [pltpu.VMEM] * len(outs)
    return pl.pallas_call(
        kernel,
        in_specs=[pl.BlockSpec(memory_space=space) for space in spaces],
        out_specs=[pl.BlockSpec(memory_space=space) for space in out_spaces],
        out_shape=outs,
        scratch_shapes=scratch,
        compiler_params=pltpu.CompilerParams(vmem_limit_bytes=limit),
        cost_estimate=pl.CostEstimate(flops=1000 + micros * 10**9, bytes_accessed=1000, transcendentals=0),
    )(*args)


def adam_update(gradient, first_moment, second_moment, weight, step_rate):
    first_new = 0.9 * first_moment + 0.1 * gradient
    second_new = 0.999 * second_moment + 0.001 * gradient * gradient
    corrected_one = first_new / (1.0 - 0.9**STEP)
    corrected_two = second_new / (1.0 - 0.999**STEP)
    weight_new = weight - step_rate * (
        corrected_one / (jnp.sqrt(corrected_two) + 1e-08) + 0.01 * weight
    )
    return (first_new, second_new, weight_new)


def local(
    dec_input,
    memory,
    out_grad,
    tgt_lengths,
    src_lengths,
    self_qkv,
    self_out,
    cross_qkv,
    cross_out,
    ffn_in,
    ffn_out,
    norm_gains,
    norm_biases,
    down_w,
    up_w,
    prefix_w,
    down_m,
    down_v,
    up_m,
    up_v,
    prefix_m,
    prefix_v,
    down_outer,
    up_outer,
    prefix_outer,
    down_mom,
    up_mom,
    prefix_mom,
):
    seq_count, target, model_width = dec_input.shape[1:]
    source = memory.shape[2]
    prefix_len = prefix_w.shape[2]
    mem_size = lax.axis_size("mem")
    grp_size = lax.axis_size("grp")
    replicas = mem_size // seq_count
    device = lax.axis_index("mem")
    seq = device % seq_count
    replica = device // seq_count
    adapt = down_w.shape[2]
    inner = ffn_in.shape[1]
    share_rows = down_w.shape[1]
    half_rows = share_rows // 2
    positions = mem_size * source
    resident = positions <= RESIDENT_POSITIONS
    half = target // 2
    bound = functools.partial

    def swap(values_in, bits):
        return lax.ppermute(values_in, "mem", [(j, j ^ bits) for j in range(mem_size)])

    def pick(values_in, index):
        return lax.dynamic_index_in_dim(values_in, index, 0, keepdims=False)

    def pack(down_part, up_part):
        return jnp.concatenate(
            [
                jnp.concatenate([down_part[:half_rows], down_part[half_rows:]], axis=1),
                up_part,
            ],
            axis=0,
        )

    def unpack(packed):
        top = packed[:half_rows]
        return (
            jnp.concatenate([top[:, :adapt], top[:, adapt:]], axis=0),
            packed[half_rows:],
        )

    def in_order(counts, pieces, dtype, after=()):
        rows = sum(piece.shape[0] for piece in pieces[: counts[0]])
        shape = (seq_count, rows, model_width)
        (result,) = call_whole(
            bound(gather_kernel, seq_count, counts),
            [],
            [shaped(shape, dtype)],
            [pltpu.VMEM(shape, dtype), pltpu.SemaphoreType.DMA((seq_count,))],
            tuple(pieces),
            out_spaces=[pl.ANY],
            after=after,
        )
        return result

    replica_bits = [seq_count * 2**j for j in range(replicas.bit_length() - 1)]
    members = range(seq_count)
    prefix_rows = prefix_len + -prefix_len % 16
    prefix_low = jnp.pad(
        prefix_w[0].astype(LOW), ((0, 0), (0, prefix_rows - prefix_len), (0, 0))
    )
    mem_send = [pick(memory[0], seq ^ j) for j in members]
    share_low = pack(down_w[0], up_w[0]).astype(LOW)
    partners = members[1:]
    mem_blocks = {0: mem_send[0]}
    prefix_pieces = {0: prefix_low}
    shares = {0: share_low}
    for bit in replica_bits:
        for k, piece in list(prefix_pieces.items()):
            prefix_pieces[k ^ bit] = swap(piece, bit)
    for j in partners:
        mem_blocks[j] = swap(mem_send[j], j)
    bit = replica_bits[0]
    mem_blocks[bit] = swap(mem_blocks[0], bit)
    plane_blocks = jnp.concatenate([mem_blocks[j] for j in partners], axis=0)
    replica_offsets = sorted(prefix_pieces)
    joined = jnp.concatenate([prefix_pieces[k] for k in replica_offsets], axis=0)
    joined, plane_blocks = lax.optimization_barrier((joined, plane_blocks))
    arrived = [swap(joined, j) for j in partners]
    plane_blocks = swap(plane_blocks, bit)
    for i, j in enumerate(partners):
        for n, k in enumerate(replica_offsets):
            prefix_pieces[k ^ j] = arrived[i][2 * n : 2 * n + 2]
    shares[0], arrived = lax.optimization_barrier((shares[0], arrived))
    for bit in replica_bits:
        for k, piece in list(shares.items()):
            shares[k ^ bit] = swap(piece, bit)
    for j in partners:
        shares[j] = swap(shares[0], j)
    prefix_pieces = [prefix_pieces[k] for k in range(mem_size)]

    rows_full = shaped((target, model_width), FULL)
    rows_low = shaped((target, model_width), LOW)
    logs = shaped((target, LANES), FULL)
    lengths_space = [pltpu.SMEM]
    dma = pltpu.SemaphoreType.DMA

    weights = (cross_qkv, cross_out, ffn_in, ffn_out) if resident else ()
    prefix, qkv, self_log, summed_one, *kept = call_whole(
        bound(self_forward_kernel, seq_count, prefix_len, mem_size),
        [pltpu.SMEM, pltpu.HBM] + [pltpu.VMEM] * mem_size + [pltpu.HBM] * (len(weights) + 2),
        [
            shaped((2, prefix_rows, model_width), LOW),
            shaped((3, target, model_width), LOW),
            logs,
            rows_full,
        ]
        + [pltpu.VMEM(weight.shape, LOW) for weight in weights],
        [
            pltpu.VMEM((target, model_width), LOW),
            pltpu.VMEM((mem_size, 2, prefix_rows, prefix_w.shape[3]), LOW),
            pltpu.VMEM(self_qkv.shape, LOW),
            pltpu.VMEM(self_out.shape, LOW),
            dma((len(weights) + 5,)),
        ],
        (tgt_lengths, dec_input, *prefix_pieces, self_qkv, self_out, *weights),
        limit=VMEM_LIMIT + 8 * 1024 * 1024,
        micros=11,
    )
    if resident:
        cross_qkv, cross_out, ffn_in, ffn_out = kept
    summed_one, plane_blocks, *moved = lax.optimization_barrier(
        (summed_one, plane_blocks, *[shares[k] for k in replica_offsets[1:]])
    )
    shares.update(zip(replica_offsets[1:], moved))
    for i, j in enumerate(partners):
        mem_blocks[j ^ replica_bits[0]] = plane_blocks[i * source : (i + 1) * source]
    for bit in replica_bits[1:]:
        known = sorted(mem_blocks)
        moved = swap(jnp.concatenate([mem_blocks[k] for k in known], axis=0), bit)
        for i, k in enumerate(known):
            mem_blocks[k ^ bit] = moved[i * source : (i + 1) * source]
    for k in replica_offsets[1:]:
        for j in partners:
            shares[k ^ j] = swap(shares[k], j)
    mem_blocks = [mem_blocks[k] for k in range(mem_size)]
    shares = [shares[k] for k in range(mem_size)]
    cross_limit = VMEM_LIMIT * (1 if resident else 2)
    cross_queries, keys_values, cross_log, summed_two = call_whole(
        bound(cross_forward_kernel, seq_count),
        lengths_space,
        [rows_low, shaped((2, positions, model_width), LOW), logs, rows_full],
        [pltpu.VMEM((positions, model_width), LOW)],
        (src_lengths, summed_one, norm_gains, norm_biases, cross_qkv, cross_out, *mem_blocks),
        cross_limit,
    )
    normed, slope, partial = call_whole(
        ffn_forward_kernel,
        [],
        [rows_low, shaped((target, inner), LOW), rows_full],
        [],
        (summed_two, norm_gains, norm_biases, ffn_in, ffn_out),
    )
    output_rows, grad_ffn, grad_hidden, *grad_pieces = call_whole(
        bound(adapter_kernel, seq_count),
        [pltpu.SMEM] + [pltpu.VMEM] * 4 + [pltpu.HBM],
        [rows_low, rows_low, rows_full] + [shaped((share_rows, model_width), LOW)] * seq_count,
        [
            pltpu.VMEM((model_width, adapt), LOW),
            pltpu.VMEM((adapt, model_width), LOW),
            pltpu.VMEM((model_width, adapt), LOW),
            pltpu.VMEM((adapt, model_width), LOW),
            pltpu.VMEM((target, model_width), LOW),
            dma,
        ],
        (tgt_lengths, partial, normed, norm_gains, norm_biases, out_grad, *shares),
    )
    output_one, output_two = swap(output_rows, 1), swap(output_rows, 2)
    grad_pieces = [grad_pieces[0]] + [
        swap(grad_pieces[j], j) for j in range(1, seq_count)
    ]
    (grad_two,) = call_whole(
        ffn_backward_kernel,
        [],
        [rows_full],
        [],
        (grad_ffn, grad_hidden, summed_two, norm_gains, norm_biases, ffn_in, ffn_out, slope),
    )
    plane_rows = seq_count * source
    grad_one, out_later, *grad_mem_pieces = call_whole(
        bound(cross_backward_kernel, seq_count),
        lengths_space + [pltpu.VMEM] * 9 + [pltpu.HBM],
        [rows_full, pltpu.VMEM(self_out.shape, LOW)]
        + [shaped((source, model_width), LOW)] * seq_count,
        [
            pltpu.VMEM((positions, model_width), LOW),
            pltpu.VMEM((positions, model_width), LOW),
            pltpu.VMEM((plane_rows, model_width), LOW),
            dma,
        ],
        (
            src_lengths,
            grad_two,
            summed_one,
            norm_gains,
            norm_biases,
            cross_qkv,
            cross_out,
            cross_queries,
            keys_values,
            cross_log,
            self_out,
        ),
        cross_limit,
    )
    grad_one, output_one, output_two = lax.optimization_barrier(
        (grad_one, output_one, output_two)
    )
    output_low, output_high = swap(output_two[:half], 1), swap(output_one[half:], 2)
    grad_mem_pieces = [grad_mem_pieces[0]] + [
        swap(grad_mem_pieces[j], j) for j in members[1:]
    ]
    share_shape = (2, prefix_rows, prefix_w.shape[3])
    grad_qkv, qkv_later, *prefix_sent = call_whole(
        bound(self_backward_kernel, seq_count, prefix_len),
        lengths_space + [pltpu.VMEM] * 5 + [pltpu.HBM],
        [shaped((3, target, model_width), LOW), pltpu.VMEM(self_qkv.shape, LOW)]
        + [shaped(share_shape, LOW)] * seq_count,
        [pltpu.VMEM((mem_size, *share_shape), LOW), dma],
        (tgt_lengths, grad_one, prefix, out_later, qkv, self_log, self_qkv),
        after=(output_one, output_two, *grad_pieces[1:]),
    )
    low, high = call_whole(
        self_project_kernel,
        [],
        [shaped((half, model_width), LOW)] * 2,
        [],
        (grad_one, qkv_later, grad_qkv),
        after=(output_low, output_high, *grad_mem_pieces[1:]),
    )
    low, grad_pieces, prefix_sent = lax.optimization_barrier((low, grad_pieces, prefix_sent))
    low_two, high_one = swap(low, 2), swap(high, 1)
    low_one, high_two = swap(low, 1), swap(high, 2)
    low_three, high_three = swap(low_two, 1), swap(high_one, 2)
    packed_total = sum(piece.astype(FULL) for piece in grad_pieces)
    grad_down, grad_up = unpack(packed_total)
    prefix_arrived = [prefix_sent[0]] + [swap(prefix_sent[j], j) for j in members[1:]]
    grad_prefix = sum(piece.astype(FULL) for piece in prefix_arrived)[:, :prefix_len]
    output = in_order(
        (1, 1, 1, 2), (output_rows, output_one, output_two, output_low, output_high), LOW
    )
    grad_memory = in_order((1,) * seq_count, grad_mem_pieces, FULL)
    new_down_m, new_down_v, new_down_w = adam_update(grad_down[None], down_m, down_v, down_w, 0.06)
    new_up_m, new_up_v, new_up_w = adam_update(grad_up[None], up_m, up_v, up_w, 0.02)
    new_prefix_m, new_prefix_v, new_prefix_w = adam_update(
        grad_prefix[None], prefix_m, prefix_v, prefix_w, 2.0
    )

    def group_sum(difference):
        total = difference.astype(LOW)
        bits = 1
        while bits < grp_size:
            if bits == 2:
                total = lax.optimization_barrier((total, low_two, high_one))[0]
            other = lax.ppermute(total, "grp", [(j, j ^ bits) for j in range(grp_size)])
            total = total.astype(jnp.float32) + other.astype(jnp.float32)
            bits *= 2
            if bits < grp_size:
                total = total.astype(jnp.bfloat16)
        return total

    summed = unpack(
        group_sum(pack(down_outer - new_down_w[0], up_outer - new_up_w[0]))
    ) + (group_sum(prefix_outer - new_prefix_w[0]),)
    group_count = lax.axis_size("grp")
    outer_results = []
    for outer_weight, momentum, difference in (
        (down_outer, down_mom, summed[0]),
        (up_outer, up_mom, summed[1]),
        (prefix_outer, prefix_mom, summed[2]),
    ):
        average = difference / group_count
        momentum_new = OUTER_MOMENTUM * momentum + average
        outer_results.append(momentum_new)
        outer_results.append(outer_weight - OUTER_RATE * (average + OUTER_MOMENTUM * momentum_new))
    grad_input = in_order(
        (2,) * seq_count,
        (low, high, low_one, high_one, low_two, high_two, low_three, high_three),
        FULL,
        (output, grad_memory, new_down_m, new_up_m, new_prefix_m, *outer_results),
    )
    return (
        output[None],
        grad_input[None],
        grad_memory[None],
        grad_down[None],
        grad_up[None],
        grad_prefix[None],
        new_down_m,
        new_down_v,
        new_down_w,
        new_up_m,
        new_up_v,
        new_up_w,
        new_prefix_m,
        new_prefix_v,
        new_prefix_w,
        outer_results[0],
        outer_results[1],
        outer_results[2],
        outer_results[3],
        outer_results[4],
        outer_results[5],
    )


def solution(mesh):
    placed = (
        P("grp", None, None, None),
        P("grp", None, "mem", None),
        P("grp", None, None, None),
        P("grp", None),
        P("grp", None),
        P(),
        P(),
        P(),
        P(),
        P(),
        P(),
        P(),
        P(),
        P("grp", "mem", None),
        P("grp", "mem", None),
        P("grp", None, None, "mem"),
        P("grp", "mem", None),
        P("grp", "mem", None),
        P("grp", "mem", None),
        P("grp", "mem", None),
        P("grp", None, None, "mem"),
        P("grp", None, None, "mem"),
        P("mem", None),
        P("mem", None),
        P(None, None, "mem"),
        P("mem", None),
        P("mem", None),
        P(None, None, "mem"),
    )
    return jax.shard_map(
        local,
        mesh=mesh,
        in_specs=placed,
        out_specs=(
            P("grp", None, None, None),
            P("grp", None, None, None),
            P("grp", None, "mem", None),
            P("grp", "mem", None),
            P("grp", "mem", None),
            P("grp", None, None, "mem"),
            P("grp", "mem", None),
            P("grp", "mem", None),
            P("grp", "mem", None),
            P("grp", "mem", None),
            P("grp", "mem", None),
            P("grp", "mem", None),
            P("grp", None, None, "mem"),
            P("grp", None, None, "mem"),
            P("grp", None, None, "mem"),
            P("mem", None),
            P("mem", None),
            P("mem", None),
            P("mem", None),
            P(None, None, "mem"),
            P(None, None, "mem"),
        ),
        check_vma=False,
    )
```

```python
import functools

import jax
import jax.numpy as jnp
from jax import lax
from jax.experimental import pallas as pl
from jax.experimental.pallas import tpu as pltpu
from jax.sharding import PartitionSpec as P

HDIM = 64
STEP = 10


EPSILON = 1e-05
NEGATIVE = -1e30
ADAPTER_SCALE = 4.0
OUTER_MOMENTUM = 0.9
OUTER_RATE = 0.7
LANES = 128
FFN_BLOCK = 1024
RESIDENT_POSITIONS = 1024
SMALL_LIMIT = 6 * 1024 * 1024
VMEM_LIMIT = 10 * 1024 * 1024
LOW = jnp.bfloat16
FULL = jnp.float32


def normalize(values_in, gain_row, bias_row):
    centered = values_in - jnp.mean(values_in, -1, keepdims=True)
    scale_inv = lax.rsqrt(jnp.mean(centered * centered, -1, keepdims=True) + EPSILON)
    normal = centered * scale_inv
    return (normal * gain_row + bias_row, normal, scale_inv)


def normalize_back(gradient, normal, scale_inv, gain_row):
    scaled = gradient * gain_row
    return scale_inv * (
        scaled
        - jnp.mean(scaled, -1, keepdims=True)
        - normal * jnp.mean(scaled * normal, -1, keepdims=True)
    )


def dot_nn(left, right):
    return lax.dot_general(left, right, (((1,), (0,)), ((), ())), preferred_element_type=FULL)


def dot_nt(left, right):
    return lax.dot_general(left, right, (((1,), (1,)), ((), ())), preferred_element_type=FULL)


def dot_tn(left, right):
    return lax.dot_general(left, right, (((0,), (0,)), ((), ())), preferred_element_type=FULL)


def gelu_both(pre_act):
    tail = jnp.exp(-0.5 * pre_act * pre_act)
    inv = pl.reciprocal(1.0 + (0.3275911 * 0.7071067811865476) * jnp.abs(pre_act))
    poly = inv * (
        0.127414796
        + inv * (-0.142248368 + inv * (0.7107068705 + inv * (-0.7265760135 + inv * 0.5307027145)))
    )
    lower = poly * tail
    cdf = jnp.where(pre_act < 0, lower, 1.0 - lower)
    return pre_act * cdf, cdf + pre_act * (tail * 0.3989422804014327)


def first_lanes(shape):
    return lax.broadcasted_iota(jnp.int32, shape, 1) < HDIM


def stack_heads(pair):
    first = first_lanes(pair.shape)
    none = jnp.zeros_like(pair)
    return jnp.concatenate([jnp.where(first, pair, none), jnp.where(first, none, pair)], axis=0)


def merge_heads(stacked):
    rows = stacked.shape[0] // 2
    return jnp.where(first_lanes((rows, LANES)), stacked[:rows], stacked[rows:])


def scaled(queries):
    return queries * jnp.asarray(HDIM ** (-0.5), LOW)


def attend(stacked, keys, values, allowed):
    scores = jnp.where(allowed, dot_nt(stacked, keys), NEGATIVE)
    top = jnp.max(scores, -1, keepdims=True)
    expo = jnp.exp(scores - top).astype(LOW)
    total = jnp.sum(expo.astype(FULL), -1, keepdims=True)
    return dot_nn(expo, values) / total, top + jnp.log(total)


def attend_back(
    stacked, keys, values, allowed, log_total, grad_stacked, delta=None, skipped=0
):
    scores = jnp.where(allowed, dot_nt(stacked, keys), NEGATIVE)
    probs = jnp.exp(scores - log_total)
    grad_probs = dot_nt(grad_stacked, values)
    if delta is None:
        delta = jnp.sum(probs * grad_probs, -1, keepdims=True)
    grad_scores = (probs * (grad_probs - delta)).astype(LOW)
    grad_queries = merge_heads(dot_nn(grad_scores, keys)) * (HDIM ** (-0.5))
    grad_keys = dot_tn(grad_scores, stacked)[skipped:]
    grad_values = dot_tn(probs.astype(LOW), grad_stacked)[skipped:]
    return grad_queries.astype(LOW), grad_keys, grad_values


def self_allowed(length, target, prefix_pad, prefix_len):
    shape = (2 * target, prefix_pad + target)
    row = lax.broadcasted_iota(jnp.int32, shape, 0)
    row = jnp.where(row >= target, row - target, row)
    column = lax.broadcasted_iota(jnp.int32, shape, 1)
    key = column - prefix_pad
    return (column < prefix_len) | (key >= 0) & (key <= row) & (key < length)


def put_lanes(columns, shape):
    lane = lax.broadcasted_iota(jnp.int32, shape, 1)
    result = jnp.zeros(shape, FULL)
    for j, column in enumerate(columns):
        result = jnp.where(lane == j, column, result)
    return result


def lane_pairs(width):
    return [slice(at, at + LANES) for at in range(0, width, LANES)]


def pair_logs(log_total, j):
    return jnp.concatenate(
        [log_total[:, 2 * j : 2 * j + 1], log_total[:, 2 * j + 1 : 2 * j + 2]], axis=0
    )


def place(members):
    device = lax.axis_index("mem")
    return device, lax.rem(device, members), lax.div(device, members)


def first_kernel(members, memory, down_w, up_w, outward, *refs):
    blocks, (block, down, up, sems) = refs[: members - 1], refs[members - 1 :]
    unused, seq, unused = place(members)
    moves = [
        pltpu.make_async_copy(memory.at[0, seq], block, sems.at[0]),
        pltpu.make_async_copy(down_w.at[0], down, sems.at[1]),
        pltpu.make_async_copy(up_w.at[0], up, sems.at[2]),
    ]
    for k, partner in enumerate(blocks):
        moves.append(pltpu.make_async_copy(memory.at[0, seq ^ (k + 1)], partner, sems.at[3 + k]))
    for move in moves:
        move.start()
    for move in moves:
        move.wait()
    source = block.shape[0]
    half = up.shape[0]
    wide = down.shape[1]
    outward[:source, :] = block[...]
    outward[source : source + half, :wide] = down[:half, :].astype(LOW)
    outward[source : source + half, wide:] = down[half:, :].astype(LOW)
    outward[source + half :, :] = up[...].astype(LOW)


def join_kernel(windows, *refs):
    at = 0
    for piece, (start, stop) in zip(refs, windows):
        refs[-1][at : at + stop - start, :] = piece[start:stop, :]
        at += stop - start


def self_forward_kernel(members, prefix_len, offsets, lengths, tokens_all, *refs):
    pieces, (self_qkv, self_out) = refs[:members], refs[members : members + 2]
    refs = refs[members + 2 :]
    count = (len(refs) - 10) // 2
    sources, refs = refs[:count], refs[count:]
    prefix, qkv, log_total, summed, context_all = refs[:5]
    kept = refs[5 : 5 + count]
    tokens, ordered, qkv_w, out_w, sems = refs[5 + count :]
    device, seq, unused = place(members)
    moves = [pltpu.make_async_copy(tokens_all.at[0, seq], tokens, sems.at[0])]
    for j in range(3):
        moves.append(pltpu.make_async_copy(self_qkv.at[j], qkv_w.at[j], sems.at[1 + j]))
    moves.append(pltpu.make_async_copy(self_out, out_w, sems.at[4]))
    for j in range(count):
        moves.append(pltpu.make_async_copy(sources[j], kept[j], sems.at[5 + j]))
    for move in moves:
        move.start()
    share = ordered.shape[3]
    size = ordered.shape[0]
    for k, piece in enumerate(pieces):
        rows = piece[piece.shape[0] - 16 :, :]
        for i, offset in enumerate(offsets):
            for j in range(4):
                at = (4 * i + j) * share
                ordered[device ^ offset ^ k, j // 2, 16 * (j % 2) : 16 * (j % 2) + 16, :] = rows[
                    :, at : at + share
                ]
    for j in range(size):
        for c in range(2):
            prefix[c, :, j * share : (j + 1) * share] = ordered[j, c]
    moves[0].wait()
    rows = tokens[...]
    target, width = rows.shape
    for j in range(3):
        moves[1 + j].wait()
        qkv[j] = dot_nn(rows, qkv_w[j]).astype(LOW)
    allowed = self_allowed(lengths[0, seq], target, prefix.shape[1], prefix_len)
    logs = []
    for part in lane_pairs(width):
        keys = jnp.concatenate([prefix[0, :, part], qkv[1, :, part]], axis=0)
        values = jnp.concatenate([prefix[1, :, part], qkv[2, :, part]], axis=0)
        context, log = attend(stack_heads(scaled(qkv[0, :, part])), keys, values, allowed)
        context_all[:, part] = merge_heads(context).astype(LOW)
        logs += [log[:target], log[target:]]
    log_total[...] = put_lanes(logs, log_total.shape)
    moves[4].wait()
    summed[...] = rows.astype(FULL) + dot_nn(context_all[...], out_w[...])
    for move in moves[5:]:
        move.wait()


def cross_forward_kernel(
    members, places, lengths, summed_one, gains, biases, qkv_w, out_w, *refs
):
    blocks = refs[:-5]
    queries, keys_values, log_total, summed_two, mem_rows = refs[-5:]
    device, seq, unused = place(members)
    source = mem_rows.shape[0] // len(places)
    target, width = queries.shape
    for k, (index, start) in enumerate(places):
        at = pl.multiple_of((device ^ k) * source, source)
        mem_rows[pl.ds(at, source), :] = blocks[index][start : start + source, :]
    hidden = normalize(summed_one[...], gains[0:1], biases[0:1])[0]
    queries[...] = dot_nn(hidden.astype(LOW), qkv_w[0]).astype(LOW)
    for j in range(2):
        keys_values[j] = dot_nn(mem_rows[...], qkv_w[1 + j]).astype(LOW)
    allowed = (
        lax.broadcasted_iota(jnp.int32, (2 * target, mem_rows.shape[0]), 1) < lengths[0, seq]
    )
    contexts, logs = [], []
    for part in lane_pairs(width):
        context, log = attend(
            stack_heads(scaled(queries[:, part])),
            keys_values[0, :, part],
            keys_values[1, :, part],
            allowed,
        )
        contexts.append(merge_heads(context).astype(LOW))
        logs += [log[:target], log[target:]]
    log_total[...] = put_lanes(logs, log_total.shape)
    summed_two[...] = hidden + dot_nn(jnp.concatenate(contexts, axis=1), out_w[...])


def ffn_forward_kernel(summed_two, gains, biases, in_w, out_w, normed, slope, partial):
    hidden = normalize(summed_two[...], gains[1:2], biases[1:2])[0]
    low = hidden.astype(LOW)
    normed[...] = low
    inner = in_w.shape[1]
    parts = [slice(at, at + FFN_BLOCK) for at in range(0, inner, FFN_BLOCK)]
    pre = dot_nn(low, in_w[:, parts[0]])
    total = hidden
    for j, part in enumerate(parts):
        following = dot_nn(low, in_w[:, parts[j + 1]]) if j + 1 < len(parts) else None
        act, slope_full = gelu_both(pre)
        slope[:, part] = slope_full.astype(LOW)
        total = total + dot_nn(act.astype(LOW), out_w[part, :])
        pre = following
    partial[...] = total


def adapter_kernel(
    members, places, lengths, partial, normed, gains, biases, cotangent_all, *refs
):
    count = 1 + max(index for index, unused in places)
    shares, refs = refs[:count], refs[count:]
    output, grad_ffn, grad_hidden = refs[:3]
    grad_pieces, refs = refs[3 : 3 + members], refs[3 + members :]
    down, up, grad_down, grad_up, cotangent, sem = refs
    device, seq, replica = place(members)
    move = pltpu.make_async_copy(cotangent_all.at[0, seq], cotangent, sem)
    move.start()
    rows = down.shape[0] // len(places)
    half = rows // 2
    wide = down.shape[1]
    for k, (index, start) in enumerate(places):
        owner, share = device ^ k, shares[index]
        at = pl.multiple_of(owner * rows, rows)
        down[pl.ds(at, half), :] = share[start : start + half, :wide]
        down[pl.ds(at + half, half), :] = share[start : start + half, wide:]
        at = pl.multiple_of(owner * half, half)
        up[pl.ds(at, half), :] = share[start + half : start + rows, :]
    act, slope = gelu_both(dot_nn(normed[...], down[...]))
    act = act.astype(LOW)
    total = partial[...] + ADAPTER_SCALE * dot_nn(act, up[...])
    rows_out, normal, inverse = normalize(total, gains[2:3], biases[2:3])
    output[...] = rows_out.astype(LOW)
    live = lax.broadcasted_iota(jnp.int32, (total.shape[0], 1), 0) < lengths[0, seq]
    move.wait()
    grad_three = normalize_back(
        jnp.where(live, cotangent[...].astype(FULL), 0.0), normal, inverse, gains[2:3]
    )
    grad_ffn[...] = grad_three.astype(LOW)
    grad_adapted = (ADAPTER_SCALE * grad_three).astype(LOW)
    grad_pre = (dot_nt(grad_adapted, up[...]) * slope).astype(LOW)
    grad_hidden[...] = grad_three + dot_nt(grad_pre, down[...])
    grad_down[...] = dot_tn(normed[...], grad_pre).astype(LOW)
    grad_up[...] = dot_tn(act, grad_adapted).astype(LOW)
    for k, piece in enumerate(grad_pieces):
        owner = replica * members + (seq ^ k)
        at = pl.multiple_of(owner * rows, rows)
        piece[:half, :wide] = grad_down[pl.ds(at, half), :]
        piece[:half, wide:] = grad_down[pl.ds(at + half, half), :]
        piece[half:, :] = grad_up[pl.ds(pl.multiple_of(owner * half, half), half), :]


def ffn_backward_kernel(
    grad_ffn, grad_hidden, summed_two, gains, biases, in_w, out_w, slope, grad_two
):
    low = grad_ffn[...]
    inner = in_w.shape[1]
    parts = [slice(at, at + FFN_BLOCK) for at in range(0, inner, FFN_BLOCK)]
    grad_act = dot_nt(low, out_w[parts[0], :])
    total = grad_hidden[...]
    for j, part in enumerate(parts):
        following = dot_nt(low, out_w[parts[j + 1], :]) if j + 1 < len(parts) else None
        grad_pre = (grad_act * slope[:, part].astype(FULL)).astype(LOW)
        total = total + dot_nt(grad_pre, in_w[:, part])
        grad_act = following
    unused, normal, inverse = normalize(summed_two[...], gains[1:2], biases[1:2])
    grad_two[...] = normalize_back(total, normal, inverse, gains[1:2])


def cross_backward_kernel(
    members,
    lengths,
    grad_two,
    summed_one,
    gains,
    biases,
    qkv_w,
    out_w,
    queries,
    keys_values,
    log_total,
    later_source,
    grad_one,
    later,
    *refs,
):
    grad_pieces = refs[:members]
    grad_keys, grad_values, grad_rows, sem = refs[members:]
    unused, seq, replica = place(members)
    target, width = queries.shape
    fetch = pltpu.make_async_copy(later_source, later, sem)
    fetch.start()
    grad_context = dot_nt(grad_two[...].astype(LOW), out_w[...]).astype(LOW)
    allowed = (
        lax.broadcasted_iota(jnp.int32, (2 * target, keys_values.shape[1]), 1) < lengths[0, seq]
    )
    grad_queries = []
    for j, part in enumerate(lane_pairs(width)):
        into_queries, into_keys, into_values = attend_back(
            stack_heads(scaled(queries[:, part])),
            keys_values[0, :, part],
            keys_values[1, :, part],
            allowed,
            pair_logs(log_total, j),
            stack_heads(grad_context[:, part]),
        )
        grad_queries.append(into_queries)
        grad_keys[:, part] = into_keys.astype(LOW)
        grad_values[:, part] = into_values.astype(LOW)
    rows = grad_rows.shape[0]
    mine = pl.ds(pl.multiple_of(replica * rows, rows), rows)
    grad_rows[...] = (
        dot_nt(grad_keys[mine, :], qkv_w[1]) + dot_nt(grad_values[mine, :], qkv_w[2])
    ).astype(LOW)
    source = rows // members
    for k, piece in enumerate(grad_pieces):
        piece[...] = grad_rows[pl.ds(pl.multiple_of((seq ^ k) * source, source), source), :]
    total = grad_two[...] + dot_nt(jnp.concatenate(grad_queries, axis=1), qkv_w[0])
    unused, normal, inverse = normalize(summed_one[...], gains[0:1], biases[0:1])
    grad_one[...] = normalize_back(total, normal, inverse, gains[0:1])
    fetch.wait()


def prefix_backward_kernel(
    members,
    prefix_len,
    grad_one,
    prefix,
    out_w,
    qkv,
    context,
    log_total,
    grad_context,
    delta_all,
    *refs,
):
    grad_pieces, (blocks,) = refs[:members], refs[members:]
    unused, seq, replica = place(members)
    target, width = grad_one.shape
    pad = prefix.shape[1]
    grad_context[...] = dot_nt(grad_one[...].astype(LOW), out_w[...]).astype(LOW)
    allowed = lax.broadcasted_iota(jnp.int32, (2 * target, pad), 1) < prefix_len
    size, unused, unused, share = blocks.shape
    grads, deltas = ([], []), []
    for j, part in enumerate(lane_pairs(width)):
        stacked = stack_heads(scaled(qkv[0, :, part]))
        grad_stacked = stack_heads(grad_context[:, part])
        both = context[:, part].astype(FULL)
        delta = jnp.sum(
            grad_stacked.astype(FULL) * jnp.concatenate([both, both], axis=0), -1, keepdims=True
        )
        deltas += [delta[:target], delta[target:]]
        scores = jnp.where(allowed, dot_nt(stacked, prefix[0, :, part]), NEGATIVE)
        probs = jnp.exp(scores - pair_logs(log_total, j))
        grad_probs = dot_nt(grad_stacked, prefix[1, :, part])
        grad_scores = (probs * (grad_probs - delta)).astype(LOW)
        grads[0].append(dot_tn(grad_scores, stacked).astype(LOW))
        grads[1].append(dot_tn(probs.astype(LOW), grad_stacked).astype(LOW))
    delta_all[...] = put_lanes(deltas, delta_all.shape)
    for c in range(2):
        row = jnp.concatenate(grads[c], axis=1)
        for j in range(size):
            blocks[j, c] = row[:, j * share : (j + 1) * share]
    for k, piece in enumerate(grad_pieces):
        owner = replica * members + (seq ^ k)
        piece[...] = jnp.zeros_like(piece)
        for j in range(4):
            piece[:, j * share : (j + 1) * share] = blocks[
                owner, j // 2, 16 * (j % 2) : 16 * (j % 2) + 16, :
            ]


def self_backward_kernel(
    members,
    prefix_len,
    lengths,
    grad_context,
    delta_all,
    prefix,
    qkv,
    log_total,
    later_source,
    grad_qkv,
    later,
    sem,
):
    unused, seq, unused = place(members)
    fetch = pltpu.make_async_copy(later_source, later, sem)
    fetch.start()
    target, width = grad_context.shape
    pad = prefix.shape[1]
    allowed = self_allowed(lengths[0, seq], target, pad, prefix_len)
    for j, part in enumerate(lane_pairs(width)):
        into_queries, into_keys, into_values = attend_back(
            stack_heads(scaled(qkv[0, :, part])),
            jnp.concatenate([prefix[0, :, part], qkv[1, :, part]], axis=0),
            jnp.concatenate([prefix[1, :, part], qkv[2, :, part]], axis=0),
            allowed,
            pair_logs(log_total, j),
            stack_heads(grad_context[:, part]),
            pair_logs(delta_all, j),
            pad,
        )
        grad_qkv[0, :, part] = into_queries
        grad_qkv[1, :, part] = into_keys.astype(LOW)
        grad_qkv[2, :, part] = into_values.astype(LOW)
    fetch.wait()


def self_project_kernel(grad_one, qkv_w, grad_qkv, low, high):
    total = grad_one[...]
    for j in range(3):
        total = total + dot_nt(grad_qkv[j], qkv_w[j])
    half = low.shape[0]
    low[...] = total[:half].astype(LOW)
    high[...] = total[half:].astype(LOW)


def gather_kernel(members, windows, first, *refs):
    pieces, (result, held, sems) = refs[:-3], refs[-3:]
    unused, seq, unused = place(members)
    moves = []
    for k, parts in enumerate(windows):
        at = 0
        for index, start, stop in parts:
            rows = pieces[index][start:stop, :]
            held[k, at : at + stop - start, :] = rows.astype(held.dtype)
            at += stop - start
        move = pltpu.make_async_copy(held.at[k], result.at[seq ^ (first + k)], sems.at[k])
        move.start()
        moves.append(move)
    for move in moves:
        move.wait()


def adam_update(gradient, first_moment, second_moment, weight, step_rate):
    first_new = 0.9 * first_moment + 0.1 * gradient
    second_new = 0.999 * second_moment + 0.001 * gradient * gradient
    corrected_one = first_new / (1.0 - 0.9**STEP)
    corrected_two = second_new / (1.0 - 0.999**STEP)
    weight_new = weight - step_rate * (
        corrected_one / (jnp.sqrt(corrected_two) + 1e-08) + 0.01 * weight
    )
    return (first_new, second_new, weight_new)


def outer_update(outer_weight, momentum, average):
    momentum_new = OUTER_MOMENTUM * momentum + average
    return momentum_new, outer_weight - OUTER_RATE * (average + OUTER_MOMENTUM * momentum_new)


def prefix_rows_of(packed, share, count):
    parts = [packed[:, j * share : (j + 1) * share] for j in range(4)]
    return [jnp.concatenate(parts[2 * c : 2 * c + 2], axis=0)[:count] for c in range(2)]


def update_kernel(members, starts, *refs):
    pieces, prefix_pieces, refs = (
        refs[:members],
        refs[members : 2 * members],
        refs[2 * members :],
    )
    down_w, down_m, down_v, up_w, up_m, up_v, down_outer, up_outer = refs[:8]
    prefix_w, prefix_m, prefix_v, prefix_outer = refs[8:12]
    grad_down, grad_up, new_down, new_up = refs[12], refs[13], refs[14:17], refs[17:20]
    grad_prefix, new_prefix, difference, padded = refs[20], refs[21:24], refs[24], refs[25]
    total = sum(piece[...].astype(FULL) for piece in pieces)
    rows_all = total.shape[0]
    half = rows_all // 2
    wide = down_w.shape[2]
    for j in range(2):
        rows, part = slice(j * half, (j + 1) * half), slice(j * wide, (j + 1) * wide)
        gradient = total[:half, part]
        grad_down[0, rows, :] = gradient
        new = adam_update(gradient, down_m[0, rows], down_v[0, rows], down_w[0, rows], 0.06)
        for ref, value in zip(new_down, new):
            ref[0, rows, :] = value
        difference[:half, part] = (down_outer[rows, :] - new[2]).astype(LOW)
    gradient = total[half:]
    grad_up[0] = gradient
    new = adam_update(gradient, up_m[0], up_v[0], up_w[0], 0.02)
    for ref, value in zip(new_up, new):
        ref[0] = value
    difference[half:rows_all, :] = (up_outer[...] - new[2]).astype(LOW)
    total = sum(
        piece[start : start + 16, :].astype(FULL) for piece, start in zip(prefix_pieces, starts)
    )
    count, unused, share = prefix_w.shape
    padded[...] = jnp.zeros_like(padded)
    for c, gradient in enumerate(prefix_rows_of(total, share, count)):
        grad_prefix[:, c, :] = gradient
        new = adam_update(gradient, prefix_m[:, c, :], prefix_v[:, c, :], prefix_w[:, c, :], 2.0)
        for ref, value in zip(new_prefix, new):
            ref[:, c, :] = value
        padded[c, :count, :] = prefix_outer[:, c, :] - new[2]
    difference[rows_all:, :] = jnp.zeros_like(difference[rows_all:, :])
    for j in range(4):
        difference[rows_all:, j * share : (j + 1) * share] = padded[
            j // 2, 16 * (j % 2) : 16 * (j % 2) + 16, :
        ].astype(LOW)


def add_kernel(left, right, result):
    result[...] = (left[...].astype(FULL) + right[...].astype(FULL)).astype(LOW)


def outer_kernel(groups, left, right, *refs):
    down_outer, up_outer, prefix_outer, down_mom, up_mom, prefix_mom = refs[:6]
    new_down, new_up, new_prefix = refs[6:8], refs[8:10], refs[10:12]
    average = (left[...].astype(FULL) + right[...].astype(FULL)) / groups
    rows_all = average.shape[0] - 16
    half = rows_all // 2
    wide = down_outer.shape[1]
    for j in range(2):
        rows, part = slice(j * half, (j + 1) * half), slice(j * wide, (j + 1) * wide)
        new = outer_update(down_outer[rows, :], down_mom[rows, :], average[:half, part])
        for ref, value in zip(new_down, new):
            ref[rows, :] = value
    new = outer_update(up_outer[...], up_mom[...], average[half:rows_all])
    for ref, value in zip(new_up, new):
        ref[...] = value
    count, unused, share = prefix_outer.shape
    for c, part in enumerate(prefix_rows_of(average[rows_all:], share, count)):
        new = outer_update(prefix_outer[:, c, :], prefix_mom[:, c, :], part)
        for ref, value in zip(new_prefix, new):
            ref[:, c, :] = value


def shaped(shape, dtype):
    return jax.ShapeDtypeStruct(shape, dtype)


def call_whole(
    kernel, spaces, outs, scratch, args, limit=VMEM_LIMIT, out_spaces=None, after=(), micros=0, aliases={}
):
    spaces = list(spaces) + [pltpu.VMEM] * (len(args) - len(spaces)) + [pl.ANY] * len(after)
    if after:
        inner_kernel, count = kernel, len(args)

        def kernel(*refs):
            inner_kernel(*refs[:count], *refs[count + len(after) :])

        args = tuple(args) + tuple(after)
    out_spaces = out_spaces or [pltpu.VMEM] * len(outs)
    return pl.pallas_call(
        kernel,
        in_specs=[pl.BlockSpec(memory_space=space) for space in spaces],
        out_specs=[pl.BlockSpec(memory_space=space) for space in out_spaces],
        out_shape=outs,
        scratch_shapes=scratch,
        input_output_aliases=aliases,
        compiler_params=pltpu.CompilerParams(vmem_limit_bytes=limit),
        cost_estimate=pl.CostEstimate(flops=1000 + int(micros * 1150000000), bytes_accessed=1000, transcendentals=0),
    )(*args)


def local(
    dec_input,
    memory,
    out_grad,
    tgt_lengths,
    src_lengths,
    self_qkv,
    self_out,
    cross_qkv,
    cross_out,
    ffn_in,
    ffn_out,
    norm_gains,
    norm_biases,
    down_w,
    up_w,
    prefix_w,
    down_m,
    down_v,
    up_m,
    up_v,
    prefix_m,
    prefix_v,
    down_outer,
    up_outer,
    prefix_outer,
    down_mom,
    up_mom,
    prefix_mom,
):
    seq_count, target, model_width = dec_input.shape[1:]
    source = memory.shape[2]
    prefix_len = prefix_w.shape[2]
    mem_size = lax.axis_size("mem")
    grp_size = lax.axis_size("grp")
    replicas = mem_size // seq_count
    device = lax.axis_index("mem")
    seq = device % seq_count
    replica = device // seq_count
    adapt = down_w.shape[2]
    inner = ffn_in.shape[1]
    share_rows = down_w.shape[1]
    half_rows = share_rows // 2
    positions = mem_size * source
    resident = positions <= RESIDENT_POSITIONS
    half = target // 2
    bound = functools.partial

    def swap(values_in, bits):
        return lax.ppermute(values_in, "mem", [(j, j ^ bits) for j in range(mem_size)])

    def join(*parts):
        rows = sum(stop - start for unused, start, stop in parts)
        (result,) = functools.partial(call_whole, micros=0.4)(
            bound(join_kernel, [(start, stop) for unused, start, stop in parts]),
            [],
            [shaped((rows, model_width), LOW)],
            [],
            tuple(piece for piece, unused, unused in parts),
            SMALL_LIMIT,
        )
        return result

    def in_order(windows, pieces, dtype, after=(), micros=2, first=0, into=None):
        rows = sum(stop - start for unused, start, stop in windows[0])
        shape = (seq_count, rows, model_width)
        pieces = tuple(pieces)
        if into is not None:
            after = (into, *after)
        (result,) = call_whole(
            bound(gather_kernel, seq_count, windows, first),
            [],
            [shaped(shape, dtype)],
            [
                pltpu.VMEM((len(windows), *shape[1:]), dtype),
                pltpu.SemaphoreType.DMA((len(windows),)),
            ],
            pieces,
            SMALL_LIMIT,
            out_spaces=[pl.ANY],
            after=after,
            micros=micros,
            aliases={} if into is None else {len(pieces): 0},
        )
        return result

    members = range(seq_count)
    partners = members[1:]
    replica_bits = [seq_count * 2**j for j in range(replicas.bit_length() - 1)]
    bit = replica_bits[0]
    prefix_rows = 32
    prefix_share = prefix_w.shape[3]
    blocks = jnp.pad(
        prefix_w[0].astype(LOW), ((0, 0), (0, prefix_rows - prefix_len), (0, 0))
    ).reshape(4, 16, prefix_share)
    offsets, prefixes = [0], jnp.concatenate([blocks[j] for j in range(4)], axis=1)
    for step in replica_bits:
        prefixes = jnp.concatenate([prefixes, swap(prefixes, step)], axis=1)
        offsets = offsets + [offset ^ step for offset in offsets]
    outward, *mem_send = functools.partial(call_whole, micros=2)(
        bound(first_kernel, seq_count),
        [pltpu.HBM] * 3,
        [shaped((source + share_rows, model_width), LOW)]
        + [shaped((source, model_width), LOW)] * (seq_count - 1),
        [
            pltpu.VMEM((source, model_width), LOW),
            pltpu.VMEM(down_w.shape[1:], FULL),
            pltpu.VMEM(up_w.shape[1:], FULL),
            pltpu.SemaphoreType.DMA((seq_count + 2,)),
        ],
        tuple(
            pltpu.with_memory_space_constraint(values_in, pltpu.HBM)
            for values_in in (memory, down_w, up_w)
        ),
        SMALL_LIMIT,
    )
    outward_arrived = swap(outward, bit)
    mem_send, prefixes = lax.optimization_barrier((mem_send, prefixes))
    arrived = [swap(mem_send[j - 1], j) for j in partners]
    prefix_pieces = [prefixes] + [swap(prefixes, j) for j in partners]
    plane_blocks = join(*[(piece, 0, source) for piece in arrived])
    stop = source + share_rows
    own, plane_blocks = lax.optimization_barrier((outward, plane_blocks))
    shares = {0: join((own, source, stop)), bit: join((outward_arrived, source, stop))}
    for step in replica_bits[1:]:
        for k, piece in list(shares.items()):
            shares[k ^ step] = swap(piece, step)
    plane_arrived = swap(plane_blocks, bit)
    beside = [swap(share, 2) for share in shares.values()]
    across = [swap(share, 1) for share in shares.values()]
    block_refs = [outward, *arrived, outward_arrived, plane_arrived]
    block_places = {0: (0, 0), bit: (seq_count, 0)}
    for j in partners:
        block_places[j] = (j, 0)
        block_places[j ^ bit] = (seq_count + 1, (j - 1) * source)

    rows_full = shaped((target, model_width), FULL)
    rows_low = shaped((target, model_width), LOW)
    logs = shaped((target, LANES), FULL)
    lengths_space = [pltpu.SMEM]
    dma = pltpu.SemaphoreType.DMA

    weights = (cross_qkv, cross_out, ffn_in, ffn_out) if resident else ()
    prefix, qkv, self_log, summed_one, context, *kept = functools.partial(call_whole, micros=11)(
        bound(self_forward_kernel, seq_count, prefix_len, offsets),
        [pltpu.SMEM, pltpu.HBM] + [pltpu.VMEM] * seq_count + [pltpu.HBM] * (len(weights) + 2),
        [
            shaped((2, prefix_rows, model_width), LOW),
            shaped((3, target, model_width), LOW),
            logs,
            rows_full,
            rows_low,
        ]
        + [pltpu.VMEM(weight.shape, LOW) for weight in weights],
        [
            pltpu.VMEM((target, model_width), LOW),
            pltpu.VMEM((mem_size, 2, prefix_rows, prefix_w.shape[3]), LOW),
            pltpu.VMEM(self_qkv.shape, LOW),
            pltpu.VMEM(self_out.shape, LOW),
            dma((len(weights) + 5,)),
        ],
        (tgt_lengths, dec_input, *prefix_pieces, self_qkv, self_out, *weights),
        after=(plane_blocks, *[shares[k] for k in shares if k]),
        limit=VMEM_LIMIT + 8 * 1024 * 1024,
    )
    if resident:
        cross_qkv, cross_out, ffn_in, ffn_out = kept
    summed_one, *beside = lax.optimization_barrier((summed_one, *beside))
    joined = join(*[(share, 0, share_rows) for share in beside])
    far = swap(joined, 1)
    share_refs = [*shares.values(), *beside, *across, far]
    share_places = [None] * mem_size
    for i, offset in enumerate(shares):
        share_places[offset] = (i, 0)
        share_places[offset ^ 2] = (i + replicas, 0)
        share_places[offset ^ 1] = (i + 2 * replicas, 0)
        share_places[offset ^ 3] = (3 * replicas, i * share_rows)
    summed_one, block_refs[-1] = lax.optimization_barrier((summed_one, block_refs[-1]))
    for step in replica_bits[1:]:
        known = sorted(block_places)
        joined = jnp.concatenate(
            [
                block_refs[index][start : start + source]
                for index, start in (block_places[k] for k in known)
            ],
            axis=0,
        )
        for i, k in enumerate(known):
            block_places[k ^ step] = (len(block_refs), i * source)
        block_refs.append(swap(joined, step))
    places = [block_places[k] for k in range(mem_size)]
    cross_limit = VMEM_LIMIT if resident else 4 * VMEM_LIMIT
    cross_queries, keys_values, cross_log, summed_two = functools.partial(call_whole, micros=8)(
        bound(cross_forward_kernel, seq_count, places),
        lengths_space,
        [rows_low, shaped((2, positions, model_width), LOW), logs, rows_full],
        [pltpu.VMEM((positions, model_width), LOW)],
        (src_lengths, summed_one, norm_gains, norm_biases, cross_qkv, cross_out, *block_refs),
        cross_limit,
        after=(joined,),
    )
    normed, slope, partial = functools.partial(call_whole, micros=1)(
        ffn_forward_kernel,
        [],
        [rows_low, shaped((target, inner), LOW), rows_full],
        [],
        (summed_two, norm_gains, norm_biases, ffn_in, ffn_out),
    )
    output_rows, grad_ffn, grad_hidden, *grad_pieces = functools.partial(call_whole, micros=4)(
        bound(adapter_kernel, seq_count, share_places),
        [pltpu.SMEM] + [pltpu.VMEM] * 4 + [pltpu.HBM],
        [rows_low, rows_low, rows_full] + [shaped((share_rows, model_width), LOW)] * seq_count,
        [
            pltpu.VMEM((model_width, adapt), LOW),
            pltpu.VMEM((adapt, model_width), LOW),
            pltpu.VMEM((model_width, adapt), LOW),
            pltpu.VMEM((adapt, model_width), LOW),
            pltpu.VMEM((target, model_width), LOW),
            dma,
        ],
        (tgt_lengths, partial, normed, norm_gains, norm_biases, out_grad, *share_refs),
    )
    output_one, output_two = swap(output_rows, 1), swap(output_rows, 2)
    grad_pieces = [grad_pieces[0]] + [swap(grad_pieces[j], j) for j in partners]
    (grad_two,) = functools.partial(call_whole, micros=5)(
        ffn_backward_kernel,
        [],
        [rows_full],
        [],
        (grad_ffn, grad_hidden, summed_two, norm_gains, norm_biases, ffn_in, ffn_out, slope),
    )
    plane_rows = seq_count * source
    grad_one, out_later, *grad_mem_pieces = functools.partial(call_whole, micros=11)(
        bound(cross_backward_kernel, seq_count),
        lengths_space + [pltpu.VMEM] * 9 + [pltpu.HBM],
        [rows_full, pltpu.VMEM(self_out.shape, LOW)]
        + [shaped((source, model_width), LOW)] * seq_count,
        [
            pltpu.VMEM((positions, model_width), LOW),
            pltpu.VMEM((positions, model_width), LOW),
            pltpu.VMEM((plane_rows, model_width), LOW),
            dma,
        ],
        (
            src_lengths,
            grad_two,
            summed_one,
            norm_gains,
            norm_biases,
            cross_qkv,
            cross_out,
            cross_queries,
            keys_values,
            cross_log,
            self_out,
        ),
        cross_limit,
    )
    grad_context, delta_all, *prefix_sent = functools.partial(call_whole, micros=3)(
        bound(prefix_backward_kernel, seq_count, prefix_len),
        [],
        [rows_low, logs] + [shaped((16, model_width), LOW)] * seq_count,
        [pltpu.VMEM((mem_size, 2, prefix_rows, prefix_share), LOW)],
        (grad_one, prefix, out_later, qkv, context, self_log),
    )
    grad_context, output_one, output_two = lax.optimization_barrier(
        (grad_context, output_one, output_two)
    )

    def wave(*parts):
        return join(*[part if isinstance(part, tuple) else (part, 0, part.shape[0]) for part in parts])

    second = [
        None,
        swap(wave((output_two, 0, half), grad_mem_pieces[1], prefix_sent[1]), 1),
        swap(wave((output_one, half, target), grad_mem_pieces[2], prefix_sent[2]), 2),
        swap(wave(grad_mem_pieces[3], prefix_sent[3]), 3),
    ]
    grad_qkv, qkv_later = functools.partial(call_whole, micros=8)(
        bound(self_backward_kernel, seq_count, prefix_len),
        lengths_space + [pltpu.VMEM] * 5 + [pltpu.HBM],
        [shaped((3, target, model_width), LOW), pltpu.VMEM(self_qkv.shape, LOW)],
        [dma],
        (tgt_lengths, grad_context, delta_all, prefix, qkv, self_log, self_qkv),
        after=tuple(grad_pieces[1:]),
    )
    low, high = functools.partial(call_whole, micros=2)(
        self_project_kernel,
        [],
        [shaped((half, model_width), LOW)] * 2,
        [],
        (grad_one, qkv_later, grad_qkv),
        after=tuple(second[1:]),
    )
    low, high, grad_pieces = lax.optimization_barrier((low, high, grad_pieces))
    low_two, high_one = swap(low, 2), swap(high, 1)
    low_one, high_two = swap(low, 1), swap(high, 2)
    low_three, high_three = swap(low_two, 1), swap(high_one, 2)

    def group_swap(values_in, bits):
        return lax.ppermute(values_in, "grp", [(j, j ^ bits) for j in range(grp_size)])

    def flip(values_in):
        return jnp.swapaxes(values_in, -3, -2)

    group_bits = [2**j for j in range(grp_size.bit_length() - 1)]
    down_shape, up_shape = shaped(down_w.shape, FULL), shaped(up_w.shape, FULL)
    flipped = shaped((prefix_len, 2, prefix_share), FULL)
    packed_rows = half + source
    results = functools.partial(call_whole, micros=1)(
        bound(update_kernel, seq_count, (0, packed_rows, packed_rows, source)),
        [],
        [down_shape, up_shape]
        + [down_shape] * 3
        + [up_shape] * 3
        + [flipped] * 4
        + [shaped((share_rows + 16, model_width), LOW)],
        [pltpu.VMEM((2, prefix_rows, prefix_share), FULL)],
        (
            *grad_pieces,
            prefix_sent[0],
            *second[1:],
            down_w,
            down_m,
            down_v,
            up_w,
            up_m,
            up_v,
            down_outer,
            up_outer,
            flip(prefix_w[0]),
            flip(prefix_m[0]),
            flip(prefix_v[0]),
            flip(prefix_outer),
        ),
        SMALL_LIMIT,
    )
    (grad_down, grad_up), updated, difference = results[:2], results[2:8], results[12]
    grad_prefix, *prefix_new = [flip(values_in)[None] for values_in in results[8:12]]
    for bits in group_bits[:-1]:
        (difference,) = functools.partial(call_whole, micros=0.4)(
            add_kernel,
            [],
            [shaped(difference.shape, LOW)],
            [],
            (difference, group_swap(difference, bits)),
            SMALL_LIMIT,
        )
    new_down_mom, new_down_outer, new_up_mom, new_up_outer, *prefix_results = functools.partial(
        call_whole, micros=1
    )(
        bound(outer_kernel, grp_size),
        [],
        [shaped(down_outer.shape, FULL)] * 2
        + [shaped(up_outer.shape, FULL)] * 2
        + [flipped] * 2,
        [],
        (
            difference,
            group_swap(difference, group_bits[-1]),
            down_outer,
            up_outer,
            flip(prefix_outer),
            down_mom,
            up_mom,
            flip(prefix_mom),
        ),
        SMALL_LIMIT,
    )
    prefix_results = [flip(values_in) for values_in in prefix_results]
    output = in_order(
        (
            ((0, 0, target),),
            ((1, 0, target),),
            ((2, 0, target),),
            ((3, 0, half), (4, 0, half)),
        ),
        (output_rows, output_one, output_two, second[1], second[2]),
        LOW,
    )
    grad_memory = in_order(
        (
            ((0, 0, source),),
            ((1, half, half + source),),
            ((2, half, half + source),),
            ((3, 0, source),),
        ),
        (grad_mem_pieces[0], *second[1:]),
        FULL,
    )
    grad_input = in_order(
        tuple(((2 * k, 0, half), (2 * k + 1, 0, half)) for k in members[:3]),
        (low, high, low_one, high_one, low_two, high_two),
        FULL,
        micros=100,
    )
    grad_input = in_order(
        (((0, 0, half), (1, 0, half)),),
        (low_three, high_three),
        FULL,
        (output, grad_memory, new_down_mom, grad_prefix, *prefix_new, *prefix_results),
        first=3,
        into=grad_input,
    )
    return (
        output[None],
        grad_input[None],
        grad_memory[None],
        grad_down,
        grad_up,
        grad_prefix,
        *updated,
        *prefix_new,
        new_down_mom,
        new_down_outer,
        new_up_mom,
        new_up_outer,
        *prefix_results,
    )


def solution(mesh):
    placed = (
        P("grp", None, None, None),
        P("grp", None, "mem", None),
        P("grp", None, None, None),
        P("grp", None),
        P("grp", None),
        P(),
        P(),
        P(),
        P(),
        P(),
        P(),
        P(),
        P(),
        P("grp", "mem", None),
        P("grp", "mem", None),
        P("grp", None, None, "mem"),
        P("grp", "mem", None),
        P("grp", "mem", None),
        P("grp", "mem", None),
        P("grp", "mem", None),
        P("grp", None, None, "mem"),
        P("grp", None, None, "mem"),
        P("mem", None),
        P("mem", None),
        P(None, None, "mem"),
        P("mem", None),
        P("mem", None),
        P(None, None, "mem"),
    )
    return jax.shard_map(
        local,
        mesh=mesh,
        in_specs=placed,
        out_specs=(
            P("grp", None, None, None),
            P("grp", None, None, None),
            P("grp", None, "mem", None),
            P("grp", "mem", None),
            P("grp", "mem", None),
            P("grp", None, None, "mem"),
            P("grp", "mem", None),
            P("grp", "mem", None),
            P("grp", "mem", None),
            P("grp", "mem", None),
            P("grp", "mem", None),
            P("grp", "mem", None),
            P("grp", None, None, "mem"),
            P("grp", None, None, "mem"),
            P("grp", None, None, "mem"),
            P("mem", None),
            P("mem", None),
            P("mem", None),
            P("mem", None),
            P(None, None, "mem"),
            P(None, None, "mem"),
        ),
        check_vma=False,
    )
```

```python
import functools

import jax
import jax.numpy as jnp
from jax import lax
from jax.experimental import pallas as pl
from jax.experimental.pallas import tpu as pltpu
from jax.sharding import PartitionSpec as P

HDIM = 64
STEP = 10


EPSILON = 1e-05
NEGATIVE = -1e30
ADAPTER_SCALE = 4.0
OUTER_MOMENTUM = 0.9
OUTER_RATE = 0.7
LANES = 128
FFN_BLOCK = 1024
RESIDENT_POSITIONS = 1024
SMALL_LIMIT = 6 * 1024 * 1024
VMEM_LIMIT = 10 * 1024 * 1024
LOW = jnp.bfloat16
FULL = jnp.float32


def normalize(values_in, gain_row, bias_row):
    centered = values_in - jnp.mean(values_in, -1, keepdims=True)
    scale_inv = lax.rsqrt(jnp.mean(centered * centered, -1, keepdims=True) + EPSILON)
    normal = centered * scale_inv
    return (normal * gain_row + bias_row, normal, scale_inv)


def normalize_back(gradient, normal, scale_inv, gain_row):
    scaled = gradient * gain_row
    return scale_inv * (
        scaled
        - jnp.mean(scaled, -1, keepdims=True)
        - normal * jnp.mean(scaled * normal, -1, keepdims=True)
    )


def dot_nn(left, right):
    return lax.dot_general(left, right, (((1,), (0,)), ((), ())), preferred_element_type=FULL)


def dot_nt(left, right):
    return lax.dot_general(left, right, (((1,), (1,)), ((), ())), preferred_element_type=FULL)


def dot_tn(left, right):
    return lax.dot_general(left, right, (((0,), (0,)), ((), ())), preferred_element_type=FULL)


def gelu_both(pre_act):
    tail = jnp.exp(-0.5 * pre_act * pre_act)
    inv = pl.reciprocal(1.0 + (0.3275911 * 0.7071067811865476) * jnp.abs(pre_act))
    poly = inv * (
        0.127414796
        + inv * (-0.142248368 + inv * (0.7107068705 + inv * (-0.7265760135 + inv * 0.5307027145)))
    )
    lower = poly * tail
    cdf = jnp.where(pre_act < 0, lower, 1.0 - lower)
    return pre_act * cdf, cdf + pre_act * (tail * 0.3989422804014327)


def first_lanes(shape):
    return lax.broadcasted_iota(jnp.int32, shape, 1) < HDIM


def stack_heads(pair):
    first = first_lanes(pair.shape)
    none = jnp.zeros_like(pair)
    return jnp.concatenate([jnp.where(first, pair, none), jnp.where(first, none, pair)], axis=0)


def merge_heads(stacked):
    rows = stacked.shape[0] // 2
    return jnp.where(first_lanes((rows, LANES)), stacked[:rows], stacked[rows:])


def scaled(queries):
    return queries * jnp.asarray(HDIM ** (-0.5), LOW)


def attend(stacked, keys, values, allowed):
    scores = jnp.where(allowed, dot_nt(stacked, keys), NEGATIVE)
    top = jnp.max(scores, -1, keepdims=True)
    expo = jnp.exp(scores - top).astype(LOW)
    total = jnp.sum(expo.astype(FULL), -1, keepdims=True)
    return dot_nn(expo, values) / total, top + jnp.log(total)


def attend_back(
    stacked, keys, values, allowed, log_total, grad_stacked, delta=None, skipped=0
):
    scores = jnp.where(allowed, dot_nt(stacked, keys), NEGATIVE)
    probs = jnp.exp(scores - log_total)
    grad_probs = dot_nt(grad_stacked, values)
    if delta is None:
        delta = jnp.sum(probs * grad_probs, -1, keepdims=True)
    grad_scores = (probs * (grad_probs - delta)).astype(LOW)
    grad_queries = merge_heads(dot_nn(grad_scores, keys)) * (HDIM ** (-0.5))
    grad_keys = dot_tn(grad_scores, stacked)[skipped:]
    grad_values = dot_tn(probs.astype(LOW), grad_stacked)[skipped:]
    return grad_queries.astype(LOW), grad_keys, grad_values


def self_allowed(length, target, prefix_pad, prefix_len):
    shape = (2 * target, prefix_pad + target)
    row = lax.broadcasted_iota(jnp.int32, shape, 0)
    row = jnp.where(row >= target, row - target, row)
    column = lax.broadcasted_iota(jnp.int32, shape, 1)
    key = column - prefix_pad
    return (column < prefix_len) | (key >= 0) & (key <= row) & (key < length)


def put_lanes(columns, shape):
    lane = lax.broadcasted_iota(jnp.int32, shape, 1)
    result = jnp.zeros(shape, FULL)
    for j, column in enumerate(columns):
        result = jnp.where(lane == j, column, result)
    return result


def lane_pairs(width):
    return [slice(at, at + LANES) for at in range(0, width, LANES)]


def pair_logs(log_total, j):
    return jnp.concatenate(
        [log_total[:, 2 * j : 2 * j + 1], log_total[:, 2 * j + 1 : 2 * j + 2]], axis=0
    )


def place(members):
    device = lax.axis_index("mem")
    return device, lax.rem(device, members), lax.div(device, members)


def first_kernel(members, memory, down_w, up_w, outward, *refs):
    blocks, (block, down, up, sems) = refs[: members - 1], refs[members - 1 :]
    unused, seq, unused = place(members)
    moves = [
        pltpu.make_async_copy(memory.at[0, seq], block, sems.at[0]),
        pltpu.make_async_copy(down_w.at[0], down, sems.at[1]),
        pltpu.make_async_copy(up_w.at[0], up, sems.at[2]),
    ]
    for k, partner in enumerate(blocks):
        moves.append(pltpu.make_async_copy(memory.at[0, seq ^ (k + 1)], partner, sems.at[3 + k]))
    for move in moves:
        move.start()
    for move in moves:
        move.wait()
    source = block.shape[0]
    half = up.shape[0]
    wide = down.shape[1]
    outward[:source, :] = block[...]
    outward[source : source + half, :wide] = down[:half, :].astype(LOW)
    outward[source : source + half, wide:] = down[half:, :].astype(LOW)
    outward[source + half :, :] = up[...].astype(LOW)


def append_kernel(count, rows, *refs):
    for block, message in zip(refs[:count], refs[count:]):
        at = block.shape[0]
        message[:at, :] = block[...]
        message[at:, :] = rows[...]


def join_kernel(windows, *refs):
    at = 0
    for piece, (start, stop) in zip(refs, windows):
        refs[-1][at : at + stop - start, :] = piece[start:stop, :]
        at += stop - start


def self_forward_kernel(members, prefix_len, offsets, lengths, tokens_all, *refs):
    pieces, (self_qkv, self_out) = refs[:members], refs[members : members + 2]
    refs = refs[members + 2 :]
    count = (len(refs) - 10) // 2
    sources, refs = refs[:count], refs[count:]
    prefix, qkv, log_total, summed, context_all = refs[:5]
    kept = refs[5 : 5 + count]
    tokens, ordered, qkv_w, out_w, sems = refs[5 + count :]
    device, seq, unused = place(members)
    moves = [pltpu.make_async_copy(tokens_all.at[0, seq], tokens, sems.at[0])]
    for j in range(3):
        moves.append(pltpu.make_async_copy(self_qkv.at[j], qkv_w.at[j], sems.at[1 + j]))
    moves.append(pltpu.make_async_copy(self_out, out_w, sems.at[4]))
    for j in range(count):
        moves.append(pltpu.make_async_copy(sources[j], kept[j], sems.at[5 + j]))
    for move in moves:
        move.start()
    share = ordered.shape[3]
    size = ordered.shape[0]
    for k, piece in enumerate(pieces):
        rows = piece[piece.shape[0] - 16 :, :]
        for i, offset in enumerate(offsets):
            for j in range(4):
                at = (4 * i + j) * share
                ordered[device ^ offset ^ k, j // 2, 16 * (j % 2) : 16 * (j % 2) + 16, :] = rows[
                    :, at : at + share
                ]
    for j in range(size):
        for c in range(2):
            prefix[c, :, j * share : (j + 1) * share] = ordered[j, c]
    moves[0].wait()
    rows = tokens[...]
    target, width = rows.shape
    for j in range(3):
        moves[1 + j].wait()
        qkv[j] = dot_nn(rows, qkv_w[j]).astype(LOW)
    allowed = self_allowed(lengths[0, seq], target, prefix.shape[1], prefix_len)
    logs = []
    for part in lane_pairs(width):
        keys = jnp.concatenate([prefix[0, :, part], qkv[1, :, part]], axis=0)
        values = jnp.concatenate([prefix[1, :, part], qkv[2, :, part]], axis=0)
        context, log = attend(stack_heads(scaled(qkv[0, :, part])), keys, values, allowed)
        context_all[:, part] = merge_heads(context).astype(LOW)
        logs += [log[:target], log[target:]]
    log_total[...] = put_lanes(logs, log_total.shape)
    moves[4].wait()
    summed[...] = rows.astype(FULL) + dot_nn(context_all[...], out_w[...])
    for move in moves[5:]:
        move.wait()


def cross_forward_kernel(
    members, places, lengths, summed_one, gains, biases, qkv_w, out_w, *refs
):
    blocks = refs[:-5]
    queries, keys_values, log_total, summed_two, mem_rows = refs[-5:]
    device, seq, unused = place(members)
    source = mem_rows.shape[0] // len(places)
    target, width = queries.shape
    for k, (index, start) in enumerate(places):
        at = pl.multiple_of((device ^ k) * source, source)
        mem_rows[pl.ds(at, source), :] = blocks[index][start : start + source, :]
    hidden = normalize(summed_one[...], gains[0:1], biases[0:1])[0]
    queries[...] = dot_nn(hidden.astype(LOW), qkv_w[0]).astype(LOW)
    for j in range(2):
        keys_values[j] = dot_nn(mem_rows[...], qkv_w[1 + j]).astype(LOW)
    allowed = (
        lax.broadcasted_iota(jnp.int32, (2 * target, mem_rows.shape[0]), 1) < lengths[0, seq]
    )
    contexts, logs = [], []
    for part in lane_pairs(width):
        context, log = attend(
            stack_heads(scaled(queries[:, part])),
            keys_values[0, :, part],
            keys_values[1, :, part],
            allowed,
        )
        contexts.append(merge_heads(context).astype(LOW))
        logs += [log[:target], log[target:]]
    log_total[...] = put_lanes(logs, log_total.shape)
    summed_two[...] = hidden + dot_nn(jnp.concatenate(contexts, axis=1), out_w[...])


def ffn_forward_kernel(summed_two, gains, biases, in_w, out_w, normed, slope, partial):
    hidden = normalize(summed_two[...], gains[1:2], biases[1:2])[0]
    low = hidden.astype(LOW)
    normed[...] = low
    inner = in_w.shape[1]
    parts = [slice(at, at + FFN_BLOCK) for at in range(0, inner, FFN_BLOCK)]
    pre = dot_nn(low, in_w[:, parts[0]])
    total = hidden
    for j, part in enumerate(parts):
        following = dot_nn(low, in_w[:, parts[j + 1]]) if j + 1 < len(parts) else None
        act, slope_full = gelu_both(pre)
        slope[:, part] = slope_full.astype(LOW)
        total = total + dot_nn(act.astype(LOW), out_w[part, :])
        pre = following
    partial[...] = total


def adapter_kernel(
    places, lengths, partial, normed, gains, biases, cotangent_all, *refs
):
    count = 1 + max(index for index, unused in places)
    shares, refs = refs[:count], refs[count:]
    output, grad_ffn, grad_hidden, act_low, grad_pre_low, grad_low, down, up, cotangent, sem = refs
    device, seq, unused = place(lengths.shape[1])
    move = pltpu.make_async_copy(cotangent_all.at[0, seq], cotangent, sem)
    move.start()
    rows = down.shape[0] // len(places)
    half = rows // 2
    wide = down.shape[1]
    for k, (index, start) in enumerate(places):
        owner, share = device ^ k, shares[index]
        at = pl.multiple_of(owner * rows, rows)
        down[pl.ds(at, half), :] = share[start : start + half, :wide]
        down[pl.ds(at + half, half), :] = share[start : start + half, wide:]
        at = pl.multiple_of(owner * half, half)
        up[pl.ds(at, half), :] = share[start + half : start + rows, :]
    act, slope = gelu_both(dot_nn(normed[...], down[...]))
    act_low[...] = act.astype(LOW)
    total = partial[...] + ADAPTER_SCALE * dot_nn(act_low[...], up[...])
    rows_out, normal, inverse = normalize(total, gains[2:3], biases[2:3])
    output[...] = rows_out.astype(LOW)
    live = lax.broadcasted_iota(jnp.int32, (total.shape[0], 1), 0) < lengths[0, seq]
    move.wait()
    grad_three = normalize_back(
        jnp.where(live, cotangent[...].astype(FULL), 0.0), normal, inverse, gains[2:3]
    )
    grad_ffn[...] = grad_three.astype(LOW)
    grad_low[...] = (ADAPTER_SCALE * grad_three).astype(LOW)
    grad_pre = (dot_nt(grad_low[...], up[...]) * slope).astype(LOW)
    grad_pre_low[...] = grad_pre
    grad_hidden[...] = grad_three + dot_nt(grad_pre, down[...])


def adapter_gradient_kernel(members, normed, act, grad_pre, grad_adapted, *refs):
    grad_pieces, (grad_down, grad_up) = refs[:members], refs[members:]
    unused, seq, replica = place(members)
    grad_down[...] = dot_tn(normed[...], grad_pre[...]).astype(LOW)
    grad_up[...] = dot_tn(act[...], grad_adapted[...]).astype(LOW)
    rows = grad_pieces[0].shape[0]
    half = rows // 2
    wide = grad_down.shape[1]
    for k, piece in enumerate(grad_pieces):
        owner = replica * members + (seq ^ k)
        at = pl.multiple_of(owner * rows, rows)
        piece[:half, :wide] = grad_down[pl.ds(at, half), :]
        piece[:half, wide:] = grad_down[pl.ds(at + half, half), :]
        piece[half:, :] = grad_up[pl.ds(pl.multiple_of(owner * half, half), half), :]


def ffn_backward_kernel(
    grad_ffn, grad_hidden, summed_two, gains, biases, in_w, out_w, slope, grad_two
):
    low = grad_ffn[...]
    inner = in_w.shape[1]
    parts = [slice(at, at + FFN_BLOCK) for at in range(0, inner, FFN_BLOCK)]
    grad_act = dot_nt(low, out_w[parts[0], :])
    total = grad_hidden[...]
    for j, part in enumerate(parts):
        following = dot_nt(low, out_w[parts[j + 1], :]) if j + 1 < len(parts) else None
        grad_pre = (grad_act * slope[:, part].astype(FULL)).astype(LOW)
        total = total + dot_nt(grad_pre, in_w[:, part])
        grad_act = following
    unused, normal, inverse = normalize(summed_two[...], gains[1:2], biases[1:2])
    grad_two[...] = normalize_back(total, normal, inverse, gains[1:2])


def cross_backward_kernel(
    members,
    lengths,
    grad_two,
    summed_one,
    gains,
    biases,
    qkv_w,
    out_w,
    queries,
    keys_values,
    log_total,
    later_source,
    grad_one,
    later,
    *refs,
):
    grad_pieces = refs[:members]
    grad_keys, grad_values, grad_rows, sem = refs[members:]
    unused, seq, replica = place(members)
    target, width = queries.shape
    fetch = pltpu.make_async_copy(later_source, later, sem)
    fetch.start()
    grad_context = dot_nt(grad_two[...].astype(LOW), out_w[...]).astype(LOW)
    allowed = (
        lax.broadcasted_iota(jnp.int32, (2 * target, keys_values.shape[1]), 1) < lengths[0, seq]
    )
    grad_queries = []
    for j, part in enumerate(lane_pairs(width)):
        into_queries, into_keys, into_values = attend_back(
            stack_heads(scaled(queries[:, part])),
            keys_values[0, :, part],
            keys_values[1, :, part],
            allowed,
            pair_logs(log_total, j),
            stack_heads(grad_context[:, part]),
        )
        grad_queries.append(into_queries)
        grad_keys[:, part] = into_keys.astype(LOW)
        grad_values[:, part] = into_values.astype(LOW)
    rows = grad_rows.shape[0]
    mine = pl.ds(pl.multiple_of(replica * rows, rows), rows)
    grad_rows[...] = (
        dot_nt(grad_keys[mine, :], qkv_w[1]) + dot_nt(grad_values[mine, :], qkv_w[2])
    ).astype(LOW)
    source = rows // members
    for k, piece in enumerate(grad_pieces):
        piece[...] = grad_rows[pl.ds(pl.multiple_of((seq ^ k) * source, source), source), :]
    total = grad_two[...] + dot_nt(jnp.concatenate(grad_queries, axis=1), qkv_w[0])
    unused, normal, inverse = normalize(summed_one[...], gains[0:1], biases[0:1])
    grad_one[...] = normalize_back(total, normal, inverse, gains[0:1])
    fetch.wait()


def prefix_backward_kernel(
    members,
    prefix_len,
    grad_one,
    prefix,
    out_w,
    qkv,
    context,
    log_total,
    grad_context,
    delta_all,
    *refs,
):
    grad_pieces, (blocks,) = refs[:members], refs[members:]
    unused, seq, replica = place(members)
    target, width = grad_one.shape
    pad = prefix.shape[1]
    grad_context[...] = dot_nt(grad_one[...].astype(LOW), out_w[...]).astype(LOW)
    allowed = lax.broadcasted_iota(jnp.int32, (2 * target, pad), 1) < prefix_len
    size, unused, unused, share = blocks.shape
    grads, deltas = ([], []), []
    for j, part in enumerate(lane_pairs(width)):
        stacked = stack_heads(scaled(qkv[0, :, part]))
        grad_stacked = stack_heads(grad_context[:, part])
        both = context[:, part].astype(FULL)
        delta = jnp.sum(
            grad_stacked.astype(FULL) * jnp.concatenate([both, both], axis=0), -1, keepdims=True
        )
        deltas += [delta[:target], delta[target:]]
        scores = jnp.where(allowed, dot_nt(stacked, prefix[0, :, part]), NEGATIVE)
        probs = jnp.exp(scores - pair_logs(log_total, j))
        grad_probs = dot_nt(grad_stacked, prefix[1, :, part])
        grad_scores = (probs * (grad_probs - delta)).astype(LOW)
        grads[0].append(dot_tn(grad_scores, stacked).astype(LOW))
        grads[1].append(dot_tn(probs.astype(LOW), grad_stacked).astype(LOW))
    delta_all[...] = put_lanes(deltas, delta_all.shape)
    for c in range(2):
        row = jnp.concatenate(grads[c], axis=1)
        for j in range(size):
            blocks[j, c] = row[:, j * share : (j + 1) * share]
    for k, piece in enumerate(grad_pieces):
        owner = replica * members + (seq ^ k)
        piece[...] = jnp.zeros_like(piece)
        for j in range(4):
            piece[:, j * share : (j + 1) * share] = blocks[
                owner, j // 2, 16 * (j % 2) : 16 * (j % 2) + 16, :
            ]


def self_backward_kernel(
    members,
    prefix_len,
    lengths,
    grad_context,
    delta_all,
    prefix,
    qkv,
    log_total,
    later_source,
    grad_qkv,
    later,
    sem,
):
    unused, seq, unused = place(members)
    fetch = pltpu.make_async_copy(later_source, later, sem)
    fetch.start()
    target, width = grad_context.shape
    pad = prefix.shape[1]
    allowed = self_allowed(lengths[0, seq], target, pad, prefix_len)
    for j, part in enumerate(lane_pairs(width)):
        into_queries, into_keys, into_values = attend_back(
            stack_heads(scaled(qkv[0, :, part])),
            jnp.concatenate([prefix[0, :, part], qkv[1, :, part]], axis=0),
            jnp.concatenate([prefix[1, :, part], qkv[2, :, part]], axis=0),
            allowed,
            pair_logs(log_total, j),
            stack_heads(grad_context[:, part]),
            pair_logs(delta_all, j),
            pad,
        )
        grad_qkv[0, :, part] = into_queries
        grad_qkv[1, :, part] = into_keys.astype(LOW)
        grad_qkv[2, :, part] = into_values.astype(LOW)
    fetch.wait()


def self_project_kernel(grad_one, qkv_w, grad_qkv, low, high):
    total = grad_one[...]
    for j in range(3):
        total = total + dot_nt(grad_qkv[j], qkv_w[j])
    half = low.shape[0]
    low[...] = total[:half].astype(LOW)
    high[...] = total[half:].astype(LOW)


def gather_kernel(members, windows, first, *refs):
    pieces, (result, held, sems) = refs[:-3], refs[-3:]
    unused, seq, unused = place(members)
    moves = []
    for k, parts in enumerate(windows):
        at = 0
        for index, start, stop in parts:
            rows = pieces[index][start:stop, :]
            held[k, at : at + stop - start, :] = rows.astype(held.dtype)
            at += stop - start
        move = pltpu.make_async_copy(held.at[k], result.at[seq ^ (first + k)], sems.at[k])
        move.start()
        moves.append(move)
    for move in moves:
        move.wait()


def adam_update(gradient, first_moment, second_moment, weight, step_rate):
    first_new = 0.9 * first_moment + 0.1 * gradient
    second_new = 0.999 * second_moment + 0.001 * gradient * gradient
    corrected_one = first_new / (1.0 - 0.9**STEP)
    corrected_two = second_new / (1.0 - 0.999**STEP)
    weight_new = weight - step_rate * (
        corrected_one / (jnp.sqrt(corrected_two) + 1e-08) + 0.01 * weight
    )
    return (first_new, second_new, weight_new)


def outer_update(outer_weight, momentum, average):
    momentum_new = OUTER_MOMENTUM * momentum + average
    return momentum_new, outer_weight - OUTER_RATE * (average + OUTER_MOMENTUM * momentum_new)


def prefix_rows_of(packed, share, count):
    parts = [packed[:, j * share : (j + 1) * share] for j in range(4)]
    return [jnp.concatenate(parts[2 * c : 2 * c + 2], axis=0)[:count] for c in range(2)]


def update_kernel(members, starts, *refs):
    pieces, prefix_pieces, refs = (
        refs[:members],
        refs[members : 2 * members],
        refs[2 * members :],
    )
    down_w, down_m, down_v, up_w, up_m, up_v, down_outer, up_outer = refs[:8]
    prefix_w, prefix_m, prefix_v, prefix_outer = refs[8:12]
    grad_down, grad_up, new_down, new_up = refs[12], refs[13], refs[14:17], refs[17:20]
    grad_prefix, new_prefix, difference, padded = refs[20], refs[21:24], refs[24], refs[25]
    total = sum(piece[...].astype(FULL) for piece in pieces)
    rows_all = total.shape[0]
    half = rows_all // 2
    wide = down_w.shape[2]
    for j in range(2):
        rows, part = slice(j * half, (j + 1) * half), slice(j * wide, (j + 1) * wide)
        gradient = total[:half, part]
        grad_down[0, rows, :] = gradient
        new = adam_update(gradient, down_m[0, rows], down_v[0, rows], down_w[0, rows], 0.06)
        for ref, value in zip(new_down, new):
            ref[0, rows, :] = value
        difference[:half, part] = (down_outer[rows, :] - new[2]).astype(LOW)
    gradient = total[half:]
    grad_up[0] = gradient
    new = adam_update(gradient, up_m[0], up_v[0], up_w[0], 0.02)
    for ref, value in zip(new_up, new):
        ref[0] = value
    difference[half:rows_all, :] = (up_outer[...] - new[2]).astype(LOW)
    total = sum(
        piece[start : start + 16, :].astype(FULL) for piece, start in zip(prefix_pieces, starts)
    )
    count, unused, share = prefix_w.shape
    padded[...] = jnp.zeros_like(padded)
    for c, gradient in enumerate(prefix_rows_of(total, share, count)):
        grad_prefix[:, c, :] = gradient
        new = adam_update(gradient, prefix_m[:, c, :], prefix_v[:, c, :], prefix_w[:, c, :], 2.0)
        for ref, value in zip(new_prefix, new):
            ref[:, c, :] = value
        padded[c, :count, :] = prefix_outer[:, c, :] - new[2]
    difference[rows_all:, :] = jnp.zeros_like(difference[rows_all:, :])
    for j in range(4):
        difference[rows_all:, j * share : (j + 1) * share] = padded[
            j // 2, 16 * (j % 2) : 16 * (j % 2) + 16, :
        ].astype(LOW)


def add_kernel(left, right, result):
    result[...] = (left[...].astype(FULL) + right[...].astype(FULL)).astype(LOW)


def outer_kernel(groups, left, right, *refs):
    down_outer, up_outer, prefix_outer, down_mom, up_mom, prefix_mom = refs[:6]
    new_down, new_up, new_prefix = refs[6:8], refs[8:10], refs[10:12]
    average = (left[...].astype(FULL) + right[...].astype(FULL)) / groups
    rows_all = average.shape[0] - 16
    half = rows_all // 2
    wide = down_outer.shape[1]
    for j in range(2):
        rows, part = slice(j * half, (j + 1) * half), slice(j * wide, (j + 1) * wide)
        new = outer_update(down_outer[rows, :], down_mom[rows, :], average[:half, part])
        for ref, value in zip(new_down, new):
            ref[rows, :] = value
    new = outer_update(up_outer[...], up_mom[...], average[half:rows_all])
    for ref, value in zip(new_up, new):
        ref[...] = value
    count, unused, share = prefix_outer.shape
    for c, part in enumerate(prefix_rows_of(average[rows_all:], share, count)):
        new = outer_update(prefix_outer[:, c, :], prefix_mom[:, c, :], part)
        for ref, value in zip(new_prefix, new):
            ref[:, c, :] = value


def shaped(shape, dtype):
    return jax.ShapeDtypeStruct(shape, dtype)


def call_whole(
    kernel, spaces, outs, scratch, args, limit=VMEM_LIMIT, out_spaces=None, after=(), micros=0, aliases={}
):
    spaces = list(spaces) + [pltpu.VMEM] * (len(args) - len(spaces)) + [pl.ANY] * len(after)
    if after:
        inner_kernel, count = kernel, len(args)

        def kernel(*refs):
            inner_kernel(*refs[:count], *refs[count + len(after) :])

        args = tuple(args) + tuple(after)
    out_spaces = out_spaces or [pltpu.VMEM] * len(outs)
    return pl.pallas_call(
        kernel,
        in_specs=[pl.BlockSpec(memory_space=space) for space in spaces],
        out_specs=[pl.BlockSpec(memory_space=space) for space in out_spaces],
        out_shape=outs,
        scratch_shapes=scratch,
        input_output_aliases=aliases,
        compiler_params=pltpu.CompilerParams(vmem_limit_bytes=limit),
        cost_estimate=pl.CostEstimate(flops=1000 + int(micros * 1150000000), bytes_accessed=1000, transcendentals=0),
    )(*args)


def local(
    dec_input,
    memory,
    out_grad,
    tgt_lengths,
    src_lengths,
    self_qkv,
    self_out,
    cross_qkv,
    cross_out,
    ffn_in,
    ffn_out,
    norm_gains,
    norm_biases,
    down_w,
    up_w,
    prefix_w,
    down_m,
    down_v,
    up_m,
    up_v,
    prefix_m,
    prefix_v,
    down_outer,
    up_outer,
    prefix_outer,
    down_mom,
    up_mom,
    prefix_mom,
):
    seq_count, target, model_width = dec_input.shape[1:]
    source = memory.shape[2]
    prefix_len = prefix_w.shape[2]
    mem_size = lax.axis_size("mem")
    grp_size = lax.axis_size("grp")
    replicas = mem_size // seq_count
    device = lax.axis_index("mem")
    seq = device % seq_count
    replica = device // seq_count
    adapt = down_w.shape[2]
    inner = ffn_in.shape[1]
    share_rows = down_w.shape[1]
    half_rows = share_rows // 2
    positions = mem_size * source
    resident = positions <= RESIDENT_POSITIONS
    half = target // 2
    bound = functools.partial

    def swap(values_in, bits):
        return lax.ppermute(values_in, "mem", [(j, j ^ bits) for j in range(mem_size)])

    def join(*parts, after=()):
        rows = sum(stop - start for unused, start, stop in parts)
        (result,) = functools.partial(call_whole, micros=0.4)(
            bound(join_kernel, [(start, stop) for unused, start, stop in parts]),
            [],
            [shaped((rows, model_width), LOW)],
            [],
            tuple(piece for piece, unused, unused in parts),
            SMALL_LIMIT,
            after=after,
        )
        return result

    def in_order(windows, pieces, dtype, after=(), micros=2, first=0, into=None):
        rows = sum(stop - start for unused, start, stop in windows[0])
        shape = (seq_count, rows, model_width)
        pieces = tuple(pieces)
        if into is not None:
            after = (into, *after)
        (result,) = call_whole(
            bound(gather_kernel, seq_count, windows, first),
            [],
            [shaped(shape, dtype)],
            [
                pltpu.VMEM((len(windows), *shape[1:]), dtype),
                pltpu.SemaphoreType.DMA((len(windows),)),
            ],
            pieces,
            SMALL_LIMIT,
            out_spaces=[pl.ANY],
            after=after,
            micros=micros,
            aliases={} if into is None else {len(pieces): 0},
        )
        return result

    members = range(seq_count)
    partners = members[1:]
    replica_bits = [seq_count * 2**j for j in range(replicas.bit_length() - 1)]
    bit = replica_bits[0]
    prefix_rows = 32
    prefix_share = prefix_w.shape[3]
    blocks = jnp.pad(
        prefix_w[0].astype(LOW), ((0, 0), (0, prefix_rows - prefix_len), (0, 0))
    ).reshape(4, 16, prefix_share)
    offsets, prefixes = [0], jnp.concatenate([blocks[j] for j in range(4)], axis=1)
    for step in replica_bits:
        prefixes = jnp.concatenate([prefixes, swap(prefixes, step)], axis=1)
        offsets = offsets + [offset ^ step for offset in offsets]
    outward, *mem_send = functools.partial(call_whole, micros=2)(
        bound(first_kernel, seq_count),
        [pltpu.HBM] * 3,
        [shaped((source + share_rows, model_width), LOW)]
        + [shaped((source, model_width), LOW)] * (seq_count - 1),
        [
            pltpu.VMEM((source, model_width), LOW),
            pltpu.VMEM(down_w.shape[1:], FULL),
            pltpu.VMEM(up_w.shape[1:], FULL),
            pltpu.SemaphoreType.DMA((seq_count + 2,)),
        ],
        tuple(
            pltpu.with_memory_space_constraint(values_in, pltpu.HBM)
            for values_in in (memory, down_w, up_w)
        ),
        SMALL_LIMIT,
    )
    outward_arrived = swap(outward, bit)
    messages = call_whole(
        bound(append_kernel, seq_count - 1),
        [],
        [shaped((source + 16, model_width), LOW)] * (seq_count - 1),
        [],
        (prefixes, *mem_send),
        SMALL_LIMIT,
    )
    arrived = [swap(messages[j - 1], j) for j in partners]
    prefix_pieces = [prefixes, *arrived]
    plane_blocks = join(*[(piece, 0, source) for piece in arrived])
    stop = source + share_rows
    own, plane_blocks = lax.optimization_barrier((outward, plane_blocks))
    shares = {
        0: join((own, source, stop)),
        bit: join((outward_arrived, source, stop)),
    }
    for step in replica_bits[1:]:
        for k, piece in list(shares.items()):
            shares[k ^ step] = swap(piece, step)
    plane_arrived = swap(plane_blocks, bit)
    beside = [swap(share, 2) for share in shares.values()]
    across = [swap(share, 1) for share in shares.values()]
    block_refs = [outward, *arrived, outward_arrived, plane_arrived]
    block_places = {0: (0, 0), bit: (seq_count, 0)}
    for j in partners:
        block_places[j] = (j, 0)
        block_places[j ^ bit] = (seq_count + 1, (j - 1) * source)

    rows_full = shaped((target, model_width), FULL)
    rows_low = shaped((target, model_width), LOW)
    logs = shaped((target, LANES), FULL)
    lengths_space = [pltpu.SMEM]
    dma = pltpu.SemaphoreType.DMA

    weights = (cross_qkv, cross_out, ffn_in, ffn_out) if resident else ()
    prefix, qkv, self_log, summed_one, context, *kept = functools.partial(call_whole, micros=2)(
        bound(self_forward_kernel, seq_count, prefix_len, offsets),
        [pltpu.SMEM, pltpu.HBM] + [pltpu.VMEM] * seq_count + [pltpu.HBM] * (len(weights) + 2),
        [
            shaped((2, prefix_rows, model_width), LOW),
            shaped((3, target, model_width), LOW),
            logs,
            rows_full,
            rows_low,
        ]
        + [pltpu.VMEM(weight.shape, LOW) for weight in weights],
        [
            pltpu.VMEM((target, model_width), LOW),
            pltpu.VMEM((mem_size, 2, prefix_rows, prefix_w.shape[3]), LOW),
            pltpu.VMEM(self_qkv.shape, LOW),
            pltpu.VMEM(self_out.shape, LOW),
            dma((len(weights) + 5,)),
        ],
        (tgt_lengths, dec_input, *prefix_pieces, self_qkv, self_out, *weights),
        after=(plane_blocks, *[shares[k] for k in shares if k]),
        limit=VMEM_LIMIT + 8 * 1024 * 1024,
    )
    if resident:
        cross_qkv, cross_out, ffn_in, ffn_out = kept
    summed_one, *beside = lax.optimization_barrier((summed_one, *beside))
    joined = join(*[(share, 0, share_rows) for share in beside])
    far = swap(joined, 1)
    share_refs = [*shares.values(), *beside, *across, far]
    share_places = [None] * mem_size
    for i, offset in enumerate(shares):
        share_places[offset] = (i, 0)
        share_places[offset ^ 2] = (i + replicas, 0)
        share_places[offset ^ 1] = (i + 2 * replicas, 0)
        share_places[offset ^ 3] = (3 * replicas, i * share_rows)
    summed_one, block_refs[-1] = lax.optimization_barrier((summed_one, block_refs[-1]))
    for step in replica_bits[1:]:
        known = sorted(block_places)
        joined = jnp.concatenate(
            [
                block_refs[index][start : start + source]
                for index, start in (block_places[k] for k in known)
            ],
            axis=0,
        )
        for i, k in enumerate(known):
            block_places[k ^ step] = (len(block_refs), i * source)
        block_refs.append(swap(joined, step))
    places = [block_places[k] for k in range(mem_size)]
    cross_limit = VMEM_LIMIT if resident else 4 * VMEM_LIMIT
    cross_queries, keys_values, cross_log, summed_two = functools.partial(call_whole, micros=8)(
        bound(cross_forward_kernel, seq_count, places),
        lengths_space,
        [rows_low, shaped((2, positions, model_width), LOW), logs, rows_full],
        [pltpu.VMEM((positions, model_width), LOW)],
        (src_lengths, summed_one, norm_gains, norm_biases, cross_qkv, cross_out, *block_refs),
        cross_limit,
        after=(joined,),
    )
    normed, slope, partial = functools.partial(call_whole, micros=1)(
        ffn_forward_kernel,
        [],
        [rows_low, shaped((target, inner), LOW), rows_full],
        [],
        (summed_two, norm_gains, norm_biases, ffn_in, ffn_out),
    )
    inner_low = shaped((target, adapt), LOW)
    output_rows, grad_ffn, grad_hidden, act, grad_pre, grad_adapted = functools.partial(
        call_whole, micros=3
    )(
        bound(adapter_kernel, share_places),
        [pltpu.SMEM] + [pltpu.VMEM] * 4 + [pltpu.HBM],
        [rows_low, rows_low, rows_full, inner_low, inner_low, rows_low],
        [
            pltpu.VMEM((model_width, adapt), LOW),
            pltpu.VMEM((adapt, model_width), LOW),
            pltpu.VMEM((target, model_width), LOW),
            dma,
        ],
        (tgt_lengths, partial, normed, norm_gains, norm_biases, out_grad, *share_refs),
    )
    output_one, output_two = swap(output_rows, 1), swap(output_rows, 2)
    grad_pieces = functools.partial(call_whole, micros=2)(
        bound(adapter_gradient_kernel, seq_count),
        [],
        [shaped((share_rows, model_width), LOW)] * seq_count,
        [pltpu.VMEM((model_width, adapt), LOW), pltpu.VMEM((adapt, model_width), LOW)],
        (normed, act, grad_pre, grad_adapted),
    )
    grad_pieces = [grad_pieces[0]] + [swap(grad_pieces[j], j) for j in partners]
    (grad_two,) = functools.partial(call_whole, micros=5)(
        ffn_backward_kernel,
        [],
        [rows_full],
        [],
        (grad_ffn, grad_hidden, summed_two, norm_gains, norm_biases, ffn_in, ffn_out, slope),
    )
    plane_rows = seq_count * source
    grad_one, out_later, *grad_mem_pieces = functools.partial(call_whole, micros=11)(
        bound(cross_backward_kernel, seq_count),
        lengths_space + [pltpu.VMEM] * 9 + [pltpu.HBM],
        [rows_full, pltpu.VMEM(self_out.shape, LOW)]
        + [shaped((source, model_width), LOW)] * seq_count,
        [
            pltpu.VMEM((positions, model_width), LOW),
            pltpu.VMEM((positions, model_width), LOW),
            pltpu.VMEM((plane_rows, model_width), LOW),
            dma,
        ],
        (
            src_lengths,
            grad_two,
            summed_one,
            norm_gains,
            norm_biases,
            cross_qkv,
            cross_out,
            cross_queries,
            keys_values,
            cross_log,
            self_out,
        ),
        cross_limit,
    )
    grad_context, delta_all, *prefix_sent = functools.partial(call_whole, micros=3)(
        bound(prefix_backward_kernel, seq_count, prefix_len),
        [],
        [rows_low, logs] + [shaped((16, model_width), LOW)] * seq_count,
        [pltpu.VMEM((mem_size, 2, prefix_rows, prefix_share), LOW)],
        (grad_one, prefix, out_later, qkv, context, self_log),
    )
    grad_context, output_one, output_two = lax.optimization_barrier(
        (grad_context, output_one, output_two)
    )

    def wave(*parts):
        return join(*[part if isinstance(part, tuple) else (part, 0, part.shape[0]) for part in parts])

    second = [
        None,
        swap(wave((output_two, 0, half), grad_mem_pieces[1], prefix_sent[1]), 1),
        swap(wave((output_one, half, target), grad_mem_pieces[2], prefix_sent[2]), 2),
        swap(wave(grad_mem_pieces[3], prefix_sent[3]), 3),
    ]
    grad_qkv, qkv_later = functools.partial(call_whole, micros=8)(
        bound(self_backward_kernel, seq_count, prefix_len),
        lengths_space + [pltpu.VMEM] * 5 + [pltpu.HBM],
        [shaped((3, target, model_width), LOW), pltpu.VMEM(self_qkv.shape, LOW)],
        [dma],
        (tgt_lengths, grad_context, delta_all, prefix, qkv, self_log, self_qkv),
        after=tuple(grad_pieces[1:]),
    )
    low, high = functools.partial(call_whole, micros=2)(
        self_project_kernel,
        [],
        [shaped((half, model_width), LOW)] * 2,
        [],
        (grad_one, qkv_later, grad_qkv),
        after=tuple(second[1:]),
    )
    low, high, grad_pieces = lax.optimization_barrier((low, high, grad_pieces))
    low_two, high_one = swap(low, 2), swap(high, 1)
    low_one, high_two = swap(low, 1), swap(high, 2)
    low_three, high_three = swap(low_two, 1), swap(high_one, 2)

    def group_swap(values_in, bits):
        return lax.ppermute(values_in, "grp", [(j, j ^ bits) for j in range(grp_size)])

    def flip(values_in):
        return jnp.swapaxes(values_in, -3, -2)

    group_bits = [2**j for j in range(grp_size.bit_length() - 1)][::-1]
    down_shape, up_shape = shaped(down_w.shape, FULL), shaped(up_w.shape, FULL)
    flipped = shaped((prefix_len, 2, prefix_share), FULL)
    packed_rows = half + source
    results = functools.partial(call_whole, micros=1)(
        bound(update_kernel, seq_count, (0, packed_rows, packed_rows, source)),
        [],
        [down_shape, up_shape]
        + [down_shape] * 3
        + [up_shape] * 3
        + [flipped] * 4
        + [shaped((share_rows + 16, model_width), LOW)],
        [pltpu.VMEM((2, prefix_rows, prefix_share), FULL)],
        (
            *grad_pieces,
            prefix_sent[0],
            *second[1:],
            down_w,
            down_m,
            down_v,
            up_w,
            up_m,
            up_v,
            down_outer,
            up_outer,
            flip(prefix_w[0]),
            flip(prefix_m[0]),
            flip(prefix_v[0]),
            flip(prefix_outer),
        ),
        SMALL_LIMIT,
    )
    (grad_down, grad_up), updated, difference = results[:2], results[2:8], results[12]
    grad_prefix, *prefix_new = [flip(values_in)[None] for values_in in results[8:12]]
    for bits in group_bits[:-1]:
        (difference,) = functools.partial(call_whole, micros=0.4)(
            add_kernel,
            [],
            [shaped(difference.shape, LOW)],
            [],
            (difference, group_swap(difference, bits)),
            SMALL_LIMIT,
        )
    new_down_mom, new_down_outer, new_up_mom, new_up_outer, *prefix_results = functools.partial(
        call_whole, micros=1
    )(
        bound(outer_kernel, grp_size),
        [],
        [shaped(down_outer.shape, FULL)] * 2
        + [shaped(up_outer.shape, FULL)] * 2
        + [flipped] * 2,
        [],
        (
            difference,
            group_swap(difference, group_bits[-1]),
            down_outer,
            up_outer,
            flip(prefix_outer),
            down_mom,
            up_mom,
            flip(prefix_mom),
        ),
        SMALL_LIMIT,
    )
    prefix_results = [flip(values_in) for values_in in prefix_results]
    output = in_order(
        (
            ((0, 0, target),),
            ((1, 0, target),),
            ((2, 0, target),),
            ((3, 0, half), (4, 0, half)),
        ),
        (output_rows, output_one, output_two, second[1], second[2]),
        LOW,
    )
    grad_memory = in_order(
        (
            ((0, 0, source),),
            ((1, half, half + source),),
            ((2, half, half + source),),
            ((3, 0, source),),
        ),
        (grad_mem_pieces[0], *second[1:]),
        FULL,
    )
    grad_input = in_order(
        tuple(((2 * k, 0, half), (2 * k + 1, 0, half)) for k in members[:3]),
        (low, high, low_one, high_one, low_two, high_two),
        FULL,
        micros=100,
    )
    grad_input = in_order(
        (((0, 0, half), (1, 0, half)),),
        (low_three, high_three),
        FULL,
        (output, grad_memory, new_down_mom, grad_prefix, *prefix_new, *prefix_results),
        first=3,
        into=grad_input,
    )
    return (
        output[None],
        grad_input[None],
        grad_memory[None],
        grad_down,
        grad_up,
        grad_prefix,
        *updated,
        *prefix_new,
        new_down_mom,
        new_down_outer,
        new_up_mom,
        new_up_outer,
        *prefix_results,
    )


def solution(mesh):
    placed = (
        P("grp", None, None, None),
        P("grp", None, "mem", None),
        P("grp", None, None, None),
        P("grp", None),
        P("grp", None),
        P(),
        P(),
        P(),
        P(),
        P(),
        P(),
        P(),
        P(),
        P("grp", "mem", None),
        P("grp", "mem", None),
        P("grp", None, None, "mem"),
        P("grp", "mem", None),
        P("grp", "mem", None),
        P("grp", "mem", None),
        P("grp", "mem", None),
        P("grp", None, None, "mem"),
        P("grp", None, None, "mem"),
        P("mem", None),
        P("mem", None),
        P(None, None, "mem"),
        P("mem", None),
        P("mem", None),
        P(None, None, "mem"),
    )
    return jax.shard_map(
        local,
        mesh=mesh,
        in_specs=placed,
        out_specs=(
            P("grp", None, None, None),
            P("grp", None, None, None),
            P("grp", None, "mem", None),
            P("grp", "mem", None),
            P("grp", "mem", None),
            P("grp", None, None, "mem"),
            P("grp", "mem", None),
            P("grp", "mem", None),
            P("grp", "mem", None),
            P("grp", "mem", None),
            P("grp", "mem", None),
            P("grp", "mem", None),
            P("grp", None, None, "mem"),
            P("grp", None, None, "mem"),
            P("grp", None, None, "mem"),
            P("mem", None),
            P("mem", None),
            P("mem", None),
            P("mem", None),
            P(None, None, "mem"),
            P(None, None, "mem"),
        ),
        check_vma=False,
    )
```

```python
import functools

import jax
import jax.numpy as jnp
from jax import lax
from jax.experimental import pallas as pl
from jax.experimental.pallas import tpu as pltpu
from jax.sharding import PartitionSpec as P

HDIM = 64
STEP = 10


EPSILON = 1e-05
NEGATIVE = -1e30
ADAPTER_SCALE = 4.0
OUTER_MOMENTUM = 0.9
OUTER_RATE = 0.7
LANES = 128
FFN_BLOCK = 1024
RESIDENT_POSITIONS = 1024
SMALL_LIMIT = 6 * 1024 * 1024
VMEM_LIMIT = 10 * 1024 * 1024
LOW = jnp.bfloat16
FULL = jnp.float32


def normalize(values_in, gain_row, bias_row):
    centered = values_in - jnp.mean(values_in, -1, keepdims=True)
    scale_inv = lax.rsqrt(jnp.mean(centered * centered, -1, keepdims=True) + EPSILON)
    normal = centered * scale_inv
    return (normal * gain_row + bias_row, normal, scale_inv)


def normalize_back(gradient, normal, scale_inv, gain_row):
    scaled = gradient * gain_row
    return scale_inv * (
        scaled
        - jnp.mean(scaled, -1, keepdims=True)
        - normal * jnp.mean(scaled * normal, -1, keepdims=True)
    )


def dot_nn(left, right):
    return lax.dot_general(left, right, (((1,), (0,)), ((), ())), preferred_element_type=FULL)


def dot_nt(left, right):
    return lax.dot_general(left, right, (((1,), (1,)), ((), ())), preferred_element_type=FULL)


def dot_tn(left, right):
    return lax.dot_general(left, right, (((0,), (0,)), ((), ())), preferred_element_type=FULL)


def gelu_both(pre_act):
    cdf = 0.5 + 0.5 * lax.erf(pre_act * 0.7071067811865476)
    density = jnp.exp(-0.5 * pre_act * pre_act) * 0.3989422804014327
    return pre_act * cdf, cdf + pre_act * density


def first_lanes(shape):
    return lax.broadcasted_iota(jnp.int32, shape, 1) < HDIM


def stack_heads(pair):
    first = first_lanes(pair.shape)
    none = jnp.zeros_like(pair)
    return jnp.concatenate([jnp.where(first, pair, none), jnp.where(first, none, pair)], axis=0)


def merge_heads(stacked):
    rows = stacked.shape[0] // 2
    return jnp.where(first_lanes((rows, LANES)), stacked[:rows], stacked[rows:])


def scaled(queries):
    return queries * jnp.asarray(HDIM ** (-0.5), LOW)


def attend(stacked, keys, values, masked):
    scores = dot_nt(stacked, keys) + masked
    top = jnp.max(scores, -1, keepdims=True)
    expo = jnp.exp(scores - top).astype(LOW)
    both = dot_nn(expo, jnp.concatenate([values, jnp.ones_like(values)], axis=1))
    total = both[:, LANES:]
    return both[:, :LANES] / total, top + jnp.log(total[:, :1])


def attend_back(stacked, keys, values, masked, log_total, grad_stacked, delta, skipped=0):
    probs = jnp.exp(dot_nt(stacked, keys) + masked - log_total)
    grad_probs = dot_nt(grad_stacked, values)
    if delta is None:
        delta = jnp.sum(probs * grad_probs, -1, keepdims=True)
    grad_scores = (probs * (grad_probs - delta)).astype(LOW)
    grad_queries = merge_heads(dot_nn(grad_scores, keys)) * (HDIM ** (-0.5))
    grad_keys = dot_tn(grad_scores, stacked)[skipped:]
    grad_values = dot_tn(probs.astype(LOW), grad_stacked)[skipped:]
    return grad_queries.astype(LOW), grad_keys, grad_values


def row_delta(grad_stacked, context):
    both = jnp.concatenate([context, context], axis=0)
    product = (grad_stacked.astype(FULL) * both.astype(FULL)).astype(LOW)
    return dot_nn(product, jnp.ones((LANES, LANES), LOW))


def self_masked(length, target, prefix_pad, prefix_len):
    shape = (2 * target, prefix_pad + target)
    row = lax.broadcasted_iota(jnp.int32, shape, 0)
    row = jnp.where(row >= target, row - target, row)
    column = lax.broadcasted_iota(jnp.int32, shape, 1)
    key = column - prefix_pad
    allowed = (column < prefix_len) | (key >= 0) & (key <= row) & (key < length)
    return jnp.where(allowed, 0.0, NEGATIVE)


def cross_masked(length, positions):
    column = lax.broadcasted_iota(jnp.int32, (1, positions), 1)
    return jnp.where(column < length, 0.0, NEGATIVE)


def put_lanes(columns, shape):
    lane = lax.broadcasted_iota(jnp.int32, shape, 1)
    result = jnp.zeros(shape, FULL)
    for j, column in enumerate(columns):
        result = jnp.where(lane == j, column, result)
    return result


def lane_pairs(width):
    return [slice(at, at + LANES) for at in range(0, width, LANES)]


def pair_logs(log_total, j):
    return jnp.concatenate(
        [log_total[:, 2 * j : 2 * j + 1], log_total[:, 2 * j + 1 : 2 * j + 2]], axis=0
    )


def place(members):
    device = lax.axis_index("mem")
    return device, lax.rem(device, members), lax.div(device, members)


def first_kernel(members, memory, down_w, up_w, outward, *refs):
    blocks, (block, down, up, sems) = refs[: members - 1], refs[members - 1 :]
    unused, seq, unused = place(members)
    moves = [
        pltpu.make_async_copy(memory.at[0, seq], block, sems.at[0]),
        pltpu.make_async_copy(down_w.at[0], down, sems.at[1]),
        pltpu.make_async_copy(up_w.at[0], up, sems.at[2]),
    ]
    for k, partner in enumerate(blocks):
        moves.append(pltpu.make_async_copy(memory.at[0, seq ^ (k + 1)], partner, sems.at[3 + k]))
    for move in moves:
        move.start()
    for move in moves:
        move.wait()
    source = block.shape[0]
    half = up.shape[0]
    wide = down.shape[1]
    outward[:source, :] = block[...]
    outward[source : source + half, :wide] = down[:half, :].astype(LOW)
    outward[source : source + half, wide:] = down[half:, :].astype(LOW)
    outward[source + half :, :] = up[...].astype(LOW)


def append_kernel(count, rows, *refs):
    for block, message in zip(refs[:count], refs[count:]):
        at = block.shape[0]
        message[:at, :] = block[...]
        message[at:, :] = rows[...]


def join_kernel(windows, *refs):
    at = 0
    for piece, (start, stop) in zip(refs, windows):
        refs[-1][at : at + stop - start, :] = piece[start:stop, :]
        at += stop - start


def self_forward_kernel(members, prefix_len, offsets, lengths, tokens_all, *refs):
    pieces, (self_qkv, self_out) = refs[:members], refs[members : members + 2]
    refs = refs[members + 2 :]
    count = (len(refs) - 10) // 2
    sources, refs = refs[:count], refs[count:]
    prefix, qkv, log_total, summed, context_all = refs[:5]
    kept = refs[5 : 5 + count]
    tokens, ordered, qkv_w, out_w, sems = refs[5 + count :]
    device, seq, unused = place(members)
    moves = [pltpu.make_async_copy(tokens_all.at[0, seq], tokens, sems.at[0])]
    for j in range(3):
        moves.append(pltpu.make_async_copy(self_qkv.at[j], qkv_w.at[j], sems.at[1 + j]))
    moves.append(pltpu.make_async_copy(self_out, out_w, sems.at[4]))
    for j in range(count):
        moves.append(pltpu.make_async_copy(sources[j], kept[j], sems.at[5 + j]))
    for move in moves:
        move.start()
    share = ordered.shape[3]
    size = ordered.shape[0]
    for k, piece in enumerate(pieces):
        rows = piece[piece.shape[0] - 16 :, :]
        for i, offset in enumerate(offsets):
            for j in range(4):
                at = (4 * i + j) * share
                ordered[device ^ offset ^ k, j // 2, 16 * (j % 2) : 16 * (j % 2) + 16, :] = rows[
                    :, at : at + share
                ]
    for j in range(size):
        for c in range(2):
            prefix[c, :, j * share : (j + 1) * share] = ordered[j, c]
    moves[0].wait()
    rows = tokens[...]
    target, width = rows.shape
    for j in range(3):
        moves[1 + j].wait()
        qkv[j] = dot_nn(rows, qkv_w[j]).astype(LOW)
    masked = self_masked(lengths[0, seq], target, prefix.shape[1], prefix_len)
    logs = []
    for part in lane_pairs(width):
        keys = jnp.concatenate([prefix[0, :, part], qkv[1, :, part]], axis=0)
        values = jnp.concatenate([prefix[1, :, part], qkv[2, :, part]], axis=0)
        context, log = attend(stack_heads(scaled(qkv[0, :, part])), keys, values, masked)
        context_all[:, part] = merge_heads(context).astype(LOW)
        logs += [log[:target], log[target:]]
    log_total[...] = put_lanes(logs, log_total.shape)
    moves[4].wait()
    summed[...] = rows.astype(FULL) + dot_nn(context_all[...], out_w[...])
    for move in moves[5:]:
        move.wait()


def project_memory(blocks, parts, rows, qkv_w, keys_values, source):
    device = lax.axis_index("mem")
    for i, (unused, index, start) in enumerate(parts):
        rows[i * source : (i + 1) * source, :] = blocks[index][start : start + source, :]
    for j in range(2):
        projected = dot_nn(rows[...], qkv_w[1 + j]).astype(LOW)
        for i, (offset, unused, unused) in enumerate(parts):
            at = pl.multiple_of((device ^ offset) * source, source)
            keys_values[j, pl.ds(at, source), :] = projected[i * source : (i + 1) * source]


def cross_start_kernel(parts, summed_one, gains, biases, qkv_w, *refs):
    blocks, (queries, keys_values, rows) = refs[:-3], refs[-3:]
    hidden = normalize(summed_one[...], gains[0:1], biases[0:1])[0]
    queries[...] = dot_nn(hidden.astype(LOW), qkv_w[0]).astype(LOW)
    project_memory(blocks, parts, rows, qkv_w, keys_values, rows.shape[0] // len(parts))


def cross_forward_kernel(
    members, parts, lengths, summed_one, gains, biases, qkv_w, out_w, queries, *refs
):
    blocks = refs[:-5]
    keys_values, log_total, summed_two, rows = refs[-4:]
    unused, seq, unused = place(members)
    target, width = queries.shape
    project_memory(blocks, parts, rows, qkv_w, keys_values, rows.shape[0] // len(parts))
    hidden = normalize(summed_one[...], gains[0:1], biases[0:1])[0]
    masked = cross_masked(lengths[0, seq], keys_values.shape[1])
    contexts, logs = [], []
    for part in lane_pairs(width):
        context, log = attend(
            stack_heads(scaled(queries[:, part])),
            keys_values[0, :, part],
            keys_values[1, :, part],
            masked,
        )
        contexts.append(merge_heads(context).astype(LOW))
        logs += [log[:target], log[target:]]
    log_total[...] = put_lanes(logs, log_total.shape)
    summed_two[...] = hidden + dot_nn(jnp.concatenate(contexts, axis=1), out_w[...])


def ffn_forward_kernel(summed_two, gains, biases, in_w, out_w, normed, slope, partial):
    hidden = normalize(summed_two[...], gains[1:2], biases[1:2])[0]
    low = hidden.astype(LOW)
    normed[...] = low
    inner = in_w.shape[1]
    parts = [slice(at, at + FFN_BLOCK) for at in range(0, inner, FFN_BLOCK)]
    pre = dot_nn(low, in_w[:, parts[0]])
    total = hidden
    for j, part in enumerate(parts):
        following = dot_nn(low, in_w[:, parts[j + 1]]) if j + 1 < len(parts) else None
        act, slope_full = gelu_both(pre)
        slope[:, part] = slope_full.astype(LOW)
        total = total + dot_nn(act.astype(LOW), out_w[part, :])
        pre = following
    partial[...] = total


def adapter_kernel(
    places, lengths, partial, normed, gains, biases, cotangent_all, *refs
):
    count = 1 + max(index for index, unused in places)
    shares, refs = refs[:count], refs[count:]
    output, grad_ffn, grad_hidden, act_low, grad_pre_low, grad_low, down, up, cotangent, sem = refs
    device, seq, unused = place(lengths.shape[1])
    move = pltpu.make_async_copy(cotangent_all.at[0, seq], cotangent, sem)
    move.start()
    rows = down.shape[0] // len(places)
    half = rows // 2
    wide = down.shape[1]
    for k, (index, start) in enumerate(places):
        owner, share = device ^ k, shares[index]
        at = pl.multiple_of(owner * rows, rows)
        down[pl.ds(at, half), :] = share[start : start + half, :wide]
        down[pl.ds(at + half, half), :] = share[start : start + half, wide:]
        at = pl.multiple_of(owner * half, half)
        up[pl.ds(at, half), :] = share[start + half : start + rows, :]
    act, slope = gelu_both(dot_nn(normed[...], down[...]))
    act_low[...] = act.astype(LOW)
    total = partial[...] + ADAPTER_SCALE * dot_nn(act_low[...], up[...])
    rows_out, normal, inverse = normalize(total, gains[2:3], biases[2:3])
    output[...] = rows_out.astype(LOW)
    live = lax.broadcasted_iota(jnp.int32, (total.shape[0], 1), 0) < lengths[0, seq]
    move.wait()
    grad_three = normalize_back(
        jnp.where(live, cotangent[...].astype(FULL), 0.0), normal, inverse, gains[2:3]
    )
    grad_ffn[...] = grad_three.astype(LOW)
    grad_low[...] = (ADAPTER_SCALE * grad_three).astype(LOW)
    grad_pre = (dot_nt(grad_low[...], up[...]) * slope).astype(LOW)
    grad_pre_low[...] = grad_pre
    grad_hidden[...] = grad_three + dot_nt(grad_pre, down[...])


def adapter_gradient_kernel(members, normed, act, grad_pre, grad_adapted, *refs):
    grad_pieces, (grad_down, grad_up) = refs[:members], refs[members:]
    unused, seq, replica = place(members)
    grad_down[...] = dot_tn(normed[...], grad_pre[...]).astype(LOW)
    grad_up[...] = dot_tn(act[...], grad_adapted[...]).astype(LOW)
    rows = grad_pieces[0].shape[0]
    half = rows // 2
    wide = grad_down.shape[1]
    for k, piece in enumerate(grad_pieces):
        owner = replica * members + (seq ^ k)
        at = pl.multiple_of(owner * rows, rows)
        piece[:half, :wide] = grad_down[pl.ds(at, half), :]
        piece[:half, wide:] = grad_down[pl.ds(at + half, half), :]
        piece[half:, :] = grad_up[pl.ds(pl.multiple_of(owner * half, half), half), :]


def ffn_backward_kernel(
    grad_ffn, grad_hidden, summed_two, gains, biases, in_w, out_w, slope, grad_two
):
    low = grad_ffn[...]
    inner = in_w.shape[1]
    parts = [slice(at, at + FFN_BLOCK) for at in range(0, inner, FFN_BLOCK)]
    grad_act = dot_nt(low, out_w[parts[0], :])
    total = grad_hidden[...]
    for j, part in enumerate(parts):
        following = dot_nt(low, out_w[parts[j + 1], :]) if j + 1 < len(parts) else None
        grad_pre = (grad_act * slope[:, part].astype(FULL)).astype(LOW)
        total = total + dot_nt(grad_pre, in_w[:, part])
        grad_act = following
    unused, normal, inverse = normalize(summed_two[...], gains[1:2], biases[1:2])
    grad_two[...] = normalize_back(total, normal, inverse, gains[1:2])


def cross_backward_kernel(
    members,
    lengths,
    grad_two,
    summed_one,
    gains,
    biases,
    qkv_w,
    out_w,
    queries,
    keys_values,
    log_total,
    later_source,
    grad_one,
    later,
    *refs,
):
    grad_pieces = refs[:members]
    grad_keys, grad_values, grad_rows, sem = refs[members:]
    unused, seq, replica = place(members)
    target, width = queries.shape
    fetch = pltpu.make_async_copy(later_source, later, sem)
    fetch.start()
    grad_context = dot_nt(grad_two[...].astype(LOW), out_w[...]).astype(LOW)
    masked = cross_masked(lengths[0, seq], keys_values.shape[1])
    grad_queries = []
    for j, part in enumerate(lane_pairs(width)):
        into_queries, into_keys, into_values = attend_back(
            stack_heads(scaled(queries[:, part])),
            keys_values[0, :, part],
            keys_values[1, :, part],
            masked,
            pair_logs(log_total, j),
            stack_heads(grad_context[:, part]),
            None,
        )
        grad_queries.append(into_queries)
        grad_keys[:, part] = into_keys.astype(LOW)
        grad_values[:, part] = into_values.astype(LOW)
    rows = grad_rows.shape[0]
    mine = pl.ds(pl.multiple_of(replica * rows, rows), rows)
    grad_rows[...] = (
        dot_nt(grad_keys[mine, :], qkv_w[1]) + dot_nt(grad_values[mine, :], qkv_w[2])
    ).astype(LOW)
    source = rows // members
    for k, piece in enumerate(grad_pieces):
        piece[...] = grad_rows[pl.ds(pl.multiple_of((seq ^ k) * source, source), source), :]
    total = grad_two[...] + dot_nt(jnp.concatenate(grad_queries, axis=1), qkv_w[0])
    unused, normal, inverse = normalize(summed_one[...], gains[0:1], biases[0:1])
    grad_one[...] = normalize_back(total, normal, inverse, gains[0:1])
    fetch.wait()


def prefix_backward_kernel(
    members,
    prefix_len,
    grad_one,
    prefix,
    out_w,
    qkv,
    context,
    log_total,
    grad_context,
    delta_all,
    *refs,
):
    grad_pieces, (blocks,) = refs[:members], refs[members:]
    unused, seq, replica = place(members)
    target, width = grad_one.shape
    pad = prefix.shape[1]
    grad_context[...] = dot_nt(grad_one[...].astype(LOW), out_w[...]).astype(LOW)
    allowed = lax.broadcasted_iota(jnp.int32, (2 * target, pad), 1) < prefix_len
    size, unused, unused, share = blocks.shape
    grads, deltas = ([], []), []
    for j, part in enumerate(lane_pairs(width)):
        stacked = stack_heads(scaled(qkv[0, :, part]))
        grad_stacked = stack_heads(grad_context[:, part])
        delta = row_delta(grad_stacked, context[:, part])
        deltas += [delta[:target], delta[target:]]
        scores = jnp.where(allowed, dot_nt(stacked, prefix[0, :, part]), NEGATIVE)
        probs = jnp.exp(scores - pair_logs(log_total, j))
        grad_probs = dot_nt(grad_stacked, prefix[1, :, part])
        grad_scores = (probs * (grad_probs - delta[:, :pad])).astype(LOW)
        grads[0].append(dot_tn(grad_scores, stacked).astype(LOW))
        grads[1].append(dot_tn(probs.astype(LOW), grad_stacked).astype(LOW))
    delta_all[...] = put_lanes(deltas, delta_all.shape)
    for c in range(2):
        row = jnp.concatenate(grads[c], axis=1)
        for j in range(size):
            blocks[j, c] = row[:, j * share : (j + 1) * share]
    for k, piece in enumerate(grad_pieces):
        owner = replica * members + (seq ^ k)
        piece[...] = jnp.zeros_like(piece)
        for j in range(4):
            piece[:, j * share : (j + 1) * share] = blocks[
                owner, j // 2, 16 * (j % 2) : 16 * (j % 2) + 16, :
            ]


def self_backward_kernel(
    members,
    prefix_len,
    lengths,
    grad_context,
    delta_all,
    prefix,
    qkv,
    log_total,
    later_source,
    grad_qkv,
    later,
    sem,
):
    unused, seq, unused = place(members)
    fetch = pltpu.make_async_copy(later_source, later, sem)
    fetch.start()
    target, width = grad_context.shape
    pad = prefix.shape[1]
    masked = self_masked(lengths[0, seq], target, pad, prefix_len)
    for j, part in enumerate(lane_pairs(width)):
        into_queries, into_keys, into_values = attend_back(
            stack_heads(scaled(qkv[0, :, part])),
            jnp.concatenate([prefix[0, :, part], qkv[1, :, part]], axis=0),
            jnp.concatenate([prefix[1, :, part], qkv[2, :, part]], axis=0),
            masked,
            pair_logs(log_total, j),
            stack_heads(grad_context[:, part]),
            pair_logs(delta_all, j),
            pad,
        )
        grad_qkv[0, :, part] = into_queries
        grad_qkv[1, :, part] = into_keys.astype(LOW)
        grad_qkv[2, :, part] = into_values.astype(LOW)
    fetch.wait()


def self_project_kernel(grad_one, qkv_w, grad_qkv, low, high):
    total = grad_one[...]
    for j in range(3):
        total = total + dot_nt(grad_qkv[j], qkv_w[j])
    half = low.shape[0]
    low[...] = total[:half].astype(LOW)
    high[...] = total[half:].astype(LOW)


def gather_kernel(members, windows, first, *refs):
    pieces, (result, held, sems) = refs[:-3], refs[-3:]
    unused, seq, unused = place(members)
    moves = []
    for k, parts in enumerate(windows):
        at = 0
        for index, start, stop in parts:
            rows = pieces[index][start:stop, :]
            held[k, at : at + stop - start, :] = rows.astype(held.dtype)
            at += stop - start
        move = pltpu.make_async_copy(held.at[k], result.at[seq ^ (first + k)], sems.at[k])
        move.start()
        moves.append(move)
    for move in moves:
        move.wait()


def adam_update(gradient, first_moment, second_moment, weight, step_rate):
    first_new = 0.9 * first_moment + 0.1 * gradient
    second_new = 0.999 * second_moment + 0.001 * gradient * gradient
    corrected_one = first_new / (1.0 - 0.9**STEP)
    corrected_two = second_new / (1.0 - 0.999**STEP)
    weight_new = weight - step_rate * (
        corrected_one / (jnp.sqrt(corrected_two) + 1e-08) + 0.01 * weight
    )
    return (first_new, second_new, weight_new)


def outer_update(outer_weight, momentum, average):
    momentum_new = OUTER_MOMENTUM * momentum + average
    return momentum_new, outer_weight - OUTER_RATE * (average + OUTER_MOMENTUM * momentum_new)


def prefix_rows_of(packed, share, count):
    parts = [packed[:, j * share : (j + 1) * share] for j in range(4)]
    return [jnp.concatenate(parts[2 * c : 2 * c + 2], axis=0)[:count] for c in range(2)]


def update_kernel(members, starts, *refs):
    pieces, prefix_pieces, refs = (
        refs[:members],
        refs[members : 2 * members],
        refs[2 * members :],
    )
    down_w, down_m, down_v, up_w, up_m, up_v, down_outer, up_outer = refs[:8]
    prefix_w, prefix_m, prefix_v, prefix_outer = refs[8:12]
    grad_down, grad_up, new_down, new_up = refs[12], refs[13], refs[14:17], refs[17:20]
    grad_prefix, new_prefix, difference, padded = refs[20], refs[21:24], refs[24], refs[25]
    total = sum(piece[...].astype(FULL) for piece in pieces)
    rows_all = total.shape[0]
    half = rows_all // 2
    wide = down_w.shape[2]
    for j in range(2):
        rows, part = slice(j * half, (j + 1) * half), slice(j * wide, (j + 1) * wide)
        gradient = total[:half, part]
        grad_down[0, rows, :] = gradient
        new = adam_update(gradient, down_m[0, rows], down_v[0, rows], down_w[0, rows], 0.06)
        for ref, value in zip(new_down, new):
            ref[0, rows, :] = value
        difference[:half, part] = (down_outer[rows, :] - new[2]).astype(LOW)
    gradient = total[half:]
    grad_up[0] = gradient
    new = adam_update(gradient, up_m[0], up_v[0], up_w[0], 0.02)
    for ref, value in zip(new_up, new):
        ref[0] = value
    difference[half:rows_all, :] = (up_outer[...] - new[2]).astype(LOW)
    total = sum(
        piece[start : start + 16, :].astype(FULL) for piece, start in zip(prefix_pieces, starts)
    )
    count, unused, share = prefix_w.shape
    padded[...] = jnp.zeros_like(padded)
    for c, gradient in enumerate(prefix_rows_of(total, share, count)):
        grad_prefix[:, c, :] = gradient
        new = adam_update(gradient, prefix_m[:, c, :], prefix_v[:, c, :], prefix_w[:, c, :], 2.0)
        for ref, value in zip(new_prefix, new):
            ref[:, c, :] = value
        padded[c, :count, :] = prefix_outer[:, c, :] - new[2]
    difference[rows_all:, :] = jnp.zeros_like(difference[rows_all:, :])
    for j in range(4):
        difference[rows_all:, j * share : (j + 1) * share] = padded[
            j // 2, 16 * (j % 2) : 16 * (j % 2) + 16, :
        ].astype(LOW)


def add_kernel(left, right, result):
    result[...] = (left[...].astype(FULL) + right[...].astype(FULL)).astype(LOW)


def outer_kernel(groups, left, right, *refs):
    down_outer, up_outer, prefix_outer, down_mom, up_mom, prefix_mom = refs[:6]
    new_down, new_up, new_prefix = refs[6:8], refs[8:10], refs[10:12]
    average = (left[...].astype(FULL) + right[...].astype(FULL)) / groups
    rows_all = average.shape[0] - 16
    half = rows_all // 2
    wide = down_outer.shape[1]
    for j in range(2):
        rows, part = slice(j * half, (j + 1) * half), slice(j * wide, (j + 1) * wide)
        new = outer_update(down_outer[rows, :], down_mom[rows, :], average[:half, part])
        for ref, value in zip(new_down, new):
            ref[rows, :] = value
    new = outer_update(up_outer[...], up_mom[...], average[half:rows_all])
    for ref, value in zip(new_up, new):
        ref[...] = value
    count, unused, share = prefix_outer.shape
    for c, part in enumerate(prefix_rows_of(average[rows_all:], share, count)):
        new = outer_update(prefix_outer[:, c, :], prefix_mom[:, c, :], part)
        for ref, value in zip(new_prefix, new):
            ref[:, c, :] = value


def fixed(shape):
    return pl.BlockSpec(shape, lambda *unused: (0,) * len(shape))


def shaped(shape, dtype):
    return jax.ShapeDtypeStruct(shape, dtype)


def call_whole(
    kernel, spaces, outs, scratch, args, limit=VMEM_LIMIT, out_spaces=None, after=(), micros=0, aliases={}
):
    spaces = list(spaces) + [pltpu.VMEM] * (len(args) - len(spaces)) + [pl.ANY] * len(after)
    if after:
        inner_kernel, count = kernel, len(args)

        def kernel(*refs):
            inner_kernel(*refs[:count], *refs[count + len(after) :])

        args = tuple(args) + tuple(after)
    out_spaces = out_spaces or [pltpu.VMEM] * len(outs)
    return pl.pallas_call(
        kernel,
        in_specs=[pl.BlockSpec(memory_space=space) for space in spaces],
        out_specs=[pl.BlockSpec(memory_space=space) for space in out_spaces],
        out_shape=outs,
        scratch_shapes=scratch,
        input_output_aliases=aliases,
        compiler_params=pltpu.CompilerParams(vmem_limit_bytes=limit),
        cost_estimate=pl.CostEstimate(flops=1000 + int(micros * 1150000000), bytes_accessed=1000, transcendentals=0),
    )(*args)


def local(
    dec_input,
    memory,
    out_grad,
    tgt_lengths,
    src_lengths,
    self_qkv,
    self_out,
    cross_qkv,
    cross_out,
    ffn_in,
    ffn_out,
    norm_gains,
    norm_biases,
    down_w,
    up_w,
    prefix_w,
    down_m,
    down_v,
    up_m,
    up_v,
    prefix_m,
    prefix_v,
    down_outer,
    up_outer,
    prefix_outer,
    down_mom,
    up_mom,
    prefix_mom,
):
    seq_count, target, model_width = dec_input.shape[1:]
    source = memory.shape[2]
    prefix_len = prefix_w.shape[2]
    mem_size = lax.axis_size("mem")
    grp_size = lax.axis_size("grp")
    replicas = mem_size // seq_count
    device = lax.axis_index("mem")
    seq = device % seq_count
    replica = device // seq_count
    adapt = down_w.shape[2]
    inner = ffn_in.shape[1]
    share_rows = down_w.shape[1]
    half_rows = share_rows // 2
    positions = mem_size * source
    resident = positions <= RESIDENT_POSITIONS
    half = target // 2
    cut = target * 96 // 256
    bound = functools.partial

    def swap(values_in, bits):
        return lax.ppermute(values_in, "mem", [(j, j ^ bits) for j in range(mem_size)])

    def join(*parts, after=()):
        rows = sum(stop - start for unused, start, stop in parts)
        (result,) = functools.partial(call_whole, micros=0.4)(
            bound(join_kernel, [(start, stop) for unused, start, stop in parts]),
            [],
            [shaped((rows, model_width), LOW)],
            [],
            tuple(piece for piece, unused, unused in parts),
            SMALL_LIMIT,
            after=after,
        )
        return result

    def in_order(windows, pieces, dtype, after=(), micros=2, first=0, into=None):
        rows = sum(stop - start for unused, start, stop in windows[0])
        shape = (seq_count, rows, model_width)
        pieces = tuple(pieces)
        if into is not None:
            after = (into, *after)
        (result,) = call_whole(
            bound(gather_kernel, seq_count, windows, first),
            [],
            [shaped(shape, dtype)],
            [
                pltpu.VMEM((len(windows), *shape[1:]), dtype),
                pltpu.SemaphoreType.DMA((len(windows),)),
            ],
            pieces,
            SMALL_LIMIT,
            out_spaces=[pl.ANY],
            after=after,
            micros=micros,
            aliases={} if into is None else {len(pieces): 0},
        )
        return result

    members = range(seq_count)
    partners = members[1:]
    replica_bits = [seq_count * 2**j for j in range(replicas.bit_length() - 1)]
    bit = replica_bits[0]
    prefix_rows = 32
    prefix_share = prefix_w.shape[3]
    blocks = jnp.pad(
        prefix_w[0].astype(LOW), ((0, 0), (0, prefix_rows - prefix_len), (0, 0))
    ).reshape(4, 16, prefix_share)
    offsets, prefixes = [0], jnp.concatenate([blocks[j] for j in range(4)], axis=1)
    for step in replica_bits:
        prefixes = jnp.concatenate([prefixes, swap(prefixes, step)], axis=1)
        offsets = offsets + [offset ^ step for offset in offsets]
    outward, *mem_send = functools.partial(call_whole, micros=2)(
        bound(first_kernel, seq_count),
        [pltpu.HBM] * 3,
        [shaped((source + share_rows, model_width), LOW)]
        + [shaped((source, model_width), LOW)] * (seq_count - 1),
        [
            pltpu.VMEM((source, model_width), LOW),
            pltpu.VMEM(down_w.shape[1:], FULL),
            pltpu.VMEM(up_w.shape[1:], FULL),
            pltpu.SemaphoreType.DMA((seq_count + 2,)),
        ],
        tuple(
            pltpu.with_memory_space_constraint(values_in, pltpu.HBM)
            for values_in in (memory, down_w, up_w)
        ),
        SMALL_LIMIT,
    )
    outward_arrived = swap(outward, bit)
    messages = call_whole(
        bound(append_kernel, seq_count - 1),
        [],
        [shaped((source + 16, model_width), LOW)] * (seq_count - 1),
        [],
        (prefixes, *mem_send),
        SMALL_LIMIT,
    )
    arrived = [swap(messages[j - 1], j) for j in partners]
    prefix_pieces = [prefixes, *arrived]
    plane_blocks = join(*[(piece, 0, source) for piece in arrived])
    stop = source + share_rows
    own, plane_blocks = lax.optimization_barrier((outward, plane_blocks))
    shares = {
        0: join((own, source, stop)),
        bit: join((outward_arrived, source, stop)),
    }
    for step in replica_bits[1:]:
        for k, piece in list(shares.items()):
            shares[k ^ step] = swap(piece, step)
    plane_arrived = swap(plane_blocks, bit)
    beside = [swap(share, 2) for share in shares.values()]
    across = [swap(share, 1) for share in shares.values()]
    block_refs = [outward, *arrived, outward_arrived, plane_arrived]
    block_places = {0: (0, 0), bit: (seq_count, 0)}
    for j in partners:
        block_places[j] = (j, 0)
        block_places[j ^ bit] = (seq_count + 1, (j - 1) * source)

    rows_full = shaped((target, model_width), FULL)
    rows_low = shaped((target, model_width), LOW)
    logs = shaped((target, LANES), FULL)
    lengths_space = [pltpu.SMEM]
    dma = pltpu.SemaphoreType.DMA

    weights = (cross_qkv, cross_out, ffn_in, ffn_out) if resident else ()
    prefix, qkv, self_log, summed_one, context, *kept = functools.partial(call_whole, micros=2)(
        bound(self_forward_kernel, seq_count, prefix_len, offsets),
        [pltpu.SMEM, pltpu.HBM] + [pltpu.VMEM] * seq_count + [pltpu.HBM] * (len(weights) + 2),
        [
            shaped((2, prefix_rows, model_width), LOW),
            shaped((3, target, model_width), LOW),
            logs,
            rows_full,
            rows_low,
        ]
        + [pltpu.VMEM(weight.shape, LOW) for weight in weights],
        [
            pltpu.VMEM((target, model_width), LOW),
            pltpu.VMEM((mem_size, 2, prefix_rows, prefix_w.shape[3]), LOW),
            pltpu.VMEM(self_qkv.shape, LOW),
            pltpu.VMEM(self_out.shape, LOW),
            dma((len(weights) + 5,)),
        ],
        (tgt_lengths, dec_input, *prefix_pieces, self_qkv, self_out, *weights),
        after=(plane_blocks, *[shares[k] for k in shares if k]),
        limit=VMEM_LIMIT + 8 * 1024 * 1024,
    )
    if resident:
        cross_qkv, cross_out, ffn_in, ffn_out = kept
    summed_one, block_refs[-1] = lax.optimization_barrier((summed_one, block_refs[-1]))
    for step in replica_bits[1:]:
        known = sorted(block_places)
        joined = jnp.concatenate(
            [
                block_refs[index][start : start + source]
                for index, start in (block_places[k] for k in known)
            ],
            axis=0,
        )
        for i, k in enumerate(known):
            block_places[k ^ step] = (len(block_refs), i * source)
        block_refs.append(swap(joined, step))
    places = [block_places[k] for k in range(mem_size)]
    cross_limit = VMEM_LIMIT if resident else 4 * VMEM_LIMIT
    early = [k for k in range(mem_size) if places[k][0] <= seq_count]
    late = [k for k in range(mem_size) if places[k][0] > seq_count]
    cross_queries, keys_values = functools.partial(call_whole, micros=3)(
        bound(cross_start_kernel, [(k, *places[k]) for k in early]),
        [],
        [rows_low, shaped((2, positions, model_width), LOW)],
        [pltpu.VMEM((len(early) * source, model_width), LOW)],
        (summed_one, norm_gains, norm_biases, cross_qkv, *block_refs[: seq_count + 1]),
    )
    cross_queries, *beside = lax.optimization_barrier((cross_queries, *beside))
    joined = join(*[(share, 0, share_rows) for share in beside])
    far = swap(joined, 1)
    share_refs = [*shares.values(), *beside, *across, far]
    share_places = [None] * mem_size
    for i, offset in enumerate(shares):
        share_places[offset] = (i, 0)
        share_places[offset ^ 2] = (i + replicas, 0)
        share_places[offset ^ 1] = (i + 2 * replicas, 0)
        share_places[offset ^ 3] = (3 * replicas, i * share_rows)
    late_refs = block_refs[seq_count + 1 :]
    late_parts = [(k, places[k][0] - seq_count - 1, places[k][1]) for k in late]
    keys_values, cross_log, summed_two = functools.partial(call_whole, micros=8)(
        bound(cross_forward_kernel, seq_count, late_parts),
        lengths_space,
        [shaped((2, positions, model_width), LOW), logs, rows_full],
        [pltpu.VMEM((len(late) * source, model_width), LOW)],
        (
            src_lengths,
            summed_one,
            norm_gains,
            norm_biases,
            cross_qkv,
            cross_out,
            cross_queries,
            *late_refs,
            keys_values,
        ),
        cross_limit,
        after=(joined,),
        aliases={7 + len(late_refs): 0},
    )
    normed, slope, partial = functools.partial(call_whole, micros=1)(
        ffn_forward_kernel,
        [],
        [rows_low, shaped((target, inner), LOW), rows_full],
        [],
        (summed_two, norm_gains, norm_biases, ffn_in, ffn_out),
    )
    inner_low = shaped((target, adapt), LOW)
    output_rows, grad_ffn, grad_hidden, act, grad_pre, grad_adapted = functools.partial(
        call_whole, micros=3
    )(
        bound(adapter_kernel, share_places),
        [pltpu.SMEM] + [pltpu.VMEM] * 4 + [pltpu.HBM],
        [rows_low, rows_low, rows_full, inner_low, inner_low, rows_low],
        [
            pltpu.VMEM((model_width, adapt), LOW),
            pltpu.VMEM((adapt, model_width), LOW),
            pltpu.VMEM((target, model_width), LOW),
            dma,
        ],
        (tgt_lengths, partial, normed, norm_gains, norm_biases, out_grad, *share_refs),
    )
    output_one, output_two = swap(output_rows, 1), swap(output_rows, 2)
    grad_pieces = functools.partial(call_whole, micros=2)(
        bound(adapter_gradient_kernel, seq_count),
        [],
        [shaped((share_rows, model_width), LOW)] * seq_count,
        [pltpu.VMEM((model_width, adapt), LOW), pltpu.VMEM((adapt, model_width), LOW)],
        (normed, act, grad_pre, grad_adapted),
    )
    grad_pieces = [grad_pieces[0]] + [swap(grad_pieces[j], j) for j in partners]
    (grad_two,) = functools.partial(call_whole, micros=5)(
        ffn_backward_kernel,
        [],
        [rows_full],
        [],
        (grad_ffn, grad_hidden, summed_two, norm_gains, norm_biases, ffn_in, ffn_out, slope),
    )
    plane_rows = seq_count * source
    grad_one, out_later, *grad_mem_pieces = functools.partial(call_whole, micros=11)(
        bound(cross_backward_kernel, seq_count),
        lengths_space + [pltpu.VMEM] * 9 + [pltpu.HBM],
        [rows_full, pltpu.VMEM(self_out.shape, LOW)]
        + [shaped((source, model_width), LOW)] * seq_count,
        [
            pltpu.VMEM((positions, model_width), LOW),
            pltpu.VMEM((positions, model_width), LOW),
            pltpu.VMEM((plane_rows, model_width), LOW),
            dma,
        ],
        (
            src_lengths,
            grad_two,
            summed_one,
            norm_gains,
            norm_biases,
            cross_qkv,
            cross_out,
            cross_queries,
            keys_values,
            cross_log,
            self_out,
        ),
        cross_limit,
    )
    grad_context, delta_all, *prefix_sent = functools.partial(call_whole, micros=3)(
        bound(prefix_backward_kernel, seq_count, prefix_len),
        [],
        [rows_low, logs] + [shaped((16, model_width), LOW)] * seq_count,
        [pltpu.VMEM((mem_size, 2, prefix_rows, prefix_share), LOW)],
        (grad_one, prefix, out_later, qkv, context, self_log),
    )
    grad_context, output_one, output_two = lax.optimization_barrier(
        (grad_context, output_one, output_two)
    )

    def wave(*parts):
        return join(*[part if isinstance(part, tuple) else (part, 0, part.shape[0]) for part in parts])

    second = [
        None,
        swap(wave((output_two, 0, cut), grad_mem_pieces[1], prefix_sent[1]), 1),
        swap(wave((output_one, cut, target), grad_mem_pieces[2], prefix_sent[2]), 2),
        swap(wave(grad_mem_pieces[3], prefix_sent[3]), 3),
    ]
    grad_qkv, qkv_later = functools.partial(call_whole, micros=8)(
        bound(self_backward_kernel, seq_count, prefix_len),
        lengths_space + [pltpu.VMEM] * 5 + [pltpu.HBM],
        [shaped((3, target, model_width), LOW), pltpu.VMEM(self_qkv.shape, LOW)],
        [dma],
        (tgt_lengths, grad_context, delta_all, prefix, qkv, self_log, self_qkv),
        after=tuple(grad_pieces[1:]),
    )
    low, high = functools.partial(call_whole, micros=2)(
        self_project_kernel,
        [],
        [shaped((half, model_width), LOW)] * 2,
        [],
        (grad_one, qkv_later, grad_qkv),
        after=tuple(second[1:]),
    )
    low, high, grad_pieces = lax.optimization_barrier((low, high, grad_pieces))
    low_two, high_one = swap(low, 2), swap(high, 1)
    low_one, high_two = swap(join((low, 0, half)), 1), swap(high, 2)
    low_three, high_three = swap(low_two, 1), swap(high_one, 2)

    def group_swap(values_in, bits):
        return lax.ppermute(values_in, "grp", [(j, j ^ bits) for j in range(grp_size)])

    def flip(values_in):
        return jnp.swapaxes(values_in, -3, -2)

    group_bits = [2**j for j in range(grp_size.bit_length() - 1)][::-1]
    down_shape, up_shape = shaped(down_w.shape, FULL), shaped(up_w.shape, FULL)
    flipped = shaped((prefix_len, 2, prefix_share), FULL)
    results = functools.partial(call_whole, micros=1)(
        bound(update_kernel, seq_count, (0, cut + source, target - cut + source, source)),
        [],
        [down_shape, up_shape]
        + [down_shape] * 3
        + [up_shape] * 3
        + [flipped] * 4
        + [shaped((share_rows + 16, model_width), LOW)],
        [pltpu.VMEM((2, prefix_rows, prefix_share), FULL)],
        (
            *grad_pieces,
            prefix_sent[0],
            *second[1:],
            down_w,
            down_m,
            down_v,
            up_w,
            up_m,
            up_v,
            down_outer,
            up_outer,
            flip(prefix_w[0]),
            flip(prefix_m[0]),
            flip(prefix_v[0]),
            flip(prefix_outer),
        ),
        SMALL_LIMIT,
    )
    (grad_down, grad_up), updated, difference = results[:2], results[2:8], results[12]
    grad_prefix, *prefix_new = [flip(values_in)[None] for values_in in results[8:12]]
    for bits in group_bits[:-1]:
        (difference,) = functools.partial(call_whole, micros=0.4)(
            add_kernel,
            [],
            [shaped(difference.shape, LOW)],
            [],
            (difference, group_swap(difference, bits)),
            SMALL_LIMIT,
        )
    outer_args = (
        difference,
        group_swap(difference, group_bits[-1]),
        down_outer,
        up_outer,
        flip(prefix_outer),
        down_mom,
        up_mom,
        flip(prefix_mom),
    )
    outer_shapes = (
        [shaped(down_outer.shape, FULL)] * 2 + [shaped(up_outer.shape, FULL)] * 2 + [flipped] * 2
    )
    new_down_mom, new_down_outer, new_up_mom, new_up_outer, *prefix_results = pl.pallas_call(
        bound(outer_kernel, grp_size),
        grid=(1,),
        in_specs=[fixed(values_in.shape) for values_in in outer_args],
        out_specs=[fixed(result.shape) for result in outer_shapes],
        out_shape=outer_shapes,
        compiler_params=pltpu.CompilerParams(vmem_limit_bytes=SMALL_LIMIT),
    )(*outer_args)
    prefix_results = [flip(values_in) for values_in in prefix_results]
    output = in_order(
        (
            ((0, 0, target),),
            ((1, 0, target),),
            ((2, 0, target),),
            ((3, 0, cut), (4, 0, target - cut)),
        ),
        (output_rows, output_one, output_two, second[1], second[2]),
        LOW,
    )
    grad_memory = in_order(
        (
            ((0, 0, source),),
            ((1, cut, cut + source),),
            ((2, target - cut, target - cut + source),),
            ((3, 0, source),),
        ),
        (grad_mem_pieces[0], *second[1:]),
        FULL,
    )
    grad_input = in_order(
        tuple(((2 * k, 0, half), (2 * k + 1, 0, half)) for k in members[:3]),
        (low, high, low_one, high_one, low_two, high_two),
        FULL,
        micros=100,
    )
    grad_input = in_order(
        (((0, 0, half), (1, 0, half)),),
        (low_three, high_three),
        FULL,
        (output, grad_memory),
        first=3,
        into=grad_input,
    )
    return (
        output[None],
        grad_input[None],
        grad_memory[None],
        grad_down,
        grad_up,
        grad_prefix,
        *updated,
        *prefix_new,
        new_down_mom,
        new_down_outer,
        new_up_mom,
        new_up_outer,
        *prefix_results,
    )


def solution(mesh):
    placed = (
        P("grp", None, None, None),
        P("grp", None, "mem", None),
        P("grp", None, None, None),
        P("grp", None),
        P("grp", None),
        P(),
        P(),
        P(),
        P(),
        P(),
        P(),
        P(),
        P(),
        P("grp", "mem", None),
        P("grp", "mem", None),
        P("grp", None, None, "mem"),
        P("grp", "mem", None),
        P("grp", "mem", None),
        P("grp", "mem", None),
        P("grp", "mem", None),
        P("grp", None, None, "mem"),
        P("grp", None, None, "mem"),
        P("mem", None),
        P("mem", None),
        P(None, None, "mem"),
        P("mem", None),
        P("mem", None),
        P(None, None, "mem"),
    )
    return jax.shard_map(
        local,
        mesh=mesh,
        in_specs=placed,
        out_specs=(
            P("grp", None, None, None),
            P("grp", None, None, None),
            P("grp", None, "mem", None),
            P("grp", "mem", None),
            P("grp", "mem", None),
            P("grp", None, None, "mem"),
            P("grp", "mem", None),
            P("grp", "mem", None),
            P("grp", "mem", None),
            P("grp", "mem", None),
            P("grp", "mem", None),
            P("grp", "mem", None),
            P("grp", None, None, "mem"),
            P("grp", None, None, "mem"),
            P("grp", None, None, "mem"),
            P("mem", None),
            P("mem", None),
            P("mem", None),
            P("mem", None),
            P(None, None, "mem"),
            P(None, None, "mem"),
        ),
        check_vma=False,
    )
```

```python
import functools

import jax
import jax.numpy as jnp
from jax import lax
from jax.experimental import pallas as pl
from jax.experimental.pallas import tpu as pltpu
from jax.sharding import PartitionSpec as P

HDIM = 64
STEP = 10


EPSILON = 1e-05
NEGATIVE = -1e30
ADAPTER_SCALE = 4.0
OUTER_MOMENTUM = 0.9
OUTER_RATE = 0.7
LANES = 128
FFN_BLOCK = 1024
RESIDENT_POSITIONS = 1024
SMALL_LIMIT = 6 * 1024 * 1024
VMEM_LIMIT = 10 * 1024 * 1024
LOW = jnp.bfloat16
FULL = jnp.float32


def normalize(values_in, gain_row, bias_row):
    centered = values_in - jnp.mean(values_in, -1, keepdims=True)
    scale_inv = lax.rsqrt(jnp.mean(centered * centered, -1, keepdims=True) + EPSILON)
    normal = centered * scale_inv
    return (normal * gain_row + bias_row, normal, scale_inv)


def normalize_back(gradient, normal, scale_inv, gain_row):
    scaled = gradient * gain_row
    return scale_inv * (
        scaled
        - jnp.mean(scaled, -1, keepdims=True)
        - normal * jnp.mean(scaled * normal, -1, keepdims=True)
    )


def dot_nn(left, right):
    return lax.dot_general(left, right, (((1,), (0,)), ((), ())), preferred_element_type=FULL)


def dot_nt(left, right):
    return lax.dot_general(left, right, (((1,), (1,)), ((), ())), preferred_element_type=FULL)


def dot_tn(left, right):
    return lax.dot_general(left, right, (((0,), (0,)), ((), ())), preferred_element_type=FULL)


def gelu_both(pre_act):
    cdf = 0.5 + 0.5 * lax.erf(pre_act * 0.7071067811865476)
    density = jnp.exp(-0.5 * pre_act * pre_act) * 0.3989422804014327
    return pre_act * cdf, cdf + pre_act * density


def first_lanes(shape):
    return lax.broadcasted_iota(jnp.int32, shape, 1) < HDIM


def stack_heads(pair):
    first = first_lanes(pair.shape)
    none = jnp.zeros_like(pair)
    return jnp.concatenate([jnp.where(first, pair, none), jnp.where(first, none, pair)], axis=0)


def merge_heads(stacked):
    rows = stacked.shape[0] // 2
    return jnp.where(first_lanes((rows, LANES)), stacked[:rows], stacked[rows:])


def scaled(queries):
    return queries * jnp.asarray(HDIM ** (-0.5), LOW)


def attend(stacked, keys, values, masked):
    scores = dot_nt(stacked, keys) + masked
    top = jnp.max(scores, -1, keepdims=True)
    expo = jnp.exp(scores - top).astype(LOW)
    both = dot_nn(expo, jnp.concatenate([values, jnp.ones_like(values)], axis=1))
    total = both[:, LANES:]
    return both[:, :LANES] / total, top + jnp.log(total[:, :1])


def attend_back(stacked, keys, values, masked, log_total, grad_stacked, delta, skipped=0):
    probs = jnp.exp(dot_nt(stacked, keys) + masked - log_total)
    grad_probs = dot_nt(grad_stacked, values)
    if delta is None:
        delta = jnp.sum(probs * grad_probs, -1, keepdims=True)
    grad_scores = (probs * (grad_probs - delta)).astype(LOW)
    grad_queries = merge_heads(dot_nn(grad_scores, keys)) * (HDIM ** (-0.5))
    grad_keys = dot_tn(grad_scores, stacked)[skipped:]
    grad_values = dot_tn(probs.astype(LOW), grad_stacked)[skipped:]
    return grad_queries.astype(LOW), grad_keys, grad_values


def row_delta(grad_stacked, context):
    both = jnp.concatenate([context, context], axis=0)
    product = (grad_stacked.astype(FULL) * both.astype(FULL)).astype(LOW)
    return dot_nn(product, jnp.ones((LANES, LANES), LOW))


def self_masked(length, target, prefix_pad, prefix_len):
    shape = (2 * target, prefix_pad + target)
    row = lax.broadcasted_iota(jnp.int32, shape, 0)
    row = jnp.where(row >= target, row - target, row)
    column = lax.broadcasted_iota(jnp.int32, shape, 1)
    key = column - prefix_pad
    allowed = (column < prefix_len) | (key >= 0) & (key <= row) & (key < length)
    return jnp.where(allowed, 0.0, NEGATIVE)


def cross_masked(length, positions):
    column = lax.broadcasted_iota(jnp.int32, (1, positions), 1)
    return jnp.where(column < length, 0.0, NEGATIVE)


def put_lanes(columns, shape):
    lane = lax.broadcasted_iota(jnp.int32, shape, 1)
    result = jnp.zeros(shape, FULL)
    for j, column in enumerate(columns):
        result = jnp.where(lane == j, column, result)
    return result


def lane_pairs(width):
    return [slice(at, at + LANES) for at in range(0, width, LANES)]


def pair_logs(log_total, j):
    return jnp.concatenate(
        [log_total[:, 2 * j : 2 * j + 1], log_total[:, 2 * j + 1 : 2 * j + 2]], axis=0
    )


def place(members):
    device = lax.axis_index("mem")
    return device, lax.rem(device, members), lax.div(device, members)


def first_kernel(members, memory, down_w, up_w, outward, *refs):
    blocks, (block, down, up, sems) = refs[: members - 1], refs[members - 1 :]
    unused, seq, unused = place(members)
    moves = [
        pltpu.make_async_copy(memory.at[0, seq], block, sems.at[0]),
        pltpu.make_async_copy(down_w.at[0], down, sems.at[1]),
        pltpu.make_async_copy(up_w.at[0], up, sems.at[2]),
    ]
    for k, partner in enumerate(blocks):
        moves.append(pltpu.make_async_copy(memory.at[0, seq ^ (k + 1)], partner, sems.at[3 + k]))
    for move in moves:
        move.start()
    for move in moves:
        move.wait()
    source = block.shape[0]
    half = up.shape[0]
    wide = down.shape[1]
    outward[:source, :] = block[...]
    outward[source : source + half, :wide] = down[:half, :].astype(LOW)
    outward[source : source + half, wide:] = down[half:, :].astype(LOW)
    outward[source + half :, :] = up[...].astype(LOW)


def append_kernel(count, rows, *refs):
    for block, message in zip(refs[:count], refs[count:]):
        at = block.shape[0]
        message[:at, :] = block[...]
        message[at:, :] = rows[...]


def join_kernel(windows, *refs):
    at = 0
    for piece, (start, stop) in zip(refs, windows):
        refs[-1][at : at + stop - start, :] = piece[start:stop, :]
        at += stop - start


def self_forward_kernel(members, prefix_len, offsets, lengths, tokens_all, *refs):
    pieces, (self_qkv, self_out) = refs[:members], refs[members : members + 2]
    refs = refs[members + 2 :]
    count = (len(refs) - 10) // 2
    sources, refs = refs[:count], refs[count:]
    prefix, qkv, log_total, summed, context_all = refs[:5]
    kept = refs[5 : 5 + count]
    tokens, ordered, qkv_w, out_w, sems = refs[5 + count :]
    device, seq, unused = place(members)
    moves = [pltpu.make_async_copy(tokens_all.at[0, seq], tokens, sems.at[0])]
    for j in range(3):
        moves.append(pltpu.make_async_copy(self_qkv.at[j], qkv_w.at[j], sems.at[1 + j]))
    moves.append(pltpu.make_async_copy(self_out, out_w, sems.at[4]))
    for j in range(count):
        moves.append(pltpu.make_async_copy(sources[j], kept[j], sems.at[5 + j]))
    for move in moves:
        move.start()
    share = ordered.shape[3]
    size = ordered.shape[0]
    for k, piece in enumerate(pieces):
        rows = piece[piece.shape[0] - 16 :, :]
        for i, offset in enumerate(offsets):
            for j in range(4):
                at = (4 * i + j) * share
                ordered[device ^ offset ^ k, j // 2, 16 * (j % 2) : 16 * (j % 2) + 16, :] = rows[
                    :, at : at + share
                ]
    for j in range(size):
        for c in range(2):
            prefix[c, :, j * share : (j + 1) * share] = ordered[j, c]
    moves[0].wait()
    rows = tokens[...]
    target, width = rows.shape
    for j in range(3):
        moves[1 + j].wait()
        qkv[j] = dot_nn(rows, qkv_w[j]).astype(LOW)
    masked = self_masked(lengths[0, seq], target, prefix.shape[1], prefix_len)
    logs = []
    for part in lane_pairs(width):
        keys = jnp.concatenate([prefix[0, :, part], qkv[1, :, part]], axis=0)
        values = jnp.concatenate([prefix[1, :, part], qkv[2, :, part]], axis=0)
        context, log = attend(stack_heads(scaled(qkv[0, :, part])), keys, values, masked)
        context_all[:, part] = merge_heads(context).astype(LOW)
        logs += [log[:target], log[target:]]
    log_total[...] = put_lanes(logs, log_total.shape)
    moves[4].wait()
    summed[...] = rows.astype(FULL) + dot_nn(context_all[...], out_w[...])
    for move in moves[5:]:
        move.wait()


def project_memory(blocks, parts, rows, qkv_w, keys_values, source):
    device = lax.axis_index("mem")
    for i, (unused, index, start) in enumerate(parts):
        rows[i * source : (i + 1) * source, :] = blocks[index][start : start + source, :]
    for j in range(2):
        projected = dot_nn(rows[...], qkv_w[1 + j]).astype(LOW)
        for i, (offset, unused, unused) in enumerate(parts):
            at = pl.multiple_of((device ^ offset) * source, source)
            keys_values[j, pl.ds(at, source), :] = projected[i * source : (i + 1) * source]


def cross_start_kernel(parts, summed_one, gains, biases, qkv_w, *refs):
    blocks, (queries, keys_values, rows) = refs[:-3], refs[-3:]
    hidden = normalize(summed_one[...], gains[0:1], biases[0:1])[0]
    queries[...] = dot_nn(hidden.astype(LOW), qkv_w[0]).astype(LOW)
    project_memory(blocks, parts, rows, qkv_w, keys_values, rows.shape[0] // len(parts))


def cross_forward_kernel(
    members, parts, lengths, summed_one, gains, biases, qkv_w, out_w, queries, *refs
):
    blocks = refs[:-5]
    keys_values, log_total, summed_two, rows = refs[-4:]
    unused, seq, unused = place(members)
    target, width = queries.shape
    project_memory(blocks, parts, rows, qkv_w, keys_values, rows.shape[0] // len(parts))
    hidden = normalize(summed_one[...], gains[0:1], biases[0:1])[0]
    masked = cross_masked(lengths[0, seq], keys_values.shape[1])
    contexts, logs = [], []
    for part in lane_pairs(width):
        context, log = attend(
            stack_heads(scaled(queries[:, part])),
            keys_values[0, :, part],
            keys_values[1, :, part],
            masked,
        )
        contexts.append(merge_heads(context).astype(LOW))
        logs += [log[:target], log[target:]]
    log_total[...] = put_lanes(logs, log_total.shape)
    summed_two[...] = hidden + dot_nn(jnp.concatenate(contexts, axis=1), out_w[...])


def ffn_forward_kernel(summed_two, gains, biases, in_w, out_w, normed, slope, partial):
    hidden = normalize(summed_two[...], gains[1:2], biases[1:2])[0]
    low = hidden.astype(LOW)
    normed[...] = low
    inner = in_w.shape[1]
    parts = [slice(at, at + FFN_BLOCK) for at in range(0, inner, FFN_BLOCK)]
    pre = dot_nn(low, in_w[:, parts[0]])
    total = hidden
    for j, part in enumerate(parts):
        following = dot_nn(low, in_w[:, parts[j + 1]]) if j + 1 < len(parts) else None
        act, slope_full = gelu_both(pre)
        slope[:, part] = slope_full.astype(LOW)
        total = total + dot_nn(act.astype(LOW), out_w[part, :])
        pre = following
    partial[...] = total


def adapter_kernel(
    places, lengths, partial, normed, gains, biases, cotangent_all, *refs
):
    count = 1 + max(index for index, unused in places)
    shares, refs = refs[:count], refs[count:]
    output, grad_ffn, grad_hidden, act_low, grad_pre_low, grad_low, down, up, cotangent, sem = refs
    device, seq, unused = place(lengths.shape[1])
    move = pltpu.make_async_copy(cotangent_all.at[0, seq], cotangent, sem)
    move.start()
    rows = down.shape[0] // len(places)
    half = rows // 2
    wide = down.shape[1]
    for k, (index, start) in enumerate(places):
        owner, share = device ^ k, shares[index]
        at = pl.multiple_of(owner * rows, rows)
        down[pl.ds(at, half), :] = share[start : start + half, :wide]
        down[pl.ds(at + half, half), :] = share[start : start + half, wide:]
        at = pl.multiple_of(owner * half, half)
        up[pl.ds(at, half), :] = share[start + half : start + rows, :]
    act, slope = gelu_both(dot_nn(normed[...], down[...]))
    act_low[...] = act.astype(LOW)
    total = partial[...] + ADAPTER_SCALE * dot_nn(act_low[...], up[...])
    rows_out, normal, inverse = normalize(total, gains[2:3], biases[2:3])
    output[...] = rows_out.astype(LOW)
    live = lax.broadcasted_iota(jnp.int32, (total.shape[0], 1), 0) < lengths[0, seq]
    move.wait()
    grad_three = normalize_back(
        jnp.where(live, cotangent[...].astype(FULL), 0.0), normal, inverse, gains[2:3]
    )
    grad_ffn[...] = grad_three.astype(LOW)
    grad_low[...] = (ADAPTER_SCALE * grad_three).astype(LOW)
    grad_pre = (dot_nt(grad_low[...], up[...]) * slope).astype(LOW)
    grad_pre_low[...] = grad_pre
    grad_hidden[...] = grad_three + dot_nt(grad_pre, down[...])


def adapter_gradient_kernel(members, normed, act, grad_pre, grad_adapted, *refs):
    grad_pieces, (grad_down, grad_up) = refs[:members], refs[members:]
    unused, seq, replica = place(members)
    grad_down[...] = dot_tn(normed[...], grad_pre[...]).astype(LOW)
    grad_up[...] = dot_tn(act[...], grad_adapted[...]).astype(LOW)
    rows = grad_pieces[0].shape[0]
    half = rows // 2
    wide = grad_down.shape[1]
    for k, piece in enumerate(grad_pieces):
        owner = replica * members + (seq ^ k)
        at = pl.multiple_of(owner * rows, rows)
        piece[:half, :wide] = grad_down[pl.ds(at, half), :]
        piece[:half, wide:] = grad_down[pl.ds(at + half, half), :]
        piece[half:, :] = grad_up[pl.ds(pl.multiple_of(owner * half, half), half), :]


def ffn_backward_kernel(
    grad_ffn, grad_hidden, summed_two, gains, biases, in_w, out_w, slope, grad_two
):
    low = grad_ffn[...]
    inner = in_w.shape[1]
    parts = [slice(at, at + FFN_BLOCK) for at in range(0, inner, FFN_BLOCK)]
    grad_act = dot_nt(low, out_w[parts[0], :])
    total = grad_hidden[...]
    for j, part in enumerate(parts):
        following = dot_nt(low, out_w[parts[j + 1], :]) if j + 1 < len(parts) else None
        grad_pre = (grad_act * slope[:, part].astype(FULL)).astype(LOW)
        total = total + dot_nt(grad_pre, in_w[:, part])
        grad_act = following
    unused, normal, inverse = normalize(summed_two[...], gains[1:2], biases[1:2])
    grad_two[...] = normalize_back(total, normal, inverse, gains[1:2])


def cross_backward_kernel(
    members,
    lengths,
    grad_two,
    summed_one,
    gains,
    biases,
    qkv_w,
    out_w,
    queries,
    keys_values,
    log_total,
    later_source,
    grad_one,
    later,
    *refs,
):
    grad_pieces = refs[:members]
    grad_keys, grad_values, grad_rows, sem = refs[members:]
    unused, seq, replica = place(members)
    target, width = queries.shape
    fetch = pltpu.make_async_copy(later_source, later, sem)
    fetch.start()
    grad_context = dot_nt(grad_two[...].astype(LOW), out_w[...]).astype(LOW)
    masked = cross_masked(lengths[0, seq], keys_values.shape[1])
    grad_queries = []
    for j, part in enumerate(lane_pairs(width)):
        into_queries, into_keys, into_values = attend_back(
            stack_heads(scaled(queries[:, part])),
            keys_values[0, :, part],
            keys_values[1, :, part],
            masked,
            pair_logs(log_total, j),
            stack_heads(grad_context[:, part]),
            None,
        )
        grad_queries.append(into_queries)
        grad_keys[:, part] = into_keys.astype(LOW)
        grad_values[:, part] = into_values.astype(LOW)
    rows = grad_rows.shape[0]
    mine = pl.ds(pl.multiple_of(replica * rows, rows), rows)
    grad_rows[...] = (
        dot_nt(grad_keys[mine, :], qkv_w[1]) + dot_nt(grad_values[mine, :], qkv_w[2])
    ).astype(LOW)
    source = rows // members
    for k, piece in enumerate(grad_pieces):
        piece[...] = grad_rows[pl.ds(pl.multiple_of((seq ^ k) * source, source), source), :]
    total = grad_two[...] + dot_nt(jnp.concatenate(grad_queries, axis=1), qkv_w[0])
    unused, normal, inverse = normalize(summed_one[...], gains[0:1], biases[0:1])
    grad_one[...] = normalize_back(total, normal, inverse, gains[0:1])
    fetch.wait()


def prefix_backward_kernel(
    members,
    prefix_len,
    grad_one,
    prefix,
    out_w,
    qkv,
    context,
    log_total,
    grad_context,
    delta_all,
    *refs,
):
    grad_pieces, (blocks,) = refs[:members], refs[members:]
    unused, seq, replica = place(members)
    target, width = grad_one.shape
    pad = prefix.shape[1]
    grad_context[...] = dot_nt(grad_one[...].astype(LOW), out_w[...]).astype(LOW)
    allowed = lax.broadcasted_iota(jnp.int32, (2 * target, pad), 1) < prefix_len
    size, unused, unused, share = blocks.shape
    grads, deltas = ([], []), []
    for j, part in enumerate(lane_pairs(width)):
        stacked = stack_heads(scaled(qkv[0, :, part]))
        grad_stacked = stack_heads(grad_context[:, part])
        delta = row_delta(grad_stacked, context[:, part])
        deltas += [delta[:target], delta[target:]]
        scores = jnp.where(allowed, dot_nt(stacked, prefix[0, :, part]), NEGATIVE)
        probs = jnp.exp(scores - pair_logs(log_total, j))
        grad_probs = dot_nt(grad_stacked, prefix[1, :, part])
        grad_scores = (probs * (grad_probs - delta[:, :pad])).astype(LOW)
        grads[0].append(dot_tn(grad_scores, stacked).astype(LOW))
        grads[1].append(dot_tn(probs.astype(LOW), grad_stacked).astype(LOW))
    delta_all[...] = put_lanes(deltas, delta_all.shape)
    for c in range(2):
        row = jnp.concatenate(grads[c], axis=1)
        for j in range(size):
            blocks[j, c] = row[:, j * share : (j + 1) * share]
    for k, piece in enumerate(grad_pieces):
        owner = replica * members + (seq ^ k)
        piece[...] = jnp.zeros_like(piece)
        for j in range(4):
            piece[:, j * share : (j + 1) * share] = blocks[
                owner, j // 2, 16 * (j % 2) : 16 * (j % 2) + 16, :
            ]


def self_backward_kernel(
    members,
    prefix_len,
    lengths,
    grad_context,
    delta_all,
    prefix,
    qkv,
    log_total,
    later_source,
    grad_qkv,
    later,
    sem,
):
    unused, seq, unused = place(members)
    fetch = pltpu.make_async_copy(later_source, later, sem)
    fetch.start()
    target, width = grad_context.shape
    pad = prefix.shape[1]
    masked = self_masked(lengths[0, seq], target, pad, prefix_len)
    for j, part in enumerate(lane_pairs(width)):
        into_queries, into_keys, into_values = attend_back(
            stack_heads(scaled(qkv[0, :, part])),
            jnp.concatenate([prefix[0, :, part], qkv[1, :, part]], axis=0),
            jnp.concatenate([prefix[1, :, part], qkv[2, :, part]], axis=0),
            masked,
            pair_logs(log_total, j),
            stack_heads(grad_context[:, part]),
            pair_logs(delta_all, j),
            pad,
        )
        grad_qkv[0, :, part] = into_queries
        grad_qkv[1, :, part] = into_keys.astype(LOW)
        grad_qkv[2, :, part] = into_values.astype(LOW)
    fetch.wait()


def self_project_kernel(grad_one, qkv_w, grad_qkv, low, high):
    total = grad_one[...]
    for j in range(3):
        total = total + dot_nt(grad_qkv[j], qkv_w[j])
    half = low.shape[0]
    low[...] = total[:half].astype(LOW)
    high[...] = total[half:].astype(LOW)


def gather_kernel(members, windows, first, *refs):
    pieces, (result, held, sems) = refs[:-3], refs[-3:]
    unused, seq, unused = place(members)
    moves = []
    for k, parts in enumerate(windows):
        at = 0
        for index, start, stop in parts:
            rows = pieces[index][start:stop, :]
            held[k, at : at + stop - start, :] = rows.astype(held.dtype)
            at += stop - start
        move = pltpu.make_async_copy(held.at[k], result.at[seq ^ (first + k)], sems.at[k])
        move.start()
        moves.append(move)
    for move in moves:
        move.wait()


def adam_update(gradient, first_moment, second_moment, weight, step_rate):
    first_new = 0.9 * first_moment + 0.1 * gradient
    second_new = 0.999 * second_moment + 0.001 * gradient * gradient
    corrected_one = first_new / (1.0 - 0.9**STEP)
    corrected_two = second_new / (1.0 - 0.999**STEP)
    weight_new = weight - step_rate * (
        corrected_one / (jnp.sqrt(corrected_two) + 1e-08) + 0.01 * weight
    )
    return (first_new, second_new, weight_new)


def outer_update(outer_weight, momentum, average):
    momentum_new = OUTER_MOMENTUM * momentum + average
    return momentum_new, outer_weight - OUTER_RATE * (average + OUTER_MOMENTUM * momentum_new)


def prefix_rows_of(packed, share, count):
    parts = [packed[:, j * share : (j + 1) * share] for j in range(4)]
    return [jnp.concatenate(parts[2 * c : 2 * c + 2], axis=0)[:count] for c in range(2)]


def update_kernel(members, starts, *refs):
    pieces, prefix_pieces, refs = (
        refs[:members],
        refs[members : 2 * members],
        refs[2 * members :],
    )
    down_w, down_m, down_v, up_w, up_m, up_v, down_outer, up_outer = refs[:8]
    prefix_w, prefix_m, prefix_v, prefix_outer = refs[8:12]
    grad_down, grad_up, new_down, new_up = refs[12], refs[13], refs[14:17], refs[17:20]
    grad_prefix, new_prefix, difference, padded = refs[20], refs[21:24], refs[24], refs[25]
    total = sum(piece[...].astype(FULL) for piece in pieces)
    rows_all = total.shape[0]
    half = rows_all // 2
    wide = down_w.shape[2]
    for j in range(2):
        rows, part = slice(j * half, (j + 1) * half), slice(j * wide, (j + 1) * wide)
        gradient = total[:half, part]
        grad_down[0, rows, :] = gradient
        new = adam_update(gradient, down_m[0, rows], down_v[0, rows], down_w[0, rows], 0.06)
        for ref, value in zip(new_down, new):
            ref[0, rows, :] = value
        difference[:half, part] = (down_outer[rows, :] - new[2]).astype(LOW)
    gradient = total[half:]
    grad_up[0] = gradient
    new = adam_update(gradient, up_m[0], up_v[0], up_w[0], 0.02)
    for ref, value in zip(new_up, new):
        ref[0] = value
    difference[half:rows_all, :] = (up_outer[...] - new[2]).astype(LOW)
    total = sum(
        piece[start : start + 16, :].astype(FULL) for piece, start in zip(prefix_pieces, starts)
    )
    count, unused, share = prefix_w.shape
    padded[...] = jnp.zeros_like(padded)
    for c, gradient in enumerate(prefix_rows_of(total, share, count)):
        grad_prefix[:, c, :] = gradient
        new = adam_update(gradient, prefix_m[:, c, :], prefix_v[:, c, :], prefix_w[:, c, :], 2.0)
        for ref, value in zip(new_prefix, new):
            ref[:, c, :] = value
        padded[c, :count, :] = prefix_outer[:, c, :] - new[2]
    difference[rows_all:, :] = jnp.zeros_like(difference[rows_all:, :])
    for j in range(4):
        difference[rows_all:, j * share : (j + 1) * share] = padded[
            j // 2, 16 * (j % 2) : 16 * (j % 2) + 16, :
        ].astype(LOW)


def add_kernel(left, right, result):
    result[...] = (left[...].astype(FULL) + right[...].astype(FULL)).astype(LOW)


def outer_kernel(groups, left, right, *refs):
    down_outer, up_outer, prefix_outer, down_mom, up_mom, prefix_mom = refs[:6]
    new_down, new_up, new_prefix, token = refs[6:8], refs[8:10], refs[10:12], refs[12]
    token[...] = jnp.zeros_like(token)
    average = (left[...].astype(FULL) + right[...].astype(FULL)) / groups
    rows_all = average.shape[0] - 16
    half = rows_all // 2
    wide = down_outer.shape[1]
    for j in range(2):
        rows, part = slice(j * half, (j + 1) * half), slice(j * wide, (j + 1) * wide)
        new = outer_update(down_outer[rows, :], down_mom[rows, :], average[:half, part])
        for ref, value in zip(new_down, new):
            ref[rows, :] = value
    new = outer_update(up_outer[...], up_mom[...], average[half:rows_all])
    for ref, value in zip(new_up, new):
        ref[...] = value
    count, unused, share = prefix_outer.shape
    for c, part in enumerate(prefix_rows_of(average[rows_all:], share, count)):
        new = outer_update(prefix_outer[:, c, :], prefix_mom[:, c, :], part)
        for ref, value in zip(new_prefix, new):
            ref[:, c, :] = value


def fixed(shape):
    return pl.BlockSpec(shape, lambda *unused: (0,) * len(shape))


def shaped(shape, dtype):
    return jax.ShapeDtypeStruct(shape, dtype)


def call_whole(
    kernel, spaces, outs, scratch, args, limit=VMEM_LIMIT, out_spaces=None, after=(), micros=0, aliases={}
):
    spaces = list(spaces) + [pltpu.VMEM] * (len(args) - len(spaces)) + [pl.ANY] * len(after)
    if after:
        inner_kernel, count = kernel, len(args)

        def kernel(*refs):
            inner_kernel(*refs[:count], *refs[count + len(after) :])

        args = tuple(args) + tuple(after)
    out_spaces = out_spaces or [pltpu.VMEM] * len(outs)
    return pl.pallas_call(
        kernel,
        in_specs=[pl.BlockSpec(memory_space=space) for space in spaces],
        out_specs=[pl.BlockSpec(memory_space=space) for space in out_spaces],
        out_shape=outs,
        scratch_shapes=scratch,
        input_output_aliases=aliases,
        compiler_params=pltpu.CompilerParams(vmem_limit_bytes=limit),
        cost_estimate=pl.CostEstimate(flops=1000 + int(micros * 1150000000), bytes_accessed=1000, transcendentals=0),
    )(*args)


def local(
    dec_input,
    memory,
    out_grad,
    tgt_lengths,
    src_lengths,
    self_qkv,
    self_out,
    cross_qkv,
    cross_out,
    ffn_in,
    ffn_out,
    norm_gains,
    norm_biases,
    down_w,
    up_w,
    prefix_w,
    down_m,
    down_v,
    up_m,
    up_v,
    prefix_m,
    prefix_v,
    down_outer,
    up_outer,
    prefix_outer,
    down_mom,
    up_mom,
    prefix_mom,
):
    seq_count, target, model_width = dec_input.shape[1:]
    source = memory.shape[2]
    prefix_len = prefix_w.shape[2]
    mem_size = lax.axis_size("mem")
    grp_size = lax.axis_size("grp")
    replicas = mem_size // seq_count
    device = lax.axis_index("mem")
    seq = device % seq_count
    replica = device // seq_count
    adapt = down_w.shape[2]
    inner = ffn_in.shape[1]
    share_rows = down_w.shape[1]
    half_rows = share_rows // 2
    positions = mem_size * source
    resident = positions <= RESIDENT_POSITIONS
    half = target // 2
    cut = target * 96 // 256
    bound = functools.partial

    def swap(values_in, bits):
        return lax.ppermute(values_in, "mem", [(j, j ^ bits) for j in range(mem_size)])

    def join(*parts, after=()):
        rows = sum(stop - start for unused, start, stop in parts)
        (result,) = functools.partial(call_whole, micros=0.4)(
            bound(join_kernel, [(start, stop) for unused, start, stop in parts]),
            [],
            [shaped((rows, model_width), LOW)],
            [],
            tuple(piece for piece, unused, unused in parts),
            SMALL_LIMIT,
            after=after,
        )
        return result

    def in_order(windows, pieces, dtype, after=(), micros=2, first=0, into=None):
        rows = sum(stop - start for unused, start, stop in windows[0])
        shape = (seq_count, rows, model_width)
        pieces = tuple(pieces)
        if into is not None:
            after = (into, *after)
        (result,) = call_whole(
            bound(gather_kernel, seq_count, windows, first),
            [],
            [shaped(shape, dtype)],
            [
                pltpu.VMEM((len(windows), *shape[1:]), dtype),
                pltpu.SemaphoreType.DMA((len(windows),)),
            ],
            pieces,
            SMALL_LIMIT,
            out_spaces=[pl.ANY],
            after=after,
            micros=micros,
            aliases={} if into is None else {len(pieces): 0},
        )
        return result

    members = range(seq_count)
    partners = members[1:]
    replica_bits = [seq_count * 2**j for j in range(replicas.bit_length() - 1)]
    bit = replica_bits[0]
    prefix_rows = 32
    prefix_share = prefix_w.shape[3]
    blocks = jnp.pad(
        prefix_w[0].astype(LOW), ((0, 0), (0, prefix_rows - prefix_len), (0, 0))
    ).reshape(4, 16, prefix_share)
    offsets, prefixes = [0], jnp.concatenate([blocks[j] for j in range(4)], axis=1)
    for step in replica_bits:
        prefixes = jnp.concatenate([prefixes, swap(prefixes, step)], axis=1)
        offsets = offsets + [offset ^ step for offset in offsets]
    outward, *mem_send = functools.partial(call_whole, micros=2)(
        bound(first_kernel, seq_count),
        [pltpu.HBM] * 3,
        [shaped((source + share_rows, model_width), LOW)]
        + [shaped((source, model_width), LOW)] * (seq_count - 1),
        [
            pltpu.VMEM((source, model_width), LOW),
            pltpu.VMEM(down_w.shape[1:], FULL),
            pltpu.VMEM(up_w.shape[1:], FULL),
            pltpu.SemaphoreType.DMA((seq_count + 2,)),
        ],
        tuple(
            pltpu.with_memory_space_constraint(values_in, pltpu.HBM)
            for values_in in (memory, down_w, up_w)
        ),
        SMALL_LIMIT,
    )
    outward_arrived = swap(outward, bit)
    messages = call_whole(
        bound(append_kernel, seq_count - 1),
        [],
        [shaped((source + 16, model_width), LOW)] * (seq_count - 1),
        [],
        (prefixes, *mem_send),
        SMALL_LIMIT,
    )
    arrived = [swap(messages[j - 1], j) for j in partners]
    prefix_pieces = [prefixes, *arrived]
    plane_blocks = join(*[(piece, 0, source) for piece in arrived])
    stop = source + share_rows
    own, plane_blocks = lax.optimization_barrier((outward, plane_blocks))
    shares = {
        0: join((own, source, stop)),
        bit: join((outward_arrived, source, stop)),
    }
    for step in replica_bits[1:]:
        for k, piece in list(shares.items()):
            shares[k ^ step] = swap(piece, step)
    plane_arrived = swap(plane_blocks, bit)
    beside = [swap(share, 2) for share in shares.values()]
    across = [swap(share, 1) for share in shares.values()]
    block_refs = [outward, *arrived, outward_arrived, plane_arrived]
    block_places = {0: (0, 0), bit: (seq_count, 0)}
    for j in partners:
        block_places[j] = (j, 0)
        block_places[j ^ bit] = (seq_count + 1, (j - 1) * source)

    rows_full = shaped((target, model_width), FULL)
    rows_low = shaped((target, model_width), LOW)
    logs = shaped((target, LANES), FULL)
    lengths_space = [pltpu.SMEM]
    dma = pltpu.SemaphoreType.DMA

    weights = (cross_qkv, cross_out, ffn_in, ffn_out) if resident else ()
    prefix, qkv, self_log, summed_one, context, *kept = functools.partial(call_whole, micros=2)(
        bound(self_forward_kernel, seq_count, prefix_len, offsets),
        [pltpu.SMEM, pltpu.HBM] + [pltpu.VMEM] * seq_count + [pltpu.HBM] * (len(weights) + 2),
        [
            shaped((2, prefix_rows, model_width), LOW),
            shaped((3, target, model_width), LOW),
            logs,
            rows_full,
            rows_low,
        ]
        + [pltpu.VMEM(weight.shape, LOW) for weight in weights],
        [
            pltpu.VMEM((target, model_width), LOW),
            pltpu.VMEM((mem_size, 2, prefix_rows, prefix_w.shape[3]), LOW),
            pltpu.VMEM(self_qkv.shape, LOW),
            pltpu.VMEM(self_out.shape, LOW),
            dma((len(weights) + 5,)),
        ],
        (tgt_lengths, dec_input, *prefix_pieces, self_qkv, self_out, *weights),
        after=(plane_blocks, *[shares[k] for k in shares if k]),
        limit=VMEM_LIMIT + 8 * 1024 * 1024,
    )
    if resident:
        cross_qkv, cross_out, ffn_in, ffn_out = kept
    summed_one, block_refs[-1] = lax.optimization_barrier((summed_one, block_refs[-1]))
    for step in replica_bits[1:]:
        known = sorted(block_places)
        joined = jnp.concatenate(
            [
                block_refs[index][start : start + source]
                for index, start in (block_places[k] for k in known)
            ],
            axis=0,
        )
        for i, k in enumerate(known):
            block_places[k ^ step] = (len(block_refs), i * source)
        block_refs.append(swap(joined, step))
    places = [block_places[k] for k in range(mem_size)]
    cross_limit = VMEM_LIMIT if resident else 4 * VMEM_LIMIT
    early = [k for k in range(mem_size) if places[k][0] <= seq_count]
    late = [k for k in range(mem_size) if places[k][0] > seq_count]
    cross_queries, keys_values = functools.partial(call_whole, micros=3)(
        bound(cross_start_kernel, [(k, *places[k]) for k in early]),
        [],
        [rows_low, shaped((2, positions, model_width), LOW)],
        [pltpu.VMEM((len(early) * source, model_width), LOW)],
        (summed_one, norm_gains, norm_biases, cross_qkv, *block_refs[: seq_count + 1]),
    )
    cross_queries, *beside = lax.optimization_barrier((cross_queries, *beside))
    joined = join(*[(share, 0, share_rows) for share in beside])
    far = swap(joined, 1)
    share_refs = [*shares.values(), *beside, *across, far]
    share_places = [None] * mem_size
    for i, offset in enumerate(shares):
        share_places[offset] = (i, 0)
        share_places[offset ^ 2] = (i + replicas, 0)
        share_places[offset ^ 1] = (i + 2 * replicas, 0)
        share_places[offset ^ 3] = (3 * replicas, i * share_rows)
    late_refs = block_refs[seq_count + 1 :]
    late_parts = [(k, places[k][0] - seq_count - 1, places[k][1]) for k in late]
    keys_values, cross_log, summed_two = functools.partial(call_whole, micros=8)(
        bound(cross_forward_kernel, seq_count, late_parts),
        lengths_space,
        [shaped((2, positions, model_width), LOW), logs, rows_full],
        [pltpu.VMEM((len(late) * source, model_width), LOW)],
        (
            src_lengths,
            summed_one,
            norm_gains,
            norm_biases,
            cross_qkv,
            cross_out,
            cross_queries,
            *late_refs,
            keys_values,
        ),
        cross_limit,
        after=(joined,),
        aliases={7 + len(late_refs): 0},
    )
    normed, slope, partial = functools.partial(call_whole, micros=1)(
        ffn_forward_kernel,
        [],
        [rows_low, shaped((target, inner), LOW), rows_full],
        [],
        (summed_two, norm_gains, norm_biases, ffn_in, ffn_out),
    )
    inner_low = shaped((target, adapt), LOW)
    output_rows, grad_ffn, grad_hidden, act, grad_pre, grad_adapted = functools.partial(
        call_whole, micros=3
    )(
        bound(adapter_kernel, share_places),
        [pltpu.SMEM] + [pltpu.VMEM] * 4 + [pltpu.HBM],
        [rows_low, rows_low, rows_full, inner_low, inner_low, rows_low],
        [
            pltpu.VMEM((model_width, adapt), LOW),
            pltpu.VMEM((adapt, model_width), LOW),
            pltpu.VMEM((target, model_width), LOW),
            dma,
        ],
        (tgt_lengths, partial, normed, norm_gains, norm_biases, out_grad, *share_refs),
    )
    output_one, output_two = swap(output_rows, 1), swap(output_rows, 2)
    grad_pieces = functools.partial(call_whole, micros=2)(
        bound(adapter_gradient_kernel, seq_count),
        [],
        [shaped((share_rows, model_width), LOW)] * seq_count,
        [pltpu.VMEM((model_width, adapt), LOW), pltpu.VMEM((adapt, model_width), LOW)],
        (normed, act, grad_pre, grad_adapted),
    )
    grad_pieces = [grad_pieces[0]] + [swap(grad_pieces[j], j) for j in partners]
    (grad_two,) = functools.partial(call_whole, micros=5)(
        ffn_backward_kernel,
        [],
        [rows_full],
        [],
        (grad_ffn, grad_hidden, summed_two, norm_gains, norm_biases, ffn_in, ffn_out, slope),
    )
    plane_rows = seq_count * source
    grad_one, out_later, *grad_mem_pieces = functools.partial(call_whole, micros=11)(
        bound(cross_backward_kernel, seq_count),
        lengths_space + [pltpu.VMEM] * 9 + [pltpu.HBM],
        [rows_full, pltpu.VMEM(self_out.shape, LOW)]
        + [shaped((source, model_width), LOW)] * seq_count,
        [
            pltpu.VMEM((positions, model_width), LOW),
            pltpu.VMEM((positions, model_width), LOW),
            pltpu.VMEM((plane_rows, model_width), LOW),
            dma,
        ],
        (
            src_lengths,
            grad_two,
            summed_one,
            norm_gains,
            norm_biases,
            cross_qkv,
            cross_out,
            cross_queries,
            keys_values,
            cross_log,
            self_out,
        ),
        cross_limit,
    )
    grad_context, delta_all, *prefix_sent = functools.partial(call_whole, micros=3)(
        bound(prefix_backward_kernel, seq_count, prefix_len),
        [],
        [rows_low, logs] + [shaped((16, model_width), LOW)] * seq_count,
        [pltpu.VMEM((mem_size, 2, prefix_rows, prefix_share), LOW)],
        (grad_one, prefix, out_later, qkv, context, self_log),
    )
    grad_context, output_one, output_two = lax.optimization_barrier(
        (grad_context, output_one, output_two)
    )

    def wave(*parts):
        return join(*[part if isinstance(part, tuple) else (part, 0, part.shape[0]) for part in parts])

    second = [
        None,
        swap(wave((output_two, 0, cut), grad_mem_pieces[1], prefix_sent[1]), 1),
        swap(wave((output_one, cut, target), grad_mem_pieces[2], prefix_sent[2]), 2),
        swap(wave(grad_mem_pieces[3], prefix_sent[3]), 3),
    ]
    grad_qkv, qkv_later = functools.partial(call_whole, micros=8)(
        bound(self_backward_kernel, seq_count, prefix_len),
        lengths_space + [pltpu.VMEM] * 5 + [pltpu.HBM],
        [shaped((3, target, model_width), LOW), pltpu.VMEM(self_qkv.shape, LOW)],
        [dma],
        (tgt_lengths, grad_context, delta_all, prefix, qkv, self_log, self_qkv),
        after=tuple(grad_pieces[1:]),
    )
    low, high = functools.partial(call_whole, micros=2)(
        self_project_kernel,
        [],
        [shaped((half, model_width), LOW)] * 2,
        [],
        (grad_one, qkv_later, grad_qkv),
        after=tuple(second[1:]),
    )
    low, high, grad_pieces = lax.optimization_barrier((low, high, grad_pieces))
    low_two, high_one = swap(low, 2), swap(high, 1)
    low_one, high_two = swap(join((low, 0, half)), 1), swap(high, 2)
    low_three, high_three = swap(low_two, 1), swap(high_one, 2)

    def group_swap(values_in, bits):
        return lax.ppermute(values_in, "grp", [(j, j ^ bits) for j in range(grp_size)])

    def flip(values_in):
        return jnp.swapaxes(values_in, -3, -2)

    group_bits = [2**j for j in range(grp_size.bit_length() - 1)][::-1]
    down_shape, up_shape = shaped(down_w.shape, FULL), shaped(up_w.shape, FULL)
    flipped = shaped((prefix_len, 2, prefix_share), FULL)
    results = functools.partial(call_whole, micros=1)(
        bound(update_kernel, seq_count, (0, cut + source, target - cut + source, source)),
        [],
        [down_shape, up_shape]
        + [down_shape] * 3
        + [up_shape] * 3
        + [flipped] * 4
        + [shaped((share_rows + 16, model_width), LOW)],
        [pltpu.VMEM((2, prefix_rows, prefix_share), FULL)],
        (
            *grad_pieces,
            prefix_sent[0],
            *second[1:],
            down_w,
            down_m,
            down_v,
            up_w,
            up_m,
            up_v,
            down_outer,
            up_outer,
            flip(prefix_w[0]),
            flip(prefix_m[0]),
            flip(prefix_v[0]),
            flip(prefix_outer),
        ),
        SMALL_LIMIT,
    )
    (grad_down, grad_up), updated, difference = results[:2], results[2:8], results[12]
    grad_prefix, *prefix_new = [flip(values_in)[None] for values_in in results[8:12]]
    for bits in group_bits[:-1]:
        (difference,) = functools.partial(call_whole, micros=0.4)(
            add_kernel,
            [],
            [shaped(difference.shape, LOW)],
            [],
            (difference, group_swap(difference, bits)),
            SMALL_LIMIT,
        )
    outer_args = (
        difference,
        group_swap(difference, group_bits[-1]),
        down_outer,
        up_outer,
        flip(prefix_outer),
        down_mom,
        up_mom,
        flip(prefix_mom),
    )
    outer_shapes = (
        [shaped(down_outer.shape, FULL)] * 2
        + [shaped(up_outer.shape, FULL)] * 2
        + [flipped] * 2
        + [shaped((8, LANES), FULL)]
    )
    *outer_results, token = pl.pallas_call(
        bound(outer_kernel, grp_size),
        grid=(1,),
        in_specs=[fixed(values_in.shape) for values_in in outer_args],
        out_specs=[fixed(result.shape) for result in outer_shapes],
        out_shape=outer_shapes,
        compiler_params=pltpu.CompilerParams(vmem_limit_bytes=SMALL_LIMIT),
    )(*outer_args)
    new_down_mom, new_down_outer, new_up_mom, new_up_outer, *prefix_results = outer_results
    prefix_results = [flip(values_in) for values_in in prefix_results]
    output = in_order(
        (
            ((0, 0, target),),
            ((1, 0, target),),
            ((2, 0, target),),
            ((3, 0, cut), (4, 0, target - cut)),
        ),
        (output_rows, output_one, output_two, second[1], second[2]),
        LOW,
    )
    grad_memory = in_order(
        (
            ((0, 0, source),),
            ((1, cut, cut + source),),
            ((2, target - cut, target - cut + source),),
            ((3, 0, source),),
        ),
        (grad_mem_pieces[0], *second[1:]),
        FULL,
    )
    grad_input = in_order(
        tuple(((2 * k, 0, half), (2 * k + 1, 0, half)) for k in members[:3]),
        (low, high, low_one, high_one, low_two, high_two),
        FULL,
        micros=100,
    )
    grad_input = in_order(
        (((0, 0, half), (1, 0, half)),),
        (low_three, high_three),
        FULL,
        (output, grad_memory, token),
        first=3,
        into=grad_input,
    )
    return (
        output[None],
        grad_input[None],
        grad_memory[None],
        grad_down,
        grad_up,
        grad_prefix,
        *updated,
        *prefix_new,
        new_down_mom,
        new_down_outer,
        new_up_mom,
        new_up_outer,
        *prefix_results,
    )


def solution(mesh):
    placed = (
        P("grp", None, None, None),
        P("grp", None, "mem", None),
        P("grp", None, None, None),
        P("grp", None),
        P("grp", None),
        P(),
        P(),
        P(),
        P(),
        P(),
        P(),
        P(),
        P(),
        P("grp", "mem", None),
        P("grp", "mem", None),
        P("grp", None, None, "mem"),
        P("grp", "mem", None),
        P("grp", "mem", None),
        P("grp", "mem", None),
        P("grp", "mem", None),
        P("grp", None, None, "mem"),
        P("grp", None, None, "mem"),
        P("mem", None),
        P("mem", None),
        P(None, None, "mem"),
        P("mem", None),
        P("mem", None),
        P(None, None, "mem"),
    )
    return jax.shard_map(
        local,
        mesh=mesh,
        in_specs=placed,
        out_specs=(
            P("grp", None, None, None),
            P("grp", None, None, None),
            P("grp", None, "mem", None),
            P("grp", "mem", None),
            P("grp", "mem", None),
            P("grp", None, None, "mem"),
            P("grp", "mem", None),
            P("grp", "mem", None),
            P("grp", "mem", None),
            P("grp", "mem", None),
            P("grp", "mem", None),
            P("grp", "mem", None),
            P("grp", None, None, "mem"),
            P("grp", None, None, "mem"),
            P("grp", None, None, "mem"),
            P("mem", None),
            P("mem", None),
            P("mem", None),
            P("mem", None),
            P(None, None, "mem"),
            P(None, None, "mem"),
        ),
        check_vma=False,
    )
```

```python
import functools

import jax
import jax.numpy as jnp
from jax import lax
from jax.experimental import pallas as pl
from jax.experimental.pallas import tpu as pltpu
from jax.sharding import PartitionSpec as P

HDIM = 64
STEP = 10


EPSILON = 1e-05
NEGATIVE = -1e30
ADAPTER_SCALE = 4.0
OUTER_MOMENTUM = 0.9
OUTER_RATE = 0.7
LANES = 128
FFN_BLOCK = 1024
RESIDENT_POSITIONS = 1024
SMALL_LIMIT = 6 * 1024 * 1024
VMEM_LIMIT = 10 * 1024 * 1024
LOW = jnp.bfloat16
FULL = jnp.float32


def normalize(values_in, gain_row, bias_row):
    centered = values_in - jnp.mean(values_in, -1, keepdims=True)
    scale_inv = lax.rsqrt(jnp.mean(centered * centered, -1, keepdims=True) + EPSILON)
    normal = centered * scale_inv
    return (normal * gain_row + bias_row, normal, scale_inv)


def normalize_back(gradient, normal, scale_inv, gain_row):
    scaled = gradient * gain_row
    return scale_inv * (
        scaled
        - jnp.mean(scaled, -1, keepdims=True)
        - normal * jnp.mean(scaled * normal, -1, keepdims=True)
    )


def dot_nn(left, right):
    return lax.dot_general(left, right, (((1,), (0,)), ((), ())), preferred_element_type=FULL)


def dot_nt(left, right):
    return lax.dot_general(left, right, (((1,), (1,)), ((), ())), preferred_element_type=FULL)


def dot_tn(left, right):
    return lax.dot_general(left, right, (((0,), (0,)), ((), ())), preferred_element_type=FULL)


def gelu_both(pre_act):
    cdf = 0.5 + 0.5 * lax.erf(pre_act * 0.7071067811865476)
    density = jnp.exp(-0.5 * pre_act * pre_act) * 0.3989422804014327
    return pre_act * cdf, cdf + pre_act * density


def first_lanes(shape):
    return lax.broadcasted_iota(jnp.int32, shape, 1) < HDIM


def stack_heads(pair):
    first = first_lanes(pair.shape)
    none = jnp.zeros_like(pair)
    return jnp.concatenate([jnp.where(first, pair, none), jnp.where(first, none, pair)], axis=0)


def merge_heads(stacked):
    rows = stacked.shape[0] // 2
    return jnp.where(first_lanes((rows, LANES)), stacked[:rows], stacked[rows:])


def scaled(queries):
    return queries * jnp.asarray(HDIM ** (-0.5), LOW)


def attend(stacked, keys, values, masked):
    scores = dot_nt(stacked, keys) + masked
    top = jnp.max(scores, -1, keepdims=True)
    expo = jnp.exp(scores - top).astype(LOW)
    both = dot_nn(expo, jnp.concatenate([values, jnp.ones_like(values)], axis=1))
    total = both[:, LANES:]
    return both[:, :LANES] / total, top + jnp.log(total[:, :1])


def attend_back(stacked, keys, values, masked, log_total, grad_stacked, delta, skipped=0):
    probs = jnp.exp(dot_nt(stacked, keys) + masked - log_total)
    grad_probs = dot_nt(grad_stacked, values)
    if delta is None:
        delta = jnp.sum(probs * grad_probs, -1, keepdims=True)
    grad_scores = (probs * (grad_probs - delta)).astype(LOW)
    grad_queries = merge_heads(dot_nn(grad_scores, keys)) * (HDIM ** (-0.5))
    grad_keys = dot_tn(grad_scores, stacked)[skipped:]
    grad_values = dot_tn(probs.astype(LOW), grad_stacked)[skipped:]
    return grad_queries.astype(LOW), grad_keys, grad_values


def row_delta(grad_stacked, context):
    both = jnp.concatenate([context, context], axis=0)
    product = (grad_stacked.astype(FULL) * both.astype(FULL)).astype(LOW)
    return dot_nn(product, jnp.ones((LANES, LANES), LOW))


def self_masked(length, target, prefix_pad, prefix_len):
    shape = (2 * target, prefix_pad + target)
    row = lax.broadcasted_iota(jnp.int32, shape, 0)
    row = jnp.where(row >= target, row - target, row)
    column = lax.broadcasted_iota(jnp.int32, shape, 1)
    key = column - prefix_pad
    allowed = (column < prefix_len) | (key >= 0) & (key <= row) & (key < length)
    return jnp.where(allowed, 0.0, NEGATIVE)


def cross_masked(length, positions):
    column = lax.broadcasted_iota(jnp.int32, (1, positions), 1)
    return jnp.where(column < length, 0.0, NEGATIVE)


def put_lanes(columns, shape):
    lane = lax.broadcasted_iota(jnp.int32, shape, 1)
    result = jnp.zeros(shape, FULL)
    for j, column in enumerate(columns):
        result = jnp.where(lane == j, column, result)
    return result


def lane_pairs(width):
    return [slice(at, at + LANES) for at in range(0, width, LANES)]


def pair_logs(log_total, j):
    return jnp.concatenate(
        [log_total[:, 2 * j : 2 * j + 1], log_total[:, 2 * j + 1 : 2 * j + 2]], axis=0
    )


def place(members):
    device = lax.axis_index("mem")
    return device, lax.rem(device, members), lax.div(device, members)


def first_kernel(members, memory, down_w, up_w, outward, *refs):
    blocks, (block, down, up, sems) = refs[: members - 1], refs[members - 1 :]
    unused, seq, unused = place(members)
    moves = [
        pltpu.make_async_copy(memory.at[0, seq], block, sems.at[0]),
        pltpu.make_async_copy(down_w.at[0], down, sems.at[1]),
        pltpu.make_async_copy(up_w.at[0], up, sems.at[2]),
    ]
    for k, partner in enumerate(blocks):
        moves.append(pltpu.make_async_copy(memory.at[0, seq ^ (k + 1)], partner, sems.at[3 + k]))
    for move in moves:
        move.start()
    for move in moves:
        move.wait()
    source = block.shape[0]
    half = up.shape[0]
    wide = down.shape[1]
    outward[:source, :] = block[...]
    outward[source : source + half, :wide] = down[:half, :].astype(LOW)
    outward[source : source + half, wide:] = down[half:, :].astype(LOW)
    outward[source + half :, :] = up[...].astype(LOW)


def append_kernel(count, rows, *refs):
    for block, message in zip(refs[:count], refs[count:]):
        at = block.shape[0]
        message[:at, :] = block[...]
        message[at:, :] = rows[...]


def join_kernel(windows, *refs):
    at = 0
    for piece, (start, stop) in zip(refs, windows):
        refs[-1][at : at + stop - start, :] = piece[start:stop, :]
        at += stop - start


def self_forward_kernel(members, prefix_len, offsets, lengths, tokens_all, *refs):
    pieces, (self_qkv, self_out) = refs[:members], refs[members : members + 2]
    refs = refs[members + 2 :]
    count = (len(refs) - 10) // 2
    sources, refs = refs[:count], refs[count:]
    prefix, qkv, log_total, summed, context_all = refs[:5]
    kept = refs[5 : 5 + count]
    tokens, ordered, qkv_w, out_w, sems = refs[5 + count :]
    device, seq, unused = place(members)
    moves = [pltpu.make_async_copy(tokens_all.at[0, seq], tokens, sems.at[0])]
    for j in range(3):
        moves.append(pltpu.make_async_copy(self_qkv.at[j], qkv_w.at[j], sems.at[1 + j]))
    moves.append(pltpu.make_async_copy(self_out, out_w, sems.at[4]))
    for j in range(count):
        moves.append(pltpu.make_async_copy(sources[j], kept[j], sems.at[5 + j]))
    for move in moves:
        move.start()
    share = ordered.shape[3]
    size = ordered.shape[0]
    for k, piece in enumerate(pieces):
        rows = piece[piece.shape[0] - 16 :, :]
        for i, offset in enumerate(offsets):
            for j in range(4):
                at = (4 * i + j) * share
                ordered[device ^ offset ^ k, j // 2, 16 * (j % 2) : 16 * (j % 2) + 16, :] = rows[
                    :, at : at + share
                ]
    for j in range(size):
        for c in range(2):
            prefix[c, :, j * share : (j + 1) * share] = ordered[j, c]
    moves[0].wait()
    rows = tokens[...]
    target, width = rows.shape
    for j in range(3):
        moves[1 + j].wait()
        qkv[j] = dot_nn(rows, qkv_w[j]).astype(LOW)
    masked = self_masked(lengths[0, seq], target, prefix.shape[1], prefix_len)
    logs = []
    for part in lane_pairs(width):
        keys = jnp.concatenate([prefix[0, :, part], qkv[1, :, part]], axis=0)
        values = jnp.concatenate([prefix[1, :, part], qkv[2, :, part]], axis=0)
        context, log = attend(stack_heads(scaled(qkv[0, :, part])), keys, values, masked)
        context_all[:, part] = merge_heads(context).astype(LOW)
        logs += [log[:target], log[target:]]
    log_total[...] = put_lanes(logs, log_total.shape)
    moves[4].wait()
    summed[...] = rows.astype(FULL) + dot_nn(context_all[...], out_w[...])
    for move in moves[5:]:
        move.wait()


def project_memory(blocks, parts, rows, qkv_w, keys_values, source):
    device = lax.axis_index("mem")
    for i, (unused, index, start) in enumerate(parts):
        rows[i * source : (i + 1) * source, :] = blocks[index][start : start + source, :]
    for j in range(2):
        projected = dot_nn(rows[...], qkv_w[1 + j]).astype(LOW)
        for i, (offset, unused, unused) in enumerate(parts):
            at = pl.multiple_of((device ^ offset) * source, source)
            keys_values[j, pl.ds(at, source), :] = projected[i * source : (i + 1) * source]


def cross_start_kernel(parts, summed_one, gains, biases, qkv_w, *refs):
    blocks, (queries, keys_values, rows) = refs[:-3], refs[-3:]
    hidden = normalize(summed_one[...], gains[0:1], biases[0:1])[0]
    queries[...] = dot_nn(hidden.astype(LOW), qkv_w[0]).astype(LOW)
    project_memory(blocks, parts, rows, qkv_w, keys_values, rows.shape[0] // len(parts))


def cross_forward_kernel(
    members, parts, lengths, summed_one, gains, biases, qkv_w, out_w, queries, *refs
):
    blocks = refs[:-5]
    keys_values, log_total, summed_two, rows = refs[-4:]
    unused, seq, unused = place(members)
    target, width = queries.shape
    project_memory(blocks, parts, rows, qkv_w, keys_values, rows.shape[0] // len(parts))
    hidden = normalize(summed_one[...], gains[0:1], biases[0:1])[0]
    masked = cross_masked(lengths[0, seq], keys_values.shape[1])
    contexts, logs = [], []
    for part in lane_pairs(width):
        context, log = attend(
            stack_heads(scaled(queries[:, part])),
            keys_values[0, :, part],
            keys_values[1, :, part],
            masked,
        )
        contexts.append(merge_heads(context).astype(LOW))
        logs += [log[:target], log[target:]]
    log_total[...] = put_lanes(logs, log_total.shape)
    summed_two[...] = hidden + dot_nn(jnp.concatenate(contexts, axis=1), out_w[...])


def ffn_forward_kernel(summed_two, gains, biases, in_w, out_w, normed, slope, partial):
    hidden = normalize(summed_two[...], gains[1:2], biases[1:2])[0]
    low = hidden.astype(LOW)
    normed[...] = low
    inner = in_w.shape[1]
    parts = [slice(at, at + FFN_BLOCK) for at in range(0, inner, FFN_BLOCK)]
    pre = dot_nn(low, in_w[:, parts[0]])
    total = hidden
    for j, part in enumerate(parts):
        following = dot_nn(low, in_w[:, parts[j + 1]]) if j + 1 < len(parts) else None
        act, slope_full = gelu_both(pre)
        slope[:, part] = slope_full.astype(LOW)
        total = total + dot_nn(act.astype(LOW), out_w[part, :])
        pre = following
    partial[...] = total


def adapter_kernel(
    places, lengths, partial, normed, gains, biases, cotangent_all, *refs
):
    count = 1 + max(index for index, unused in places)
    shares, refs = refs[:count], refs[count:]
    output, grad_ffn, grad_hidden, act_low, grad_pre_low, grad_low, down, up, cotangent, sem = refs
    device, seq, unused = place(lengths.shape[1])
    move = pltpu.make_async_copy(cotangent_all.at[0, seq], cotangent, sem)
    move.start()
    rows = down.shape[0] // len(places)
    half = rows // 2
    wide = down.shape[1]
    for k, (index, start) in enumerate(places):
        owner, share = device ^ k, shares[index]
        at = pl.multiple_of(owner * rows, rows)
        down[pl.ds(at, half), :] = share[start : start + half, :wide]
        down[pl.ds(at + half, half), :] = share[start : start + half, wide:]
        at = pl.multiple_of(owner * half, half)
        up[pl.ds(at, half), :] = share[start + half : start + rows, :]
    act, slope = gelu_both(dot_nn(normed[...], down[...]))
    act_low[...] = act.astype(LOW)
    total = partial[...] + ADAPTER_SCALE * dot_nn(act_low[...], up[...])
    rows_out, normal, inverse = normalize(total, gains[2:3], biases[2:3])
    output[...] = rows_out.astype(LOW)
    live = lax.broadcasted_iota(jnp.int32, (total.shape[0], 1), 0) < lengths[0, seq]
    move.wait()
    grad_three = normalize_back(
        jnp.where(live, cotangent[...].astype(FULL), 0.0), normal, inverse, gains[2:3]
    )
    grad_ffn[...] = grad_three.astype(LOW)
    grad_low[...] = (ADAPTER_SCALE * grad_three).astype(LOW)
    grad_pre = (dot_nt(grad_low[...], up[...]) * slope).astype(LOW)
    grad_pre_low[...] = grad_pre
    grad_hidden[...] = grad_three + dot_nt(grad_pre, down[...])


def adapter_gradient_kernel(members, normed, act, grad_pre, grad_adapted, *refs):
    grad_pieces, (grad_down, grad_up) = refs[:members], refs[members:]
    unused, seq, replica = place(members)
    grad_down[...] = dot_tn(normed[...], grad_pre[...]).astype(LOW)
    grad_up[...] = dot_tn(act[...], grad_adapted[...]).astype(LOW)
    rows = grad_pieces[0].shape[0]
    half = rows // 2
    wide = grad_down.shape[1]
    for k, piece in enumerate(grad_pieces):
        owner = replica * members + (seq ^ k)
        at = pl.multiple_of(owner * rows, rows)
        piece[:half, :wide] = grad_down[pl.ds(at, half), :]
        piece[:half, wide:] = grad_down[pl.ds(at + half, half), :]
        piece[half:, :] = grad_up[pl.ds(pl.multiple_of(owner * half, half), half), :]


def ffn_backward_kernel(
    grad_ffn, grad_hidden, summed_two, gains, biases, in_w, out_w, slope, grad_two
):
    low = grad_ffn[...]
    inner = in_w.shape[1]
    parts = [slice(at, at + FFN_BLOCK) for at in range(0, inner, FFN_BLOCK)]
    grad_act = dot_nt(low, out_w[parts[0], :])
    total = grad_hidden[...]
    for j, part in enumerate(parts):
        following = dot_nt(low, out_w[parts[j + 1], :]) if j + 1 < len(parts) else None
        grad_pre = (grad_act * slope[:, part].astype(FULL)).astype(LOW)
        total = total + dot_nt(grad_pre, in_w[:, part])
        grad_act = following
    unused, normal, inverse = normalize(summed_two[...], gains[1:2], biases[1:2])
    grad_two[...] = normalize_back(total, normal, inverse, gains[1:2])


def cross_backward_kernel(
    members,
    lengths,
    grad_two,
    summed_one,
    gains,
    biases,
    qkv_w,
    out_w,
    queries,
    keys_values,
    log_total,
    later_source,
    grad_one,
    later,
    *refs,
):
    grad_pieces = refs[:members]
    grad_keys, grad_values, grad_rows, sem = refs[members:]
    unused, seq, replica = place(members)
    target, width = queries.shape
    fetch = pltpu.make_async_copy(later_source, later, sem)
    fetch.start()
    grad_context = dot_nt(grad_two[...].astype(LOW), out_w[...]).astype(LOW)
    masked = cross_masked(lengths[0, seq], keys_values.shape[1])
    grad_queries = []
    for j, part in enumerate(lane_pairs(width)):
        into_queries, into_keys, into_values = attend_back(
            stack_heads(scaled(queries[:, part])),
            keys_values[0, :, part],
            keys_values[1, :, part],
            masked,
            pair_logs(log_total, j),
            stack_heads(grad_context[:, part]),
            None,
        )
        grad_queries.append(into_queries)
        grad_keys[:, part] = into_keys.astype(LOW)
        grad_values[:, part] = into_values.astype(LOW)
    rows = grad_rows.shape[0]
    mine = pl.ds(pl.multiple_of(replica * rows, rows), rows)
    grad_rows[...] = (
        dot_nt(grad_keys[mine, :], qkv_w[1]) + dot_nt(grad_values[mine, :], qkv_w[2])
    ).astype(LOW)
    source = rows // members
    for k, piece in enumerate(grad_pieces):
        piece[...] = grad_rows[pl.ds(pl.multiple_of((seq ^ k) * source, source), source), :]
    total = grad_two[...] + dot_nt(jnp.concatenate(grad_queries, axis=1), qkv_w[0])
    unused, normal, inverse = normalize(summed_one[...], gains[0:1], biases[0:1])
    grad_one[...] = normalize_back(total, normal, inverse, gains[0:1])
    fetch.wait()


def prefix_backward_kernel(
    members,
    prefix_len,
    grad_one,
    prefix,
    out_w,
    qkv,
    context,
    log_total,
    grad_context,
    delta_all,
    *refs,
):
    grad_pieces, (blocks,) = refs[:members], refs[members:]
    unused, seq, replica = place(members)
    target, width = grad_one.shape
    pad = prefix.shape[1]
    grad_context[...] = dot_nt(grad_one[...].astype(LOW), out_w[...]).astype(LOW)
    allowed = lax.broadcasted_iota(jnp.int32, (2 * target, pad), 1) < prefix_len
    size, unused, unused, share = blocks.shape
    grads, deltas = ([], []), []
    for j, part in enumerate(lane_pairs(width)):
        stacked = stack_heads(scaled(qkv[0, :, part]))
        grad_stacked = stack_heads(grad_context[:, part])
        delta = row_delta(grad_stacked, context[:, part])
        deltas += [delta[:target], delta[target:]]
        scores = jnp.where(allowed, dot_nt(stacked, prefix[0, :, part]), NEGATIVE)
        probs = jnp.exp(scores - pair_logs(log_total, j))
        grad_probs = dot_nt(grad_stacked, prefix[1, :, part])
        grad_scores = (probs * (grad_probs - delta[:, :pad])).astype(LOW)
        grads[0].append(dot_tn(grad_scores, stacked).astype(LOW))
        grads[1].append(dot_tn(probs.astype(LOW), grad_stacked).astype(LOW))
    delta_all[...] = put_lanes(deltas, delta_all.shape)
    for c in range(2):
        row = jnp.concatenate(grads[c], axis=1)
        for j in range(size):
            blocks[j, c] = row[:, j * share : (j + 1) * share]
    for k, piece in enumerate(grad_pieces):
        owner = replica * members + (seq ^ k)
        piece[...] = jnp.zeros_like(piece)
        for j in range(4):
            piece[:, j * share : (j + 1) * share] = blocks[
                owner, j // 2, 16 * (j % 2) : 16 * (j % 2) + 16, :
            ]


def self_backward_kernel(
    members,
    prefix_len,
    lengths,
    grad_context,
    delta_all,
    prefix,
    qkv,
    log_total,
    later_source,
    grad_qkv,
    later,
    sem,
):
    unused, seq, unused = place(members)
    fetch = pltpu.make_async_copy(later_source, later, sem)
    fetch.start()
    target, width = grad_context.shape
    pad = prefix.shape[1]
    masked = self_masked(lengths[0, seq], target, pad, prefix_len)
    for j, part in enumerate(lane_pairs(width)):
        into_queries, into_keys, into_values = attend_back(
            stack_heads(scaled(qkv[0, :, part])),
            jnp.concatenate([prefix[0, :, part], qkv[1, :, part]], axis=0),
            jnp.concatenate([prefix[1, :, part], qkv[2, :, part]], axis=0),
            masked,
            pair_logs(log_total, j),
            stack_heads(grad_context[:, part]),
            pair_logs(delta_all, j),
            pad,
        )
        grad_qkv[0, :, part] = into_queries
        grad_qkv[1, :, part] = into_keys.astype(LOW)
        grad_qkv[2, :, part] = into_values.astype(LOW)
    fetch.wait()


def self_project_kernel(grad_one, qkv_w, grad_qkv, low, high):
    total = grad_one[...]
    for j in range(3):
        total = total + dot_nt(grad_qkv[j], qkv_w[j])
    half = low.shape[0]
    low[...] = total[:half].astype(LOW)
    high[...] = total[half:].astype(LOW)


def gather_kernel(members, windows, first, *refs):
    pieces, (result, held, sems) = refs[:-3], refs[-3:]
    unused, seq, unused = place(members)
    moves = []
    for k, parts in enumerate(windows):
        at = 0
        for index, start, stop in parts:
            rows = pieces[index][start:stop, :]
            held[k, at : at + stop - start, :] = rows.astype(held.dtype)
            at += stop - start
        move = pltpu.make_async_copy(held.at[k], result.at[seq ^ (first + k)], sems.at[k])
        move.start()
        moves.append(move)
    for move in moves:
        move.wait()


def adam_update(gradient, first_moment, second_moment, weight, step_rate):
    first_new = 0.9 * first_moment + 0.1 * gradient
    second_new = 0.999 * second_moment + 0.001 * gradient * gradient
    corrected_one = first_new / (1.0 - 0.9**STEP)
    corrected_two = second_new / (1.0 - 0.999**STEP)
    weight_new = weight - step_rate * (
        corrected_one / (jnp.sqrt(corrected_two) + 1e-08) + 0.01 * weight
    )
    return (first_new, second_new, weight_new)


def outer_update(outer_weight, momentum, average):
    momentum_new = OUTER_MOMENTUM * momentum + average
    return momentum_new, outer_weight - OUTER_RATE * (average + OUTER_MOMENTUM * momentum_new)


def prefix_rows_of(packed, share, count):
    parts = [packed[:, j * share : (j + 1) * share] for j in range(4)]
    return [jnp.concatenate(parts[2 * c : 2 * c + 2], axis=0)[:count] for c in range(2)]


def update_kernel(members, starts, *refs):
    pieces, prefix_pieces, refs = (
        refs[:members],
        refs[members : 2 * members],
        refs[2 * members :],
    )
    down_w, down_m, down_v, up_w, up_m, up_v, down_outer, up_outer = refs[:8]
    prefix_w, prefix_m, prefix_v, prefix_outer = refs[8:12]
    grad_down, grad_up, new_down, new_up = refs[12], refs[13], refs[14:17], refs[17:20]
    grad_prefix, new_prefix, difference, padded = refs[20], refs[21:24], refs[24], refs[25]
    total = sum(piece[...].astype(FULL) for piece in pieces)
    rows_all = total.shape[0]
    half = rows_all // 2
    wide = down_w.shape[2]
    for j in range(2):
        rows, part = slice(j * half, (j + 1) * half), slice(j * wide, (j + 1) * wide)
        gradient = total[:half, part]
        grad_down[0, rows, :] = gradient
        new = adam_update(gradient, down_m[0, rows], down_v[0, rows], down_w[0, rows], 0.06)
        for ref, value in zip(new_down, new):
            ref[0, rows, :] = value
        difference[:half, part] = (down_outer[rows, :] - new[2]).astype(LOW)
    gradient = total[half:]
    grad_up[0] = gradient
    new = adam_update(gradient, up_m[0], up_v[0], up_w[0], 0.02)
    for ref, value in zip(new_up, new):
        ref[0] = value
    difference[half:rows_all, :] = (up_outer[...] - new[2]).astype(LOW)
    total = sum(
        piece[start : start + 16, :].astype(FULL) for piece, start in zip(prefix_pieces, starts)
    )
    count, unused, share = prefix_w.shape
    padded[...] = jnp.zeros_like(padded)
    for c, gradient in enumerate(prefix_rows_of(total, share, count)):
        grad_prefix[:, c, :] = gradient
        new = adam_update(gradient, prefix_m[:, c, :], prefix_v[:, c, :], prefix_w[:, c, :], 2.0)
        for ref, value in zip(new_prefix, new):
            ref[:, c, :] = value
        padded[c, :count, :] = prefix_outer[:, c, :] - new[2]
    difference[rows_all:, :] = jnp.zeros_like(difference[rows_all:, :])
    for j in range(4):
        difference[rows_all:, j * share : (j + 1) * share] = padded[
            j // 2, 16 * (j % 2) : 16 * (j % 2) + 16, :
        ].astype(LOW)


def add_kernel(left, right, result):
    result[...] = (left[...].astype(FULL) + right[...].astype(FULL)).astype(LOW)


def outer_kernel(groups, left, right, *refs):
    down_outer, up_outer, prefix_outer, down_mom, up_mom, prefix_mom = refs[:6]
    new_down, new_up, new_prefix, token = refs[6:8], refs[8:10], refs[10:12], refs[12]
    token[...] = jnp.zeros_like(token)
    average = (left[...].astype(FULL) + right[...].astype(FULL)) / groups
    rows_all = average.shape[0] - 16
    half = rows_all // 2
    wide = down_outer.shape[1]
    for j in range(2):
        rows, part = slice(j * half, (j + 1) * half), slice(j * wide, (j + 1) * wide)
        new = outer_update(down_outer[rows, :], down_mom[rows, :], average[:half, part])
        for ref, value in zip(new_down, new):
            ref[rows, :] = value
    new = outer_update(up_outer[...], up_mom[...], average[half:rows_all])
    for ref, value in zip(new_up, new):
        ref[...] = value
    count, unused, share = prefix_outer.shape
    for c, part in enumerate(prefix_rows_of(average[rows_all:], share, count)):
        new = outer_update(prefix_outer[:, c, :], prefix_mom[:, c, :], part)
        for ref, value in zip(new_prefix, new):
            ref[:, c, :] = value


def fixed(shape):
    return pl.BlockSpec(shape, lambda *unused: (0,) * len(shape))


def shaped(shape, dtype):
    return jax.ShapeDtypeStruct(shape, dtype)


def call_whole(
    kernel, spaces, outs, scratch, args, limit=VMEM_LIMIT, out_spaces=None, after=(), micros=0, aliases={}
):
    spaces = list(spaces) + [pltpu.VMEM] * (len(args) - len(spaces)) + [pl.ANY] * len(after)
    if after:
        inner_kernel, count = kernel, len(args)

        def kernel(*refs):
            inner_kernel(*refs[:count], *refs[count + len(after) :])

        args = tuple(args) + tuple(after)
    out_spaces = out_spaces or [pltpu.VMEM] * len(outs)
    return pl.pallas_call(
        kernel,
        in_specs=[pl.BlockSpec(memory_space=space) for space in spaces],
        out_specs=[pl.BlockSpec(memory_space=space) for space in out_spaces],
        out_shape=outs,
        scratch_shapes=scratch,
        input_output_aliases=aliases,
        compiler_params=pltpu.CompilerParams(vmem_limit_bytes=limit),
        cost_estimate=pl.CostEstimate(flops=1000 + int(micros * 1150000000), bytes_accessed=1000, transcendentals=0),
    )(*args)


def local(
    dec_input,
    memory,
    out_grad,
    tgt_lengths,
    src_lengths,
    self_qkv,
    self_out,
    cross_qkv,
    cross_out,
    ffn_in,
    ffn_out,
    norm_gains,
    norm_biases,
    down_w,
    up_w,
    prefix_w,
    down_m,
    down_v,
    up_m,
    up_v,
    prefix_m,
    prefix_v,
    down_outer,
    up_outer,
    prefix_outer,
    down_mom,
    up_mom,
    prefix_mom,
):
    seq_count, target, model_width = dec_input.shape[1:]
    source = memory.shape[2]
    prefix_len = prefix_w.shape[2]
    mem_size = lax.axis_size("mem")
    grp_size = lax.axis_size("grp")
    replicas = mem_size // seq_count
    device = lax.axis_index("mem")
    seq = device % seq_count
    replica = device // seq_count
    adapt = down_w.shape[2]
    inner = ffn_in.shape[1]
    share_rows = down_w.shape[1]
    half_rows = share_rows // 2
    positions = mem_size * source
    resident = positions <= RESIDENT_POSITIONS
    half = target // 2
    cut = target * 112 // 256
    bound = functools.partial

    def swap(values_in, bits):
        return lax.ppermute(values_in, "mem", [(j, j ^ bits) for j in range(mem_size)])

    def join(*parts, after=()):
        rows = sum(stop - start for unused, start, stop in parts)
        (result,) = functools.partial(call_whole, micros=0.4)(
            bound(join_kernel, [(start, stop) for unused, start, stop in parts]),
            [],
            [shaped((rows, model_width), LOW)],
            [],
            tuple(piece for piece, unused, unused in parts),
            SMALL_LIMIT,
            after=after,
        )
        return result

    def in_order(windows, pieces, dtype, after=(), micros=2, first=0, into=None):
        rows = sum(stop - start for unused, start, stop in windows[0])
        shape = (seq_count, rows, model_width)
        pieces = tuple(pieces)
        if into is not None:
            after = (into, *after)
        (result,) = call_whole(
            bound(gather_kernel, seq_count, windows, first),
            [],
            [shaped(shape, dtype)],
            [
                pltpu.VMEM((len(windows), *shape[1:]), dtype),
                pltpu.SemaphoreType.DMA((len(windows),)),
            ],
            pieces,
            SMALL_LIMIT,
            out_spaces=[pl.ANY],
            after=after,
            micros=micros,
            aliases={} if into is None else {len(pieces): 0},
        )
        return result

    members = range(seq_count)
    partners = members[1:]
    replica_bits = [seq_count * 2**j for j in range(replicas.bit_length() - 1)]
    bit = replica_bits[0]
    prefix_rows = 32
    prefix_share = prefix_w.shape[3]
    blocks = jnp.pad(
        prefix_w[0].astype(LOW), ((0, 0), (0, prefix_rows - prefix_len), (0, 0))
    ).reshape(4, 16, prefix_share)
    offsets, prefixes = [0], jnp.concatenate([blocks[j] for j in range(4)], axis=1)
    for step in replica_bits:
        prefixes = jnp.concatenate([prefixes, swap(prefixes, step)], axis=1)
        offsets = offsets + [offset ^ step for offset in offsets]
    outward, *mem_send = functools.partial(call_whole, micros=2)(
        bound(first_kernel, seq_count),
        [pltpu.HBM] * 3,
        [shaped((source + share_rows, model_width), LOW)]
        + [shaped((source, model_width), LOW)] * (seq_count - 1),
        [
            pltpu.VMEM((source, model_width), LOW),
            pltpu.VMEM(down_w.shape[1:], FULL),
            pltpu.VMEM(up_w.shape[1:], FULL),
            pltpu.SemaphoreType.DMA((seq_count + 2,)),
        ],
        tuple(
            pltpu.with_memory_space_constraint(values_in, pltpu.HBM)
            for values_in in (memory, down_w, up_w)
        ),
        SMALL_LIMIT,
    )
    outward_arrived = swap(outward, bit)
    messages = call_whole(
        bound(append_kernel, seq_count - 1),
        [],
        [shaped((source + 16, model_width), LOW)] * (seq_count - 1),
        [],
        (prefixes, *mem_send),
        SMALL_LIMIT,
    )
    arrived = [swap(messages[j - 1], j) for j in partners]
    prefix_pieces = [prefixes, *arrived]
    plane_blocks = join(*[(piece, 0, source) for piece in arrived])
    stop = source + share_rows
    own, plane_blocks = lax.optimization_barrier((outward, plane_blocks))
    shares = {
        0: join((own, source, stop)),
        bit: join((outward_arrived, source, stop)),
    }
    for step in replica_bits[1:]:
        for k, piece in list(shares.items()):
            shares[k ^ step] = swap(piece, step)
    plane_arrived = swap(plane_blocks, bit)
    beside = [swap(share, 2) for share in shares.values()]
    across = [swap(share, 1) for share in shares.values()]
    block_refs = [outward, *arrived, outward_arrived, plane_arrived]
    block_places = {0: (0, 0), bit: (seq_count, 0)}
    for j in partners:
        block_places[j] = (j, 0)
        block_places[j ^ bit] = (seq_count + 1, (j - 1) * source)

    rows_full = shaped((target, model_width), FULL)
    rows_low = shaped((target, model_width), LOW)
    logs = shaped((target, LANES), FULL)
    lengths_space = [pltpu.SMEM]
    dma = pltpu.SemaphoreType.DMA

    weights = (cross_qkv, cross_out, ffn_in, ffn_out) if resident else ()
    prefix, qkv, self_log, summed_one, context, *kept = functools.partial(call_whole, micros=2)(
        bound(self_forward_kernel, seq_count, prefix_len, offsets),
        [pltpu.SMEM, pltpu.HBM] + [pltpu.VMEM] * seq_count + [pltpu.HBM] * (len(weights) + 2),
        [
            shaped((2, prefix_rows, model_width), LOW),
            shaped((3, target, model_width), LOW),
            logs,
            rows_full,
            rows_low,
        ]
        + [pltpu.VMEM(weight.shape, LOW) for weight in weights],
        [
            pltpu.VMEM((target, model_width), LOW),
            pltpu.VMEM((mem_size, 2, prefix_rows, prefix_w.shape[3]), LOW),
            pltpu.VMEM(self_qkv.shape, LOW),
            pltpu.VMEM(self_out.shape, LOW),
            dma((len(weights) + 5,)),
        ],
        (tgt_lengths, dec_input, *prefix_pieces, self_qkv, self_out, *weights),
        after=(plane_blocks, *[shares[k] for k in shares if k]),
        limit=VMEM_LIMIT + 8 * 1024 * 1024,
    )
    if resident:
        cross_qkv, cross_out, ffn_in, ffn_out = kept
    summed_one, block_refs[-1] = lax.optimization_barrier((summed_one, block_refs[-1]))
    for step in replica_bits[1:]:
        known = sorted(block_places)
        joined = jnp.concatenate(
            [
                block_refs[index][start : start + source]
                for index, start in (block_places[k] for k in known)
            ],
            axis=0,
        )
        for i, k in enumerate(known):
            block_places[k ^ step] = (len(block_refs), i * source)
        block_refs.append(swap(joined, step))
    places = [block_places[k] for k in range(mem_size)]
    cross_limit = VMEM_LIMIT if resident else 4 * VMEM_LIMIT
    early = [k for k in range(mem_size) if places[k][0] <= seq_count]
    late = [k for k in range(mem_size) if places[k][0] > seq_count]
    cross_queries, keys_values = functools.partial(call_whole, micros=3)(
        bound(cross_start_kernel, [(k, *places[k]) for k in early]),
        [],
        [rows_low, shaped((2, positions, model_width), LOW)],
        [pltpu.VMEM((len(early) * source, model_width), LOW)],
        (summed_one, norm_gains, norm_biases, cross_qkv, *block_refs[: seq_count + 1]),
    )
    cross_queries, *beside = lax.optimization_barrier((cross_queries, *beside))
    joined = join(*[(share, 0, share_rows) for share in beside])
    far = swap(joined, 1)
    share_refs = [*shares.values(), *beside, *across, far]
    share_places = [None] * mem_size
    for i, offset in enumerate(shares):
        share_places[offset] = (i, 0)
        share_places[offset ^ 2] = (i + replicas, 0)
        share_places[offset ^ 1] = (i + 2 * replicas, 0)
        share_places[offset ^ 3] = (3 * replicas, i * share_rows)
    late_refs = block_refs[seq_count + 1 :]
    late_parts = [(k, places[k][0] - seq_count - 1, places[k][1]) for k in late]
    keys_values, cross_log, summed_two = functools.partial(call_whole, micros=8)(
        bound(cross_forward_kernel, seq_count, late_parts),
        lengths_space,
        [shaped((2, positions, model_width), LOW), logs, rows_full],
        [pltpu.VMEM((len(late) * source, model_width), LOW)],
        (
            src_lengths,
            summed_one,
            norm_gains,
            norm_biases,
            cross_qkv,
            cross_out,
            cross_queries,
            *late_refs,
            keys_values,
        ),
        cross_limit,
        after=(joined,),
        aliases={7 + len(late_refs): 0},
    )
    normed, slope, partial = functools.partial(call_whole, micros=1)(
        ffn_forward_kernel,
        [],
        [rows_low, shaped((target, inner), LOW), rows_full],
        [],
        (summed_two, norm_gains, norm_biases, ffn_in, ffn_out),
    )
    inner_low = shaped((target, adapt), LOW)
    output_rows, grad_ffn, grad_hidden, act, grad_pre, grad_adapted = functools.partial(
        call_whole, micros=3
    )(
        bound(adapter_kernel, share_places),
        [pltpu.SMEM] + [pltpu.VMEM] * 4 + [pltpu.HBM],
        [rows_low, rows_low, rows_full, inner_low, inner_low, rows_low],
        [
            pltpu.VMEM((model_width, adapt), LOW),
            pltpu.VMEM((adapt, model_width), LOW),
            pltpu.VMEM((target, model_width), LOW),
            dma,
        ],
        (tgt_lengths, partial, normed, norm_gains, norm_biases, out_grad, *share_refs),
    )
    output_one, output_two = swap(output_rows, 1), swap(output_rows, 2)
    grad_pieces = functools.partial(call_whole, micros=2)(
        bound(adapter_gradient_kernel, seq_count),
        [],
        [shaped((share_rows, model_width), LOW)] * seq_count,
        [pltpu.VMEM((model_width, adapt), LOW), pltpu.VMEM((adapt, model_width), LOW)],
        (normed, act, grad_pre, grad_adapted),
    )
    grad_pieces = [grad_pieces[0]] + [swap(grad_pieces[j], j) for j in partners]
    (grad_two,) = functools.partial(call_whole, micros=5)(
        ffn_backward_kernel,
        [],
        [rows_full],
        [],
        (grad_ffn, grad_hidden, summed_two, norm_gains, norm_biases, ffn_in, ffn_out, slope),
    )
    plane_rows = seq_count * source
    grad_one, out_later, *grad_mem_pieces = functools.partial(call_whole, micros=11)(
        bound(cross_backward_kernel, seq_count),
        lengths_space + [pltpu.VMEM] * 9 + [pltpu.HBM],
        [rows_full, pltpu.VMEM(self_out.shape, LOW)]
        + [shaped((source, model_width), LOW)] * seq_count,
        [
            pltpu.VMEM((positions, model_width), LOW),
            pltpu.VMEM((positions, model_width), LOW),
            pltpu.VMEM((plane_rows, model_width), LOW),
            dma,
        ],
        (
            src_lengths,
            grad_two,
            summed_one,
            norm_gains,
            norm_biases,
            cross_qkv,
            cross_out,
            cross_queries,
            keys_values,
            cross_log,
            self_out,
        ),
        cross_limit,
    )
    grad_context, delta_all, *prefix_sent = functools.partial(call_whole, micros=3)(
        bound(prefix_backward_kernel, seq_count, prefix_len),
        [],
        [rows_low, logs] + [shaped((16, model_width), LOW)] * seq_count,
        [pltpu.VMEM((mem_size, 2, prefix_rows, prefix_share), LOW)],
        (grad_one, prefix, out_later, qkv, context, self_log),
    )
    grad_context, output_one, output_two = lax.optimization_barrier(
        (grad_context, output_one, output_two)
    )

    def wave(*parts):
        return join(*[part if isinstance(part, tuple) else (part, 0, part.shape[0]) for part in parts])

    second = [
        None,
        swap(wave((output_two, 0, cut), grad_mem_pieces[1], prefix_sent[1]), 1),
        swap(wave((output_one, cut, target), grad_mem_pieces[2], prefix_sent[2]), 2),
        swap(wave(grad_mem_pieces[3], prefix_sent[3]), 3),
    ]
    grad_qkv, qkv_later = functools.partial(call_whole, micros=8)(
        bound(self_backward_kernel, seq_count, prefix_len),
        lengths_space + [pltpu.VMEM] * 5 + [pltpu.HBM],
        [shaped((3, target, model_width), LOW), pltpu.VMEM(self_qkv.shape, LOW)],
        [dma],
        (tgt_lengths, grad_context, delta_all, prefix, qkv, self_log, self_qkv),
        after=tuple(grad_pieces[1:]),
    )
    low, high = functools.partial(call_whole, micros=2)(
        self_project_kernel,
        [],
        [shaped((half, model_width), LOW)] * 2,
        [],
        (grad_one, qkv_later, grad_qkv),
        after=tuple(second[1:]),
    )
    low, high, grad_pieces = lax.optimization_barrier((low, high, grad_pieces))
    low_two, high_one = swap(low, 2), swap(high, 1)
    low_one, high_two = swap(join((low, 0, half)), 1), swap(high, 2)
    low_three, high_three = swap(low_two, 1), swap(high_one, 2)

    def group_swap(values_in, bits):
        return lax.ppermute(values_in, "grp", [(j, j ^ bits) for j in range(grp_size)])

    def flip(values_in):
        return jnp.swapaxes(values_in, -3, -2)

    group_bits = [2**j for j in range(grp_size.bit_length() - 1)][::-1]
    down_shape, up_shape = shaped(down_w.shape, FULL), shaped(up_w.shape, FULL)
    flipped = shaped((prefix_len, 2, prefix_share), FULL)
    results = functools.partial(call_whole, micros=1)(
        bound(update_kernel, seq_count, (0, cut + source, target - cut + source, source)),
        [],
        [down_shape, up_shape]
        + [down_shape] * 3
        + [up_shape] * 3
        + [flipped] * 4
        + [shaped((share_rows + 16, model_width), LOW)],
        [pltpu.VMEM((2, prefix_rows, prefix_share), FULL)],
        (
            *grad_pieces,
            prefix_sent[0],
            *second[1:],
            down_w,
            down_m,
            down_v,
            up_w,
            up_m,
            up_v,
            down_outer,
            up_outer,
            flip(prefix_w[0]),
            flip(prefix_m[0]),
            flip(prefix_v[0]),
            flip(prefix_outer),
        ),
        SMALL_LIMIT,
    )
    (grad_down, grad_up), updated, difference = results[:2], results[2:8], results[12]
    grad_prefix, *prefix_new = [flip(values_in)[None] for values_in in results[8:12]]
    for bits in group_bits[:-1]:
        (difference,) = functools.partial(call_whole, micros=0.4)(
            add_kernel,
            [],
            [shaped(difference.shape, LOW)],
            [],
            (difference, group_swap(difference, bits)),
            SMALL_LIMIT,
        )
    outer_args = (
        difference,
        group_swap(difference, group_bits[-1]),
        down_outer,
        up_outer,
        flip(prefix_outer),
        down_mom,
        up_mom,
        flip(prefix_mom),
    )
    outer_shapes = (
        [shaped(down_outer.shape, FULL)] * 2
        + [shaped(up_outer.shape, FULL)] * 2
        + [flipped] * 2
        + [shaped((8, LANES), FULL)]
    )
    *outer_results, token = pl.pallas_call(
        bound(outer_kernel, grp_size),
        grid=(1,),
        in_specs=[fixed(values_in.shape) for values_in in outer_args],
        out_specs=[fixed(result.shape) for result in outer_shapes],
        out_shape=outer_shapes,
        compiler_params=pltpu.CompilerParams(vmem_limit_bytes=SMALL_LIMIT),
    )(*outer_args)
    new_down_mom, new_down_outer, new_up_mom, new_up_outer, *prefix_results = outer_results
    prefix_results = [flip(values_in) for values_in in prefix_results]
    output = in_order(
        (
            ((0, 0, target),),
            ((1, 0, target),),
            ((2, 0, target),),
            ((3, 0, cut), (4, 0, target - cut)),
        ),
        (output_rows, output_one, output_two, second[1], second[2]),
        LOW,
    )
    grad_memory = in_order(
        (
            ((0, 0, source),),
            ((1, cut, cut + source),),
            ((2, target - cut, target - cut + source),),
            ((3, 0, source),),
        ),
        (grad_mem_pieces[0], *second[1:]),
        FULL,
    )
    grad_input = in_order(
        tuple(((2 * k, 0, half), (2 * k + 1, 0, half)) for k in members[:3]),
        (low, high, low_one, high_one, low_two, high_two),
        FULL,
        micros=100,
    )
    grad_input = in_order(
        (((0, 0, half), (1, 0, half)),),
        (low_three, high_three),
        FULL,
        (output, grad_memory, token),
        first=3,
        into=grad_input,
    )
    return (
        output[None],
        grad_input[None],
        grad_memory[None],
        grad_down,
        grad_up,
        grad_prefix,
        *updated,
        *prefix_new,
        new_down_mom,
        new_down_outer,
        new_up_mom,
        new_up_outer,
        *prefix_results,
    )


def solution(mesh):
    placed = (
        P("grp", None, None, None),
        P("grp", None, "mem", None),
        P("grp", None, None, None),
        P("grp", None),
        P("grp", None),
        P(),
        P(),
        P(),
        P(),
        P(),
        P(),
        P(),
        P(),
        P("grp", "mem", None),
        P("grp", "mem", None),
        P("grp", None, None, "mem"),
        P("grp", "mem", None),
        P("grp", "mem", None),
        P("grp", "mem", None),
        P("grp", "mem", None),
        P("grp", None, None, "mem"),
        P("grp", None, None, "mem"),
        P("mem", None),
        P("mem", None),
        P(None, None, "mem"),
        P("mem", None),
        P("mem", None),
        P(None, None, "mem"),
    )
    return jax.shard_map(
        local,
        mesh=mesh,
        in_specs=placed,
        out_specs=(
            P("grp", None, None, None),
            P("grp", None, None, None),
            P("grp", None, "mem", None),
            P("grp", "mem", None),
            P("grp", "mem", None),
            P("grp", None, None, "mem"),
            P("grp", "mem", None),
            P("grp", "mem", None),
            P("grp", "mem", None),
            P("grp", "mem", None),
            P("grp", "mem", None),
            P("grp", "mem", None),
            P("grp", None, None, "mem"),
            P("grp", None, None, "mem"),
            P("grp", None, None, "mem"),
            P("mem", None),
            P("mem", None),
            P("mem", None),
            P("mem", None),
            P(None, None, "mem"),
            P(None, None, "mem"),
        ),
        check_vma=False,
    )
```
